32 devices in a mesh: ep: 16 (over z, y, x), tp: 2 (over core).
Axes of the slice: x: 2, y: 2, z: 4, core: 2. Of those that a mesh axis runs over, the one named last changes fastest.
Arguments:
- tokens: bfloat16 [256, 7168], P('ep', 'tp'), may hold values from -6 to 6
- expert_ids: int32 [256, 8], P('ep'), may hold values from 0 to 15, all different within a row; in each aligned block of 16 rows (0 to 15, 16 to 31, ...) at most 16 rows name the same one
- gate_weights: float32 [256, 8], P('ep'), may hold values from 0.1 to 1
- expert_gate_up: bfloat16 [16, 7168, 2, 1024], P('ep', None, None, 'tp'), may hold values from -0.0625 to 0.0625
- expert_down: bfloat16 [16, 7168, 1024], P('ep', None, 'tp'), may hold values from -0.1875 to 0.1875
- queries: bfloat16 [256, 64, 576], P('ep', 'tp'), may hold values from -8 to 8
- latent_cache: bfloat16 [768, 16, 576], P('ep'), may hold values from -8 to 8
- block_source: int32 [768], replicated, may hold values from 0 to 767, as said below
- block_request: int32 [768], P('ep'), may hold values from -1 to 15, as said below
- block_used: int32 [768], P('ep'), may hold values from 0 to 16, as said below
Outputs:
- moe_out: bfloat16 [256, 7168], P('ep', 'tp')
- attention_out: bfloat16 [256, 64, 512], P('ep', 'tp')
The draws below stay inside these ranges and needn't reach their ends.
Inputs may be any that keep to these rules, and one draw needn't show every extreme that they name: `expert_ids`: each row names 8 different experts; among the rows of one index of ep no expert is named by more than 16 rows, a bound that some block reaches. `block_source`: A permutation. `block_request`: within one index of ep each row holds a run of 1 to 3 consecutive slots, rows in order from the first slot, unused slots (-1) after them; some index of ep holds 3 slots for every row, and some has unused slots. `block_used`: 16 in every used slot but a row's last one, which holds 2 to 16; 0 in unused slots.
All inputs are finite; a program needn't handle non-finite values.
Results may differ from the reference program's by a relative error of at most 0.015.
Values may be sent and summed in bfloat16 or wider, within the bound.
No kernel may reach another device: no remote copies, remote signals or barrier semaphores. Data moves between devices by JAX's collectives and lax.ppermute only.
A program may use at most 64 MiB of HBM per device.

```python
import math
import jax
import jax.numpy as jnp
import numpy as np
from jax import lax

D = 7168
FFE = 1024
HEADS = 64
KV = 512
TOPK = 8
BLK = 16
ROWS = 16
EXPERTS = 16
TOKENS = 256
SLOTS = 48
ALL_SLOTS = 768
CAP = 16
LAT = 576
FFE_PART = 512
N_EP = 16
N_TP = 2


def layout(key):
    subkeys = jax.random.split(jax.random.fold_in(key, 7), 5)
    devices = jnp.arange(N_EP, dtype=jnp.int32)
    device_caps = jax.random.randint(subkeys[0], (N_EP,), 0, 3)
    full_device = jax.random.randint(subkeys[1], (), 0, N_EP)
    light_device = (full_device + 1) % N_EP
    device_caps = jnp.where(devices == full_device, 2, jnp.where(devices == light_device, 0, device_caps))
    extra_blocks = jax.random.randint(subkeys[2], (N_EP, ROWS), 0, 3)
    counts = 1 + jnp.minimum(extra_blocks, device_caps[:, None])
    counts = jnp.where(devices[:, None] == full_device, 3, counts)
    run_ends = jnp.cumsum(counts, axis=1)
    starts = run_ends - counts
    slot_range = jnp.arange(SLOTS, dtype=jnp.int32)
    inside = (slot_range[None, :, None] >= starts[:, None, :]) & (slot_range[None, :, None] < run_ends[:, None, :])
    occupied = jnp.any(inside, axis=2)
    request = jnp.where(occupied, jnp.sum(inside * jnp.arange(ROWS, dtype=jnp.int32)[None, None, :], axis=2), -1)
    is_last = jnp.any(inside & (slot_range[None, :, None] == run_ends[:, None, :] - 1), axis=2)
    tail_used = jax.random.randint(subkeys[3], (N_EP, SLOTS), 2, BLK + 1)
    used_tokens = jnp.where(occupied, jnp.where(is_last, tail_used, BLK), 0)
    source = jax.random.permutation(subkeys[4], N_EP * SLOTS)
    return (request.reshape(-1), used_tokens.reshape(-1), source)


def draw_block_source(key, part):
    return layout(key)[2].astype(jnp.int32)


def draw_block_request(key, part):
    return layout(key)[0].astype(jnp.int32)


def draw_block_used(key, part):
    return layout(key)[1].astype(jnp.int32)


def draw_latent_cache(key, part):
    key = jax.random.fold_in(key, 11)
    cache_values = jnp.clip(jax.random.normal(key, (ALL_SLOTS, BLK, LAT), jnp.float32), -8.0, 8.0)
    return cache_values.astype(jnp.bfloat16)


def draw_queries(key, part):
    key = jax.random.fold_in(key, 13)
    query_values = jnp.clip(jax.random.normal(key, (TOKENS, HEADS, LAT), jnp.float32), -8.0, 8.0)
    return query_values.astype(jnp.bfloat16)


def block_levels(rng, extent, cuts, smallest, top_value):
    factor_of = 1.0
    for axis_at, blocks in cuts:
        draws = jax.random.uniform(jax.random.fold_in(jax.random.fold_in(rng, 6), axis_at), (blocks,), jnp.float32, smallest / len(cuts), top_value / len(cuts))
        factor_of = factor_of * jnp.repeat(jnp.exp(draws), extent[axis_at] // blocks).reshape((-1,) + (1,) * (len(extent) - 1 - axis_at))
    return factor_of


def routed_block(rng, own, number, rows, count, top, limit, slope):
    sequence = jax.random.permutation(rng, count)
    crowded, usual = portions_of(count, rows * top, limit, slope, True), portions_of(count, rows * top, limit, slope, False)
    places = jnp.arange(count)

    def named(lengths, turn):
        used = int((lengths > 0).sum())
        fixed = max(1, used // 4)
        moved = fixed + (places - fixed + turn * (used - fixed)) % max(1, count - fixed)
        return jnp.zeros((count,), jnp.int32).at[sequence[jnp.where(places < fixed, places, moved)]].set(jnp.asarray(lengths, jnp.int32))

    lengths = jnp.where(number % 4 == 0, named(crowded, number // 4), named(usual, number - number // 4 - 1))
    mixed = jax.random.permutation(jax.random.fold_in(own, 3), count)
    donor, taker = mixed[0:count // 2 * 2:2], mixed[1:count // 2 * 2:2]
    margin = jnp.minimum(lengths[donor] - 1, limit - lengths[taker]) // 2
    margin = jnp.where((donor == sequence[0]) | (taker == sequence[0]) | (lengths[taker] == 0), 0, jnp.maximum(margin, 0))
    moved = jax.random.randint(jax.random.fold_in(own, 4), (count // 2,), 0, 1 << 20) % (margin + 1)
    lengths = lengths.at[donor].add(-moved).at[taker].add(moved)
    members = jnp.searchsorted(jnp.cumsum(lengths), jnp.arange(rows * top), side="right").astype(jnp.int32)
    grid = members.reshape(top, rows).T
    grid = grid[jax.random.permutation(jax.random.fold_in(own, 1), rows)]
    turn = jax.random.randint(jax.random.fold_in(own, 2), (rows, 1), 0, top)
    return jnp.take_along_axis(grid, (jnp.arange(top)[None, :] + turn) % top, axis=1)


def portions_of(amount, total, limit, skew, full):
    portions = [(1 << 20) // math.isqrt(rank ** skew) + 1 for rank in range(1, amount + 1)]
    largest = limit if full else min(limit, max(-(-total // amount), total * portions[0] // sum(portions)))
    least = 1 if total - largest >= amount - 1 else 0
    holding, rest = [largest] + [least] * (amount - 1), total - largest - least * (amount - 1)
    while rest > 0:
        candidates = [i for i in range(1, amount) if holding[i] < largest] or [i for i in range(1, amount) if holding[i] < limit]
        pool, budget = sum([portions[i] for i in candidates]), rest
        for i in candidates:
            more = min(limit - holding[i], max(1, budget * portions[i] // pool), rest)
            holding[i] = holding[i] + more
            rest = rest - more
    return np.array(holding)


def noise(own_key, shape, scale, bound, cuts=(), kind=jnp.bfloat16):
    entries = jax.random.normal(own_key, shape, jnp.float32) * scale
    if len(cuts) > 0:
        entries = block_levels(own_key, shape, cuts, -0.22, 0.18) * entries
    return jnp.clip(entries, min=-bound, max=bound).astype(kind)


def setup_inputs(seed: int = 0) -> dict:
    seeds = jax.random.split(jax.random.key(seed), 11)
    tokens = noise(seeds[0], (TOKENS, D), 1.0, 6.0, ((0, 16), (1, 2)))
    expert_ids_keys = jax.random.split(jax.random.fold_in(seeds[1], 1), TOKENS // ROWS)
    expert_ids_turns = jax.random.permutation(jax.random.fold_in(seeds[1], 3), TOKENS // ROWS)
    expert_ids = jax.vmap(lambda own, number: routed_block(jax.random.fold_in(seeds[1], 2), own, number, ROWS, EXPERTS, TOPK, CAP, 2))(expert_ids_keys, expert_ids_turns).reshape((TOKENS, TOPK))
    gate_weights = jnp.clip(0.1 + 0.9 * jax.random.uniform(seeds[2], (TOKENS, TOPK), jnp.float32) ** block_levels(seeds[2], (TOKENS, TOPK), ((0, 16),), -0.2, 0.2), 0.1, 1.0)
    expert_gate_up = noise(seeds[3], (EXPERTS, D, 2, FFE), D ** -0.5, 0.0625, ((0, 16), (3, 2)))
    expert_down = noise(seeds[4], (EXPERTS, D, FFE), FFE ** -0.5, 0.1875, ((0, 16), (2, 2)))
    queries = draw_queries(jax.random.fold_in(seeds[10], 71), 0)
    latent_cache = draw_latent_cache(jax.random.fold_in(seeds[10], 71), 0)
    block_source = draw_block_source(jax.random.fold_in(seeds[10], 71), 0)
    block_request = draw_block_request(jax.random.fold_in(seeds[10], 71), 0)
    block_used = draw_block_used(jax.random.fold_in(seeds[10], 71), 0)
    return dict(tokens=tokens, expert_ids=expert_ids, gate_weights=gate_weights, expert_gate_up=expert_gate_up, expert_down=expert_down, queries=queries, latent_cache=latent_cache, block_source=block_source, block_request=block_request, block_used=block_used)


score_scale = 192.0 ** -0.5


def expert_layer(tokens, expert_ids, gate_weights, expert_gate_up, expert_down):
    pair_count = ROWS * TOPK
    flat_ids = expert_ids.reshape(N_EP, pair_count).astype(jnp.int32)
    expert_hot = (flat_ids[:, :, None] == jnp.arange(EXPERTS, dtype=jnp.int32)[None, None, :]).astype(jnp.int32)
    earlier = jnp.sum((jnp.cumsum(expert_hot, axis=1) - expert_hot) * expert_hot, axis=2).astype(jnp.int32)
    device_index = jnp.broadcast_to(jnp.arange(N_EP, dtype=jnp.int32)[:, None], (N_EP, pair_count))
    row_index = jnp.broadcast_to((jnp.arange(pair_count, dtype=jnp.int32) // TOPK)[None, :], (N_EP, pair_count))
    token_index = device_index * ROWS + row_index
    slot_table = jnp.full((EXPERTS, N_EP, CAP), -1, jnp.int32).at[flat_ids, device_index, earlier].set(token_index)
    weight_table = jnp.zeros((EXPERTS, N_EP, CAP), jnp.float32).at[flat_ids, device_index, earlier].set(
        gate_weights.reshape(N_EP, pair_count).astype(jnp.float32))

    def one_expert(running, expert):
        token_slots = slot_table[expert].reshape(-1)
        present = token_slots >= 0
        safe_index = jnp.maximum(token_slots, 0).astype(jnp.int32)
        picked = jnp.where(present[:, None], tokens[safe_index], jnp.zeros((), tokens.dtype))
        expert_block = lax.dynamic_index_in_dim(expert_gate_up, expert.astype(jnp.int32), 0, keepdims=False)
        gate_and_up = jnp.einsum("rd,dgf->rgf", picked.astype(jnp.float32), expert_block.astype(jnp.float32))
        hidden = (jax.nn.silu(gate_and_up[:, 0]) * gate_and_up[:, 1]).astype(jnp.bfloat16)
        hidden = lax.optimization_barrier(hidden)
        down_block = lax.dynamic_index_in_dim(expert_down, expert.astype(jnp.int32), 0, keepdims=False).astype(jnp.float32)
        groups = hidden.astype(jnp.float32).reshape(-1, N_TP, FFE_PART)
        partial_value = jnp.einsum("rpf,dpf->prd", groups, down_block.reshape(D, N_TP, FFE_PART)).astype(jnp.bfloat16)
        partial_value = lax.optimization_barrier(partial_value)
        summed = jnp.sum(partial_value.astype(jnp.float32), axis=0).astype(jnp.bfloat16)
        summed = lax.optimization_barrier(summed)
        weighted = summed.astype(jnp.float32) * weight_table[expert].reshape(-1)[:, None]
        weighted = jnp.where(present[:, None], weighted, jnp.zeros((), jnp.float32))
        return running.at[safe_index].add(weighted), None

    start = jnp.zeros((TOKENS, D), jnp.float32)
    result, unused = lax.scan(one_expert, start, jnp.arange(EXPERTS, dtype=jnp.int32))
    return result.astype(jnp.bfloat16)


def attention_layer(queries, latent_cache, block_source, block_request, block_used):
    moved_cache = latent_cache[block_source.astype(jnp.int32)].reshape(N_EP, SLOTS * BLK, LAT)
    owners = jnp.repeat(block_request.reshape(N_EP, SLOTS), BLK, axis=1)
    limits = jnp.repeat(block_used.reshape(N_EP, SLOTS), BLK, axis=1)
    within = jnp.tile(jnp.arange(BLK, dtype=jnp.int32), SLOTS)
    grouped = queries.reshape(N_EP, ROWS, HEADS, LAT)

    def one_device(device_inputs):
        query_block, key_block, owner_row, limit_row = device_inputs
        visible = (owner_row[None, :] == jnp.arange(ROWS, dtype=jnp.int32)[:, None]) & (within < limit_row)[None, :]
        scores = jnp.einsum("rhc,tc->rht", query_block.astype(jnp.float32), key_block.astype(jnp.float32)) * score_scale
        scores = jnp.where(visible[:, None, :], scores, -jnp.inf)
        row_max = jnp.max(scores, axis=2, keepdims=True)
        exponent_terms = jnp.exp(scores - row_max)
        weights = (exponent_terms / jnp.sum(exponent_terms, axis=2, keepdims=True)).astype(jnp.bfloat16)
        weights = lax.optimization_barrier(weights)
        attended = jnp.einsum("rht,tc->rhc", weights.astype(jnp.float32), key_block[:, :KV].astype(jnp.float32))
        return attended.astype(jnp.bfloat16)

    result = lax.map(one_device, (grouped, moved_cache, owners, limits))
    return result.reshape(TOKENS, HEADS, KV)


def reference(tokens, expert_ids, gate_weights, expert_gate_up, expert_down, queries, latent_cache, block_source, block_request, block_used):
    moe_out = expert_layer(tokens, expert_ids, gate_weights, expert_gate_up, expert_down)
    attention_out = attention_layer(queries, latent_cache, block_source, block_request, block_used)
    return (moe_out, attention_out)
```

```python
import jax
import jax.numpy as jnp
from jax import lax
from jax.sharding import PartitionSpec as P

KV = 512


score_scale = 192.0 ** (-0.5)


def move_blocks(latent_cache, block_source):
    ep_size = lax.axis_size("ep")
    tp_size = lax.axis_size("tp")
    slots, block_size, latent = latent_cache.shape
    share = slots // tp_size
    piece = block_size * latent // ep_size
    mine = lax.dynamic_slice_in_dim(latent_cache, lax.axis_index("tp") * share, share, axis=0)
    pieces = mine.reshape(share, ep_size, piece).transpose(1, 0, 2)
    spread = lax.all_to_all(pieces, "ep", split_axis=0, concat_axis=0, tiled=True)
    every = lax.all_gather(spread, "tp", axis=0, tiled=False)
    source_device = block_source // slots
    source_slot = block_source % slots
    row = (source_slot // share) * (ep_size * share) + source_device * share + source_slot % share
    row = lax.dynamic_slice_in_dim(
        row.reshape(ep_size, tp_size, share), lax.axis_index("tp"), 1, axis=1
    ).reshape(-1)
    ordered = jnp.take(every.reshape(-1, piece), row, axis=0, mode="clip")
    arrived = lax.all_to_all(
        ordered.reshape(ep_size, share, piece), "ep", split_axis=0, concat_axis=0, tiled=True
    )
    if piece != latent:
        arrived = arrived.transpose(1, 0, 2).reshape(share, block_size, latent).transpose(1, 0, 2)
    return lax.all_gather(arrived, "tp", axis=0, tiled=False)


def ep_bits():
    ep_size = lax.axis_size("ep")
    return [1 << place for place in reversed(range(ep_size.bit_length() - 1))]


def exchange(value, bit):
    ep_size = lax.axis_size("ep")
    return lax.ppermute(value, "ep", [(index, index ^ bit) for index in range(ep_size)])


def swap_tp(value):
    tp_size = lax.axis_size("tp")
    return [
        lax.ppermute(value, "tp", [(index, (index + step) % tp_size) for index in range(tp_size)])
        for step in range(1, tp_size)
    ]


def gather_blocks(block, order):
    bits = ep_bits()[::-1]
    value = block.reshape((1,) * len(bits) + block.shape)
    for bit in order:
        value = jnp.concatenate([value, exchange(value, bit)], axis=bits.index(bit))
    return value.reshape((-1,) + block.shape[1:])


def scatter_sum(partial, order):
    bits = ep_bits()[::-1]
    ep_size = lax.axis_size("ep")
    block = (partial.shape[0] // ep_size,) + partial.shape[1:]
    value = partial.reshape((2,) * len(bits) + block)
    for bit in reversed(order):
        axis = bits.index(bit)
        kept = lax.slice_in_dim(value, 0, 1, axis=axis)
        sent = lax.slice_in_dim(value, 1, 2, axis=axis)
        value = (kept.astype(jnp.float32) + exchange(sent, bit).astype(jnp.float32)).astype(
            jnp.bfloat16
        )
    return value.reshape(block)


def three_parts(value):
    parts = []
    for _ in range(3):
        part = lax.reduce_precision(value, 8, 7)
        parts.append(part.astype(jnp.bfloat16))
        value = value - part
    return parts


def body(
    tokens,
    expert_ids,
    gate_weights,
    expert_gate_up,
    expert_down,
    queries,
    latent_cache,
    block_source,
    block_request,
    block_used,
):
    row_count, top_count = expert_ids.shape
    ep_size = lax.axis_size("ep")
    tp_size = lax.axis_size("tp")
    tp_index = lax.axis_index("tp")
    bits = ep_bits()
    orders = (bits, bits[:-2] + [bits[-1], bits[-2]])
    width = tokens.shape[1]
    cut = width // 2
    expert_range = jnp.arange(ep_size, dtype=jnp.int32)
    dense_gate = jnp.sum(
        jnp.where(
            expert_ids[:, :, None] == expert_range[None, None, :], gate_weights[:, :, None], 0.0
        ),
        axis=1,
    )
    gate_parts = jnp.concatenate(three_parts(dense_gate), axis=1)
    pad = -gate_parts.shape[1] % 128
    sent_rows = (
        jnp.concatenate([tokens[:, :cut], jnp.pad(gate_parts, ((0, 0), (0, pad)))], axis=1),
        tokens[:, cut:],
    )
    gathered = [gather_blocks(rows, order) for rows, order in zip(sent_rows, orders)]
    all_gate = gathered[0][:, cut : cut + 3 * ep_size].astype(jnp.float32)
    mine = (jnp.arange(3 * ep_size, dtype=jnp.int32) % ep_size) == lax.axis_index("ep")
    my_gate = jnp.sum(jnp.where(mine[None, :], all_gate, 0.0), axis=1)
    halves = (gathered[0][:, :cut], gathered[1])
    gate_and_up = 0.0
    for part, half_rows in enumerate(halves):
        for step, rows in enumerate([half_rows] + swap_tp(half_rows)):
            start = ((tp_index + tp_size - step) % tp_size) * width + part * cut
            weight = lax.dynamic_slice_in_dim(expert_gate_up[0], start, cut, axis=0)
            gate_and_up = gate_and_up + jnp.einsum(
                "sd,dgf->sgf", rows, weight, preferred_element_type=jnp.float32
            )
    hidden = (
        jax.nn.silu(gate_and_up[:, 0]) * gate_and_up[:, 1] * my_gate[:, None]
    ).astype(jnp.bfloat16)

    def down(start):
        weight = lax.dynamic_slice_in_dim(expert_down[0], start, cut, axis=0)
        return lax.dot_general(
            hidden, weight, (((1,), (1,)), ((), ())), preferred_element_type=jnp.float32
        ).astype(jnp.bfloat16)

    moe_parts = []
    for part, order in enumerate(orders):
        total = down(tp_index * width + part * cut).astype(jnp.float32)
        for step in range(1, tp_size):
            target = (tp_index + step) % tp_size
            other = lax.ppermute(
                down(target * width + part * cut),
                "tp",
                [(index, (index + step) % tp_size) for index in range(tp_size)],
            )
            total = total + other.astype(jnp.float32)
        moe_parts.append(scatter_sum(total.astype(jnp.bfloat16), order))
    moe_out = jnp.concatenate(moe_parts, axis=1)

    slot_total, block_size, latent = latent_cache.shape
    half = slot_total // tp_size
    key_rows = move_blocks(latent_cache, block_source).reshape(slot_total * block_size, latent)

    def per_token(values):
        return jnp.broadcast_to(
            values.reshape(tp_size, 1, half), (tp_size, block_size, half)
        ).reshape(-1)

    owner_token = per_token(block_request)
    limit_token = per_token(block_used)
    within = jnp.broadcast_to(
        jnp.arange(block_size, dtype=jnp.int32)[None, :, None], (tp_size, block_size, half)
    ).reshape(-1)
    visible = (owner_token[None, :] == jnp.arange(row_count, dtype=jnp.int32)[:, None]) & (
        within < limit_token
    )[None, :]
    scores = (
        jnp.einsum("rhc,tc->rht", queries, key_rows, preferred_element_type=jnp.float32)
        * score_scale
    )
    scores = jnp.where(visible[:, None, :], scores, -jnp.inf)
    row_max = jnp.max(scores, axis=2, keepdims=True)
    exponent_terms = jnp.exp(scores - row_max)
    weights = (exponent_terms / jnp.sum(exponent_terms, axis=2, keepdims=True)).astype(jnp.bfloat16)
    attended = jnp.einsum(
        "rht,tc->rhc", weights, key_rows[:, :KV], preferred_element_type=jnp.float32
    ).astype(jnp.bfloat16)
    return (moe_out, attended)


def solution(mesh):
    placed = (
        P("ep", "tp"),
        P("ep", None),
        P("ep", None),
        P("ep", None, None, "tp"),
        P("ep", None, "tp"),
        P("ep", "tp", None),
        P("ep", None, None),
        P(),
        P("ep"),
        P("ep"),
    )
    return jax.shard_map(
        body,
        mesh=mesh,
        in_specs=placed,
        out_specs=(P("ep", "tp"), P("ep", "tp", None)),
        check_vma=False,
    )
```

```python
import functools

import jax
import jax.numpy as jnp
from jax import lax
from jax.experimental import pallas as pl
from jax.experimental.pallas import tpu as pltpu
from jax.sharding import PartitionSpec as P

KV = 512


score_scale = 192.0 ** (-0.5)

WHOLE = pl.BlockSpec(memory_space=pltpu.VMEM)


def kernel_call(kernel, out_shape, arguments, flops, in_specs=None, scratch_shapes=()):
    moved = sum(array.size * array.dtype.itemsize for array in arguments)
    out_leaves = jax.tree.leaves(out_shape)
    moved += sum(array.size * array.dtype.itemsize for array in out_leaves)
    return pl.pallas_call(
        kernel,
        out_shape=out_shape,
        in_specs=in_specs or [WHOLE] * len(arguments),
        out_specs=jax.tree.map(lambda _: WHOLE, out_shape),
        scratch_shapes=scratch_shapes,
        compiler_params=pltpu.CompilerParams(vmem_limit_bytes=40 << 20),
        cost_estimate=pl.CostEstimate(flops=flops, bytes_accessed=moved, transcendentals=0),
    )(*arguments)


def tie(values, others):
    return lax.optimization_barrier((values, others))[0]


def ep_bits():
    ep_size = lax.axis_size("ep")
    return [1 << place for place in reversed(range(ep_size.bit_length() - 1))]


def exchange(value, bit):
    ep_size = lax.axis_size("ep")
    return lax.ppermute(value, "ep", [(index, index ^ bit) for index in range(ep_size)])


def pass_tp(value, step):
    tp_size = lax.axis_size("tp")
    return lax.ppermute(
        value, "tp", [(index, (index + step) % tp_size) for index in range(tp_size)]
    )


def swap_tp(value):
    return [pass_tp(value, step) for step in range(1, lax.axis_size("tp"))]


def gather_blocks(block, order, last=None):
    bits = ep_bits()[::-1]
    value = block.reshape((1,) * len(bits) + block.shape)
    for bit in order[:-1]:
        value = jnp.concatenate([value, exchange(value, bit)], axis=bits.index(bit))
    arrived = exchange(value, order[-1])
    if last is not None:
        last(value)
    return value, arrived, bits.index(order[-1])


def join(halves, axis):
    whole = jnp.concatenate(halves, axis=axis)
    return whole.reshape((-1,) + whole.shape[-1:])


def sum_kernel(rows, count, picked, *refs):
    out = refs[count]
    for place, blocks in enumerate(picked):
        total = refs[0][blocks[0] * rows : (blocks[0] + 1) * rows].astype(jnp.float32)
        for ref, block in zip(refs[1:count], blocks[1:]):
            total = total + ref[block * rows : (block + 1) * rows].astype(jnp.float32)
        out[place * rows : (place + 1) * rows] = total.astype(out.dtype)


def add_up(terms, places, rows):
    arrays = [array for array, _ in terms]
    picked = [[held.index(place) for _, held in terms] for place in places]
    shape = jax.ShapeDtypeStruct((len(places) * rows, arrays[0].shape[1]), jnp.bfloat16)
    kernel = functools.partial(sum_kernel, rows, len(arrays), picked)
    return kernel_call(kernel, shape, arrays, flops=shape.size * len(arrays))


def scatter_sum(arrays, order, rows, first=None, last=None):
    bits = ep_bits()[::-1]
    number = len(bits)
    places = [
        sum(((spot >> (number - 1 - axis)) & 1) * bit for axis, bit in enumerate(bits))
        for spot in range(1 << number)
    ]
    terms = [(array, places) for array in arrays]
    for bit in reversed(order):
        sent_places = [place for place in places if place & bit]
        places = [place for place in places if not place & bit]
        sent = add_up(terms, sent_places, rows)
        if first is not None and bit == order[-1]:
            sent = first(sent)
        if last is not None and bit == order[0]:
            sent = last(sent)
        terms = terms + [(exchange(sent, bit), [place ^ bit for place in sent_places])]
    return add_up(terms, places, rows)


def three_parts(value):
    parts = []
    for _ in range(3):
        part = lax.reduce_precision(value, 8, 7)
        parts.append(part.astype(jnp.bfloat16))
        value = value - part
    return parts


def pick(choices, index):
    value = choices[0]
    for number, choice in enumerate(choices[1:], 1):
        value = jnp.where(index == number, choice, value)
    return value


def down_kernel(step, parts, tp_size, cut, hidden, weight, *refs):
    outs, held, arrived = refs[:parts], refs[parts], refs[parts + 1]
    target = lax.rem(lax.axis_index("tp") + step, tp_size)
    copies = []
    for part in range(parts):
        start = pl.multiple_of(target * (parts * cut) + part * cut, cut)
        copies.append(
            pltpu.make_async_copy(
                weight.at[pl.ds(start, cut)],
                held.at[pl.ds(part * cut, cut)],
                arrived.at[part],
            )
        )
    for copy in copies:
        copy.start()
    width = 256 if cut % 256 == 0 else 128
    chunk = min(256, hidden.shape[0])
    for part in range(parts):
        copies[part].wait()
        for column in range(0, cut, width):
            for row in range(0, hidden.shape[0], chunk):
                outs[part][row : row + chunk, column : column + width] = lax.dot_general(
                    hidden[row : row + chunk],
                    held[part * cut + column : part * cut + column + width],
                    (((1,), (1,)), ((), ())),
                    preferred_element_type=jnp.float32,
                ).astype(jnp.bfloat16)


def down(hidden, weight, step, parts):
    tp_size = lax.axis_size("tp")
    cut = weight.shape[0] // tp_size // parts
    shape = jax.ShapeDtypeStruct((hidden.shape[0], cut), jnp.bfloat16)
    return kernel_call(
        functools.partial(down_kernel, step, parts, tp_size, cut),
        [shape] * parts,
        [hidden, weight],
        flops=2 * hidden.size * cut * parts,
        in_specs=[WHOLE, pl.BlockSpec(memory_space=pl.ANY)],
        scratch_shapes=[
            pltpu.VMEM((parts * cut, weight.shape[1]), weight.dtype),
            pltpu.SemaphoreType.DMA((parts,)),
        ],
    )


def order_kernel(index, *refs):
    rows, out = refs[:-1], refs[-1]
    columns = lax.broadcasted_iota(jnp.int32, (out.shape[0], rows[0].shape[0]), 1)
    total = jnp.zeros(out.shape, jnp.float32)
    for step, ref in enumerate(rows):
        hot = (columns == index[:, step : step + 1]).astype(jnp.bfloat16)
        total = total + jnp.dot(hot, ref[...], preferred_element_type=jnp.float32)
    out[...] = total.astype(out.dtype)


def cache_out(latent_cache):
    ep_size = lax.axis_size("ep")
    slots, block_size, latent = latent_cache.shape
    share = slots // lax.axis_size("tp")
    mine = lax.dynamic_slice_in_dim(latent_cache, lax.axis_index("tp") * share, share, axis=0)
    return mine.reshape(share, ep_size, block_size * latent // ep_size).transpose(1, 0, 2)


def cache_turn(pieces, block_source, slots):
    ep_size = lax.axis_size("ep")
    tp_size = lax.axis_size("tp")
    tp_index = lax.axis_index("tp")
    share, piece = pieces.shape[1:]
    spread = lax.all_to_all(pieces, "ep", split_axis=0, concat_axis=0, tiled=True)
    wanted = lax.dynamic_slice_in_dim(
        block_source.reshape(ep_size, tp_size, share), tp_index, 1, axis=1
    ).reshape(-1)
    place = (wanted // slots) * share + wanted % share
    holder = (wanted % slots) // share
    from_step = (tp_index + tp_size - holder) % tp_size
    index = jnp.where(
        from_step[:, None] == jnp.arange(tp_size, dtype=jnp.int32)[None, :], place[:, None], -1
    )
    rows = [part.reshape(-1, piece) for part in [spread] + swap_tp(spread)]
    shape = jax.ShapeDtypeStruct(rows[0].shape, rows[0].dtype)
    ordered = kernel_call(
        order_kernel, shape, [index] + rows, flops=2 * tp_size * rows[0].size * rows[0].shape[0]
    )
    return ordered.reshape(ep_size, share, piece)


def cache_in(ordered, block_size, latent):
    share, piece = ordered.shape[1:]
    arrived = lax.all_to_all(ordered, "ep", split_axis=0, concat_axis=0, tiled=True)
    if piece != latent:
        arrived = arrived.transpose(1, 0, 2).reshape(share, block_size, latent).transpose(1, 0, 2)
    return arrived


def attention_kernel(heads, chunk, owner, queries, *refs):
    keys, out = refs[:-1], refs[-1]
    tokens = keys[0].shape[0]
    for start in range(0, queries.shape[0], chunk):
        row = (lax.broadcasted_iota(jnp.int32, (chunk, tokens), 0) + start) // heads
        scores = []
        for step, key in enumerate(keys):
            part = lax.dot_general(
                queries[start : start + chunk],
                key[...],
                (((1,), (1,)), ((), ())),
                preferred_element_type=jnp.float32,
            )
            scores.append(
                jnp.where(row == owner[step : step + 1, :], part * score_scale, -jnp.inf)
            )
        row_max = scores[0].max(axis=1, keepdims=True)
        for part in scores[1:]:
            row_max = jnp.maximum(row_max, part.max(axis=1, keepdims=True))
        terms = [jnp.exp(part - row_max) for part in scores]
        total = sum(term.sum(axis=1, keepdims=True) for term in terms)
        attended = jnp.zeros((chunk, KV), jnp.float32)
        for term, key in zip(terms, keys):
            attended = attended + jnp.dot(
                (term / total).astype(jnp.bfloat16),
                key[:, :KV],
                preferred_element_type=jnp.float32,
            )
        out[start : start + chunk] = attended.astype(out.dtype)


def attend(queries, keys, block_request, block_used):
    tp_size = lax.axis_size("tp")
    row_count, heads, latent = queries.shape
    block_size, share = keys[0].shape[:2]
    within = jnp.arange(block_size, dtype=jnp.int32)[:, None]
    owners = []
    for step in range(tp_size):
        first = ((lax.axis_index("tp") + tp_size - step) % tp_size) * share
        owner = lax.dynamic_slice_in_dim(block_request, first, share)[None, :]
        limit = lax.dynamic_slice_in_dim(block_used, first, share)[None, :]
        owners.append(jnp.where(within < limit, owner, -1).reshape(1, -1))
    keys = [part.reshape(-1, latent) for part in keys]
    rows = queries.reshape(-1, latent)
    shape = jax.ShapeDtypeStruct((rows.shape[0], KV), jnp.bfloat16)
    result = kernel_call(
        functools.partial(attention_kernel, heads, min(128, rows.shape[0])),
        shape,
        [jnp.concatenate(owners, axis=0), rows] + keys,
        flops=4 * rows.size * keys[0].shape[0] * tp_size,
    )
    return result.reshape(row_count, heads, KV)


def body(
    tokens,
    expert_ids,
    gate_weights,
    expert_gate_up,
    expert_down,
    queries,
    latent_cache,
    block_source,
    block_request,
    block_used,
):
    row_count, top_count = expert_ids.shape
    slot_total, block_size, latent = latent_cache.shape
    ep_size = lax.axis_size("ep")
    tp_size = lax.axis_size("tp")
    tp_index = lax.axis_index("tp")
    bits = ep_bits()
    orders = (bits, bits[:-2] + [bits[-1], bits[-2]])
    parts = len(orders)
    cut = tokens.shape[1] // parts
    held = {}

    sent_rows = [tokens[:, part * cut : (part + 1) * cut] for part in range(parts)]
    expert_ids, gate_weights = tie((expert_ids, gate_weights), sent_rows[0])
    expert_range = jnp.arange(ep_size, dtype=jnp.int32)
    dense_gate = jnp.sum(
        jnp.where(
            expert_ids[:, :, None] == expert_range[None, None, :], gate_weights[:, :, None], 0.0
        ),
        axis=1,
    )
    gate_parts = jnp.concatenate(three_parts(dense_gate), axis=1)
    pad = -gate_parts.shape[1] % 128
    sent_rows[-1] = jnp.concatenate(
        [sent_rows[-1], jnp.pad(gate_parts, ((0, 0), (0, pad)))], axis=1
    )

    def beside_last_gather(sent):
        pieces = tie(cache_out(latent_cache), sent)
        held["ordered"] = cache_turn(pieces, block_source, slot_total)

    hooks = [None] * (parts - 1) + [beside_last_gather]
    columns = [[None] * parts for _ in range(tp_size)]
    for part, (rows, order, hook) in enumerate(zip(sent_rows, orders, hooks)):
        early, late, axis = gather_blocks(rows, order, hook)
        steps = [(early, late)] + list(zip(swap_tp(early), swap_tp(late)))
        steps = [join(halves, axis) for halves in steps]
        if part == parts - 1:
            all_gate = steps[0][:, cut : cut + 3 * ep_size].astype(jnp.float32)
        for owner in range(tp_size):
            chosen = pick(steps, (tp_index + tp_size - owner) % tp_size)
            columns[owner][part] = chosen[:, :cut]
    mine = (jnp.arange(3 * ep_size, dtype=jnp.int32) % ep_size) == lax.axis_index("ep")
    my_gate = jnp.sum(jnp.where(mine[None, :], all_gate, 0.0), axis=1)
    gate_and_up = jnp.einsum(
        "sd,dgf->sgf",
        jnp.concatenate([column for group in columns for column in group], axis=1),
        expert_gate_up[0],
        preferred_element_type=jnp.float32,
    )
    hidden = (
        jax.nn.silu(gate_and_up[:, 0]) * gate_and_up[:, 1] * my_gate[:, None]
    ).astype(jnp.bfloat16)

    sums = [[] for _ in range(parts)]
    for step in range(1, tp_size):
        for part, other in enumerate(down(hidden, expert_down[0], step, parts)):
            sums[part].append(pass_tp(other, step))
    own = down(hidden, expert_down[0], 0, parts)

    def beside_first_sum(sent):
        sent, held["ordered"] = lax.optimization_barrier((sent, held["ordered"]))
        return sent

    def beside_last_sum(sent):
        keys = cache_in(held["ordered"], block_size, latent)
        sent, held["keys"] = lax.optimization_barrier((sent, keys))
        return sent

    moe_parts = []
    for part, order in enumerate(orders):
        final = part == parts - 1
        moe_parts.append(
            scatter_sum(
                [own[part]] + sums[part],
                order,
                row_count,
                beside_first_sum if final else None,
                beside_last_sum if final else None,
            )
        )
    moe_out = jnp.concatenate(moe_parts, axis=1)
    keys = [held["keys"]] + swap_tp(held["keys"])
    return (moe_out, attend(queries, keys, block_request, block_used))


def solution(mesh):
    placed = (
        P("ep", "tp"),
        P("ep", None),
        P("ep", None),
        P("ep", None, None, "tp"),
        P("ep", None, "tp"),
        P("ep", "tp", None),
        P("ep", None, None),
        P(),
        P("ep"),
        P("ep"),
    )
    return jax.shard_map(
        body,
        mesh=mesh,
        in_specs=placed,
        out_specs=(P("ep", "tp"), P("ep", "tp", None)),
        check_vma=False,
    )
```

```python
import functools

import jax
import jax.numpy as jnp
from jax import lax
from jax.experimental import pallas as pl
from jax.experimental.pallas import tpu as pltpu
from jax.sharding import PartitionSpec as P

KV = 512


score_scale = 192.0 ** (-0.5)

WHOLE = pl.BlockSpec(memory_space=pltpu.VMEM)


def kernel_call(kernel, out_shape, arguments, flops, in_specs=None, scratch_shapes=()):
    moved = sum(array.size * array.dtype.itemsize for array in arguments)
    out_leaves = jax.tree.leaves(out_shape)
    moved += sum(array.size * array.dtype.itemsize for array in out_leaves)
    return pl.pallas_call(
        kernel,
        out_shape=out_shape,
        in_specs=in_specs or [WHOLE] * len(arguments),
        out_specs=jax.tree.map(lambda _: WHOLE, out_shape),
        scratch_shapes=scratch_shapes,
        compiler_params=pltpu.CompilerParams(vmem_limit_bytes=54 << 20),
        cost_estimate=pl.CostEstimate(flops=flops, bytes_accessed=moved, transcendentals=0),
    )(*arguments)


def tie(values, others):
    return lax.optimization_barrier((values, others))[0]


def ep_bits():
    ep_size = lax.axis_size("ep")
    return [1 << place for place in reversed(range(ep_size.bit_length() - 1))]


def exchange(value, bit):
    ep_size = lax.axis_size("ep")
    return lax.ppermute(value, "ep", [(index, index ^ bit) for index in range(ep_size)])


def pass_tp(value, step):
    tp_size = lax.axis_size("tp")
    return lax.ppermute(
        value, "tp", [(index, (index + step) % tp_size) for index in range(tp_size)]
    )


def swap_tp(value):
    return [pass_tp(value, step) for step in range(1, lax.axis_size("tp"))]


def gather_blocks(block, order):
    value = block[None]
    for bit in order[:-1]:
        value = jnp.concatenate([value, exchange(value, bit)], axis=0)
    return value, exchange(value, order[-1])


def places_of(order):
    places = [0]
    for bit in order:
        places = places + [place ^ bit for place in places]
    return places


def join(halves, order, wanted):
    axes = len(order)
    whole = jnp.stack(halves)
    whole = whole.reshape((2,) * axes + whole.shape[2:])
    moved = [axes - 1 - order.index(bit) for bit in reversed(wanted)]
    whole = whole.transpose(moved + [axes, axes + 1])
    return whole.reshape(-1, whole.shape[-1])


def scatter_sum(terms, order, first=None, last=None):
    for bit in reversed(order):
        half = terms[0].shape[0] // 2
        sent = add_up([term[half:] for term in terms])
        if first is not None and bit == order[-1]:
            sent = first(sent)
        if last is not None and bit == order[0]:
            sent = last(sent)
        terms = [term[:half] for term in terms] + [exchange(sent, bit)]
    return add_up(terms)


def add_up(terms):
    total = terms[0].astype(jnp.float32)
    for term in terms[1:]:
        total = total + term.astype(jnp.float32)
    return total.astype(jnp.bfloat16)


def three_parts(value):
    parts = []
    for _ in range(3):
        part = lax.reduce_precision(value, 8, 7)
        parts.append(part.astype(jnp.bfloat16))
        value = value - part
    return parts


def pick(choices, index):
    value = choices[0]
    for number, choice in enumerate(choices[1:], 1):
        value = jnp.where(index == number, choice, value)
    return value


def down_kernel(step, spots, tp_size, cut, width, rows, hidden, weight, *refs):
    parts = len(spots)
    outs, held, arrived = refs[:parts], refs[parts], refs[parts + 1]
    first = lax.rem(lax.axis_index("tp") + step, tp_size) * (parts * cut)
    copies = []
    for run in range(parts * cut // width):
        start = pl.multiple_of(first + run * width, width)
        copies.append(
            pltpu.make_async_copy(
                weight.at[pl.ds(start, width)], held.at[pl.ds(run * width, width)], arrived.at[run]
            )
        )
    for copy in copies:
        copy.start()
    chunk = min(256, hidden.shape[0])
    for run, copy in enumerate(copies):
        copy.wait()
        part, column = divmod(run * width, cut)
        for row in range(0, hidden.shape[0], chunk):
            result = lax.dot_general(
                hidden[row : row + chunk],
                held[run * width : (run + 1) * width],
                (((1,), (1,)), ((), ())),
                preferred_element_type=jnp.float32,
            ).astype(jnp.bfloat16)
            for block in range(chunk // rows):
                spot = spots[part][row // rows + block] * rows
                outs[part][spot : spot + rows, column : column + width] = result[
                    block * rows : (block + 1) * rows
                ]


def down(hidden, weight, step, spots, rows):
    parts = len(spots)
    tp_size = lax.axis_size("tp")
    cut = weight.shape[0] // tp_size // parts
    width = 256 if cut % 256 == 0 else 128
    shape = jax.ShapeDtypeStruct((hidden.shape[0], cut), jnp.bfloat16)
    return kernel_call(
        functools.partial(down_kernel, step, spots, tp_size, cut, width, rows),
        [shape] * parts,
        [hidden, weight],
        flops=2 * hidden.size * cut * parts,
        in_specs=[WHOLE, pl.BlockSpec(memory_space=pl.ANY)],
        scratch_shapes=[
            pltpu.VMEM((parts * cut, weight.shape[1]), weight.dtype),
            pltpu.SemaphoreType.DMA((parts * cut // width,)),
        ],
    )


def order_kernel(index, *refs):
    rows, out = refs[:-1], refs[-1]
    columns = lax.broadcasted_iota(jnp.int32, (out.shape[0], rows[0].shape[0]), 1)
    total = jnp.zeros(out.shape, jnp.float32)
    for step, ref in enumerate(rows):
        hot = (columns == index[:, step : step + 1]).astype(jnp.bfloat16)
        total = total + jnp.dot(hot, ref[...], preferred_element_type=jnp.float32)
    out[...] = total.astype(out.dtype)


def cache_out(latent_cache):
    ep_size = lax.axis_size("ep")
    slots, block_size, latent = latent_cache.shape
    share = slots // lax.axis_size("tp")
    mine = lax.dynamic_slice_in_dim(latent_cache, lax.axis_index("tp") * share, share, axis=0)
    return mine.reshape(share, ep_size, block_size * latent // ep_size).transpose(1, 0, 2)


def cache_turn(pieces, block_source, slots):
    ep_size = lax.axis_size("ep")
    tp_size = lax.axis_size("tp")
    tp_index = lax.axis_index("tp")
    share, piece = pieces.shape[1:]
    spread = lax.all_to_all(pieces, "ep", split_axis=0, concat_axis=0, tiled=True)
    wanted = lax.dynamic_slice_in_dim(
        block_source.reshape(ep_size, tp_size, share), tp_index, 1, axis=1
    ).reshape(-1)
    place = (wanted // slots) * share + wanted % share
    holder = (wanted % slots) // share
    from_step = (tp_index + tp_size - holder) % tp_size
    index = jnp.where(
        from_step[:, None] == jnp.arange(tp_size, dtype=jnp.int32)[None, :], place[:, None], -1
    )
    rows = [part.reshape(-1, piece) for part in [spread] + swap_tp(spread)]
    shape = jax.ShapeDtypeStruct(rows[0].shape, rows[0].dtype)
    ordered = kernel_call(
        order_kernel, shape, [index] + rows, flops=2 * tp_size * rows[0].size * rows[0].shape[0]
    )
    return ordered.reshape(ep_size, share, piece)


def cache_in(ordered, block_size, latent):
    share, piece = ordered.shape[1:]
    arrived = lax.all_to_all(ordered, "ep", split_axis=0, concat_axis=0, tiled=True)
    if piece != latent:
        arrived = arrived.transpose(1, 0, 2).reshape(share, block_size, latent).transpose(1, 0, 2)
    return arrived


def attention_kernel(heads, chunk, owner, queries, *refs):
    keys, out = refs[:-1], refs[-1]
    tokens = keys[0].shape[0]
    for start in range(0, queries.shape[0], chunk):
        row = (lax.broadcasted_iota(jnp.int32, (chunk, tokens), 0) + start) // heads
        scores = []
        for step, key in enumerate(keys):
            part = lax.dot_general(
                queries[start : start + chunk],
                key[...],
                (((1,), (1,)), ((), ())),
                preferred_element_type=jnp.float32,
            )
            scores.append(
                jnp.where(row == owner[step : step + 1, :], part * score_scale, -jnp.inf)
            )
        row_max = scores[0].max(axis=1, keepdims=True)
        for part in scores[1:]:
            row_max = jnp.maximum(row_max, part.max(axis=1, keepdims=True))
        terms = [jnp.exp(part - row_max) for part in scores]
        total = sum(term.sum(axis=1, keepdims=True) for term in terms)
        attended = jnp.zeros((chunk, KV), jnp.float32)
        for term, key in zip(terms, keys):
            attended = attended + jnp.dot(
                (term / total).astype(jnp.bfloat16),
                key[:, :KV],
                preferred_element_type=jnp.float32,
            )
        out[start : start + chunk] = attended.astype(out.dtype)


def attend(queries, keys, block_request, block_used):
    tp_size = lax.axis_size("tp")
    row_count, heads, latent = queries.shape
    block_size, share = keys[0].shape[:2]
    within = jnp.arange(block_size, dtype=jnp.int32)[:, None]
    owners = []
    for step in range(tp_size):
        first = ((lax.axis_index("tp") + tp_size - step) % tp_size) * share
        owner = lax.dynamic_slice_in_dim(block_request, first, share)[None, :]
        limit = lax.dynamic_slice_in_dim(block_used, first, share)[None, :]
        owners.append(jnp.where(within < limit, owner, -1).reshape(1, -1))
    keys = [part.reshape(-1, latent) for part in keys]
    rows = queries.reshape(-1, latent)
    shape = jax.ShapeDtypeStruct((rows.shape[0], KV), jnp.bfloat16)
    result = kernel_call(
        functools.partial(attention_kernel, heads, min(256, rows.shape[0])),
        shape,
        [jnp.concatenate(owners, axis=0), rows] + keys,
        flops=4 * rows.size * keys[0].shape[0] * tp_size,
    )
    return result.reshape(row_count, heads, KV)


def body(
    tokens,
    expert_ids,
    gate_weights,
    expert_gate_up,
    expert_down,
    queries,
    latent_cache,
    block_source,
    block_request,
    block_used,
):
    row_count, top_count = expert_ids.shape
    slot_total, block_size, latent = latent_cache.shape
    ep_size = lax.axis_size("ep")
    tp_size = lax.axis_size("tp")
    tp_index = lax.axis_index("tp")
    bits = ep_bits()
    orders = (bits, bits[:-2] + [bits[-1], bits[-2]])
    parts = len(orders)
    cut = tokens.shape[1] // parts

    sent_rows = [tokens[:, part * cut : (part + 1) * cut] for part in range(parts)]
    pieces = tie(cache_out(latent_cache), sent_rows[0])
    ordered = cache_turn(pieces, block_source, slot_total)
    expert_range = jnp.arange(ep_size, dtype=jnp.int32)
    dense_gate = jnp.sum(
        jnp.where(
            expert_ids[:, :, None] == expert_range[None, None, :], gate_weights[:, :, None], 0.0
        ),
        axis=1,
    )
    gate_parts = jnp.concatenate(three_parts(dense_gate), axis=1)
    pad = -gate_parts.shape[1] % 128
    sent_rows[-1] = jnp.concatenate(
        [sent_rows[-1], jnp.pad(gate_parts, ((0, 0), (0, pad)))], axis=1
    )

    halves = [gather_blocks(rows, order) for rows, order in zip(sent_rows, orders)]
    last_sent = halves[-1][0]
    halves[-1] = (last_sent, tie(halves[-1][1], ordered))
    columns = [[None] * parts for _ in range(tp_size)]
    for part, ((early, late), order) in enumerate(zip(halves, orders)):
        passed = tie(early, last_sent) if part < parts - 1 else early
        steps = [(early, late)] + list(zip(swap_tp(passed), swap_tp(late)))
        steps = [join(pair, order, orders[0]) for pair in steps]
        if part == parts - 1:
            all_gate = steps[0][:, cut : cut + 3 * ep_size].astype(jnp.float32)
        for owner in range(tp_size):
            chosen = pick(steps, (tp_index + tp_size - owner) % tp_size)
            columns[owner][part] = chosen[:, :cut]
    mine = (jnp.arange(3 * ep_size, dtype=jnp.int32) % ep_size) == lax.axis_index("ep")
    my_gate = jnp.sum(jnp.where(mine[None, :], all_gate, 0.0), axis=1)
    gate_and_up = jnp.einsum(
        "sd,dgf->sgf",
        jnp.concatenate([column for group in columns for column in group], axis=1),
        expert_gate_up[0],
        preferred_element_type=jnp.float32,
    )
    hidden = (
        jax.nn.silu(gate_and_up[:, 0]) * gate_and_up[:, 1] * my_gate[:, None]
    ).astype(jnp.bfloat16)

    keys = cache_in(ordered, block_size, latent)
    places = [places_of(order) for order in orders]
    spots = [[held.index(place) for place in places[0]] for held in places]
    sums = [[] for _ in range(parts)]
    for step in range(1, tp_size):
        for part, other in enumerate(down(hidden, expert_down[0], step, spots, row_count)):
            sums[part].append(pass_tp(other, step))
    own = down(hidden, expert_down[0], 0, spots, row_count)

    held = {}

    def beside_first_sum(sent):
        sent, near = lax.optimization_barrier((sent, keys))
        held["attended"] = attend(queries, [near] + swap_tp(near), block_request, block_used)
        return sent

    def beside_last_sum(sent):
        sent, held["attended"] = lax.optimization_barrier((sent, held["attended"]))
        return sent

    moe_parts = []
    for part, order in enumerate(orders):
        final = part == parts - 1
        moe_parts.append(
            scatter_sum(
                [own[part]] + sums[part],
                order,
                beside_first_sum if final else None,
                beside_last_sum if final else None,
            )
        )
    return (jnp.concatenate(moe_parts, axis=1), held["attended"])


def solution(mesh):
    placed = (
        P("ep", "tp"),
        P("ep", None),
        P("ep", None),
        P("ep", None, None, "tp"),
        P("ep", None, "tp"),
        P("ep", "tp", None),
        P("ep", None, None),
        P(),
        P("ep"),
        P("ep"),
    )
    return jax.shard_map(
        body,
        mesh=mesh,
        in_specs=placed,
        out_specs=(P("ep", "tp"), P("ep", "tp", None)),
        check_vma=False,
    )
```

```python
import functools

import jax
import jax.numpy as jnp
from jax import lax
from jax.experimental import pallas as pl
from jax.experimental.pallas import tpu as pltpu
from jax.sharding import PartitionSpec as P

KV = 512


score_scale = 192.0 ** (-0.5)

WHOLE = pl.BlockSpec(memory_space=pltpu.VMEM)


def kernel_call(kernel, out_shape, arguments, flops, spare, in_specs=None, scratch_shapes=()):
    held = sum(array.size * array.dtype.itemsize for array in jax.tree.leaves(out_shape))
    for array, spec in zip(arguments, in_specs or [WHOLE] * len(arguments)):
        held += array.size * array.dtype.itemsize if spec is WHOLE else 0
    moved = sum(array.size * array.dtype.itemsize for array in arguments)
    return pl.pallas_call(
        kernel,
        out_shape=out_shape,
        in_specs=in_specs or [WHOLE] * len(arguments),
        out_specs=jax.tree.map(lambda _: WHOLE, out_shape),
        scratch_shapes=scratch_shapes,
        compiler_params=pltpu.CompilerParams(vmem_limit_bytes=held + spare),
        cost_estimate=pl.CostEstimate(
            flops=flops, bytes_accessed=moved + held, transcendentals=0
        ),
    )(*arguments)


def tie(values, others):
    return lax.optimization_barrier((values, others))[0]


def ep_bits():
    ep_size = lax.axis_size("ep")
    return [1 << place for place in reversed(range(ep_size.bit_length() - 1))]


def exchange(value, bit):
    ep_size = lax.axis_size("ep")
    return lax.ppermute(value, "ep", [(index, index ^ bit) for index in range(ep_size)])


def pass_tp(value, step):
    tp_size = lax.axis_size("tp")
    return lax.ppermute(
        value, "tp", [(index, (index + step) % tp_size) for index in range(tp_size)]
    )


def swap_tp(value):
    return [pass_tp(value, step) for step in range(1, lax.axis_size("tp"))]


def gather_rows(rows, orders, ends):
    value = rows[None]
    for bit in orders[0][:-2]:
        value = jnp.concatenate([value, exchange(value, bit)], axis=0)
    halves = []
    for order, start, end in zip(orders, (0,) + ends, ends):
        part = value[:, :, start:end]
        part = jnp.concatenate([part, exchange(part, order[-2])], axis=0)
        halves.append((part, exchange(part, order[-1])))
    return halves


def places_of(order):
    places = [0]
    for bit in order:
        places = places + [place ^ bit for place in places]
    return places


def join_kernel(spots, ends, count, tp_size, *refs):
    out = refs[-1]
    parts = len(spots)
    rows = out.shape[0] // len(spots[0])
    width = out.shape[1] // tp_size
    index = lax.axis_index("tp")

    def place(tp_index):
        for step in range(tp_size):
            owner = (tp_index - step) % tp_size
            for part in range(parts):
                start, end = ((0,) + ends)[part], ends[part]
                for half in range(2):
                    ref = refs[(step * parts + part) * 2 + half]
                    blocks = ref.shape[0] // rows
                    for block in range(blocks):
                        spot = spots[part][half * blocks + block] * rows
                        out[spot : spot + rows, owner * width + start : owner * width + end] = ref[
                            block * rows : (block + 1) * rows, : end - start
                        ]

    for tp_index in range(tp_size):
        pl.when(index == tp_index)(functools.partial(place, tp_index))


def join_rows(by_step, spots, ends, rows):
    tp_size = len(by_step)
    arrays = [
        half.reshape(-1, half.shape[-1]) for parts in by_step for pair in parts for half in pair
    ]
    shape = jax.ShapeDtypeStruct((len(spots[0]) * rows, ends[-1] * tp_size), jnp.bfloat16)
    return kernel_call(
        functools.partial(join_kernel, spots, ends, len(arrays), tp_size),
        shape,
        arrays,
        flops=0,
        spare=4 << 20,
    )


def scatter_sums(totals, orders, hooks):
    steps = len(orders[0])
    for step in range(steps):
        if step == 2:
            totals = [jnp.concatenate(totals, axis=1)]
        half = totals[0].shape[0] // 2
        sents = [total[half:] for total in totals]
        if step in hooks:
            sents[-1] = hooks[step](sents[-1])
        totals = [
            add_up([total[:half], exchange(sent, order[steps - 1 - step])])
            for total, sent, order in zip(totals, sents, orders)
        ]
    return totals[0]


def add_up(terms):
    total = terms[0].astype(jnp.float32)
    for term in terms[1:]:
        total = total + term.astype(jnp.float32)
    return total.astype(jnp.bfloat16)


def three_parts(value):
    parts = []
    for _ in range(3):
        part = lax.reduce_precision(value, 8, 7)
        parts.append(part.astype(jnp.bfloat16))
        value = value - part
    return parts


def down_kernel(spots, tp_size, cut, width, rows, hidden, weight, *refs):
    parts = len(spots)
    outs, (held, turned, arrived) = refs[:-3], refs[-3:]
    copies = []
    for step in range(tp_size):
        target = lax.rem(lax.axis_index("tp") + step + 1, tp_size)
        for part in range(parts):
            run = step * parts + part
            start = pl.multiple_of((target * parts + part) * cut, cut)
            copies.append(
                pltpu.make_async_copy(
                    weight.at[pl.ds(start, cut)],
                    held.at[pl.ds(run * cut, cut)],
                    arrived.at[run],
                )
            )
    for copy in copies:
        copy.start()
    chunk = min(256, hidden.shape[0])
    for part in range(parts):
        for block, spot in enumerate(spots[part]):
            turned[part, spot * rows : (spot + 1) * rows] = hidden[
                block * rows : (block + 1) * rows
            ]
    for run, copy in enumerate(copies):
        copy.wait()
        for column in range(0, cut, width):
            for row in range(0, hidden.shape[0], chunk):
                outs[run][row : row + chunk, column : column + width] = lax.dot_general(
                    turned[run % parts, row : row + chunk],
                    held[run * cut + column : run * cut + column + width],
                    (((1,), (1,)), ((), ())),
                    preferred_element_type=jnp.float32,
                ).astype(jnp.bfloat16)


def down(hidden, weight, spots, rows):
    parts = len(spots)
    tp_size = lax.axis_size("tp")
    cut = weight.shape[0] // tp_size // parts
    width = 256 if cut % 256 == 0 else 128
    shape = jax.ShapeDtypeStruct((hidden.shape[0], cut), jnp.bfloat16)
    outs = kernel_call(
        functools.partial(down_kernel, spots, tp_size, cut, width, rows),
        [shape] * (parts * tp_size),
        [hidden, weight],
        flops=2 * hidden.size * weight.shape[0],
        spare=weight.size * 2 + (4 << 20),
        in_specs=[WHOLE, pl.BlockSpec(memory_space=pl.ANY)],
        scratch_shapes=[
            pltpu.VMEM(weight.shape, weight.dtype),
            pltpu.VMEM((parts,) + hidden.shape, hidden.dtype),
            pltpu.SemaphoreType.DMA((parts * tp_size,)),
        ],
    )
    return [outs[step * parts : (step + 1) * parts] for step in range(tp_size)]


def order_kernel(index, *refs):
    rows, out = refs[:-1], refs[-1]
    columns = lax.broadcasted_iota(jnp.int32, (out.shape[0], rows[0].shape[0]), 1)
    total = jnp.zeros(out.shape, jnp.float32)
    for step, ref in enumerate(rows):
        hot = (columns == index[:, step : step + 1]).astype(jnp.bfloat16)
        total = total + jnp.dot(hot, ref[...], preferred_element_type=jnp.float32)
    out[...] = total.astype(out.dtype)


def cache_out(latent_cache):
    ep_size = lax.axis_size("ep")
    slots, block_size, latent = latent_cache.shape
    share = slots // lax.axis_size("tp")
    mine = lax.dynamic_slice_in_dim(latent_cache, lax.axis_index("tp") * share, share, axis=0)
    return mine.reshape(share, ep_size, block_size * latent // ep_size).transpose(1, 0, 2)


def cache_turn(pieces, block_source, slots):
    ep_size = lax.axis_size("ep")
    tp_size = lax.axis_size("tp")
    tp_index = lax.axis_index("tp")
    share, piece = pieces.shape[1:]
    spread = lax.all_to_all(pieces, "ep", split_axis=0, concat_axis=0, tiled=True)
    wanted = lax.dynamic_slice_in_dim(
        block_source.reshape(ep_size, tp_size, share), tp_index, 1, axis=1
    ).reshape(-1)
    place = (wanted // slots) * share + wanted % share
    holder = (wanted % slots) // share
    from_step = (tp_index + tp_size - holder) % tp_size
    index = jnp.where(
        from_step[:, None] == jnp.arange(tp_size, dtype=jnp.int32)[None, :], place[:, None], -1
    )
    rows = [part.reshape(-1, piece) for part in [spread] + swap_tp(spread)]
    shape = jax.ShapeDtypeStruct(rows[0].shape, rows[0].dtype)
    ordered = kernel_call(
        order_kernel,
        shape,
        [index] + rows,
        flops=2 * tp_size * rows[0].size * rows[0].shape[0],
        spare=6 << 20,
    )
    return ordered.reshape(ep_size, share, piece)


def cache_in(ordered, block_size, latent):
    share, piece = ordered.shape[1:]
    arrived = lax.all_to_all(ordered, "ep", split_axis=0, concat_axis=0, tiled=True)
    if piece != latent:
        arrived = arrived.transpose(1, 0, 2).reshape(share, block_size, latent).transpose(1, 0, 2)
    return arrived


def attention_kernel(chunk, owner, request, queries, *refs):
    keys, out = refs[:-1], refs[-1]
    for start in range(0, queries.shape[0], chunk):
        row = request[start : start + chunk]
        scores = []
        for step, key in enumerate(keys):
            part = lax.dot_general(
                queries[start : start + chunk],
                key[...],
                (((1,), (1,)), ((), ())),
                preferred_element_type=jnp.float32,
            )
            scores.append(
                jnp.where(row == owner[step : step + 1, :], part * score_scale, -jnp.inf)
            )
        row_max = scores[0].max(axis=1, keepdims=True)
        for part in scores[1:]:
            row_max = jnp.maximum(row_max, part.max(axis=1, keepdims=True))
        terms = [jnp.exp(part - row_max) for part in scores]
        total = 1.0 / sum(term.sum(axis=1, keepdims=True) for term in terms)
        attended = jnp.zeros((chunk, KV), jnp.float32)
        for term, key in zip(terms, keys):
            attended = attended + jnp.dot(
                (term * total).astype(jnp.bfloat16),
                key[:, :KV],
                preferred_element_type=jnp.float32,
            )
        out[start : start + chunk] = attended.astype(out.dtype)


def attend(queries, keys, block_request, block_used):
    tp_size = lax.axis_size("tp")
    row_count, heads, latent = queries.shape
    block_size, share = keys[0].shape[:2]
    within = jnp.arange(block_size, dtype=jnp.int32)[:, None]
    owners = []
    for step in range(tp_size):
        first = ((lax.axis_index("tp") + tp_size - step) % tp_size) * share
        owner = lax.dynamic_slice_in_dim(block_request, first, share)[None, :]
        limit = lax.dynamic_slice_in_dim(block_used, first, share)[None, :]
        owners.append(jnp.where(within < limit, owner, -1).reshape(1, -1))
    keys = [part.reshape(-1, latent) for part in keys]
    rows = queries.reshape(-1, latent)
    request = jnp.repeat(jnp.arange(row_count, dtype=jnp.int32), heads)[:, None]
    shape = jax.ShapeDtypeStruct((rows.shape[0], KV), jnp.bfloat16)
    result = kernel_call(
        functools.partial(attention_kernel, min(256, rows.shape[0])),
        shape,
        [jnp.concatenate(owners, axis=0), request, rows] + keys,
        flops=4 * rows.size * keys[0].shape[0] * tp_size,
        spare=8 << 20,
    )
    return result.reshape(row_count, heads, KV)


def body(
    tokens,
    expert_ids,
    gate_weights,
    expert_gate_up,
    expert_down,
    queries,
    latent_cache,
    block_source,
    block_request,
    block_used,
):
    row_count, top_count = expert_ids.shape
    slot_total, block_size, latent = latent_cache.shape
    ep_size = lax.axis_size("ep")
    tp_size = lax.axis_size("tp")
    tp_index = lax.axis_index("tp")
    bits = ep_bits()
    orders = (bits, bits[:-2] + [bits[-1], bits[-2]])
    parts = len(orders)
    cut = tokens.shape[1] // parts

    expert_range = jnp.arange(ep_size, dtype=jnp.int32)
    dense_gate = jnp.sum(
        jnp.where(
            expert_ids[:, :, None] == expert_range[None, None, :], gate_weights[:, :, None], 0.0
        ),
        axis=1,
    )
    gate_parts = jnp.concatenate(three_parts(dense_gate), axis=1)
    pad = -gate_parts.shape[1] % 128
    sent_rows = jnp.concatenate([tokens, jnp.pad(gate_parts, ((0, 0), (0, pad)))], axis=1)
    ends = tuple(cut * part for part in range(1, parts)) + (sent_rows.shape[1],)

    halves = gather_rows(sent_rows, orders, ends)
    last_sent = halves[-1][0]
    pieces = tie(cache_out(latent_cache), last_sent)
    ordered = cache_turn(pieces, block_source, slot_total)
    places = [places_of(order) for order in orders]
    to_first = [[places[0].index(place) for place in own] for own in places]
    from_first = [[own.index(place) for place in places[0]] for own in places]

    passed = [tie(early, last_sent) for early, _ in halves[:-1]]
    passed.append(tie(last_sent, halves[0][1]))
    arrived = [
        [(pass_tp(early, step), pass_tp(late, step)) for early, (_, late) in zip(passed, halves)]
        for step in range(1, tp_size)
    ]
    all_rows = join_rows(
        [halves] + arrived, to_first, tuple(cut * part for part in range(1, parts + 1)), row_count
    )
    gate_halves = [half[..., cut : cut + 3 * ep_size] for half in halves[-1]]
    all_gate = jnp.concatenate(gate_halves, axis=0)
    all_gate = jnp.stack([all_gate[block] for block in from_first[-1]]).astype(jnp.float32)
    mine = (jnp.arange(3 * ep_size, dtype=jnp.int32) % ep_size) == lax.axis_index("ep")
    my_gate = jnp.sum(jnp.where(mine, all_gate, 0.0), axis=2).reshape(-1)
    gate_and_up = jnp.einsum(
        "sd,dgf->sgf", all_rows, expert_gate_up[0], preferred_element_type=jnp.float32
    )
    hidden = (
        jax.nn.silu(gate_and_up[:, 0]) * gate_and_up[:, 1] * my_gate[:, None]
    ).astype(jnp.bfloat16)

    hidden = tie(hidden, ordered)
    by_step = down(hidden, expert_down[0], from_first, row_count)
    ordered = tie(ordered, by_step)
    sums = list(by_step[-1])
    for part in range(parts):
        others = [pass_tp(by_step[step - 1][part], step) for step in range(1, tp_size)]
        sums[part] = add_up([sums[part]] + others)
    keys = cache_in(ordered, block_size, latent)

    held = {}

    def beside_second_sum(sent):
        sent, near = lax.optimization_barrier((sent, keys))
        held["attended"] = attend(queries, [near] + swap_tp(near), block_request, block_used)
        return sent

    def beside_last_sum(sent):
        sent, held["attended"] = lax.optimization_barrier((sent, held["attended"]))
        return sent

    hooks = {1: beside_second_sum, len(bits) - 1: beside_last_sum}
    return (scatter_sums(sums, orders, hooks), held["attended"])


def solution(mesh):
    placed = (
        P("ep", "tp"),
        P("ep", None),
        P("ep", None),
        P("ep", None, None, "tp"),
        P("ep", None, "tp"),
        P("ep", "tp", None),
        P("ep", None, None),
        P(),
        P("ep"),
        P("ep"),
    )
    return jax.shard_map(
        body,
        mesh=mesh,
        in_specs=placed,
        out_specs=(P("ep", "tp"), P("ep", "tp", None)),
        check_vma=False,
    )
```

```python
import functools

import jax
import jax.numpy as jnp
from jax import lax
from jax.experimental import pallas as pl
from jax.experimental.pallas import tpu as pltpu
from jax.sharding import PartitionSpec as P

KV = 512


score_scale = 192.0 ** (-0.5)

WHOLE = pl.BlockSpec(memory_space=pltpu.VMEM)


def kernel_call(kernel, out_shape, arguments, flops, spare, in_specs=None, scratch_shapes=()):
    held = sum(array.size * array.dtype.itemsize for array in jax.tree.leaves(out_shape))
    for array, spec in zip(arguments, in_specs or [WHOLE] * len(arguments)):
        held += array.size * array.dtype.itemsize if spec is WHOLE else 0
    moved = sum(array.size * array.dtype.itemsize for array in arguments)
    return pl.pallas_call(
        kernel,
        out_shape=out_shape,
        in_specs=in_specs or [WHOLE] * len(arguments),
        out_specs=jax.tree.map(lambda _: WHOLE, out_shape),
        scratch_shapes=scratch_shapes,
        compiler_params=pltpu.CompilerParams(vmem_limit_bytes=held + spare),
        cost_estimate=pl.CostEstimate(
            flops=flops, bytes_accessed=moved + held, transcendentals=0
        ),
    )(*arguments)


def tie(values, others):
    return lax.optimization_barrier((values, others))[0]


def ep_bits():
    ep_size = lax.axis_size("ep")
    return [1 << place for place in reversed(range(ep_size.bit_length() - 1))]


def exchange(value, bit):
    ep_size = lax.axis_size("ep")
    return lax.ppermute(value, "ep", [(index, index ^ bit) for index in range(ep_size)])


def pass_tp(value, step):
    tp_size = lax.axis_size("tp")
    return lax.ppermute(
        value, "tp", [(index, (index + step) % tp_size) for index in range(tp_size)]
    )


def swap_tp(value):
    return [pass_tp(value, step) for step in range(1, lax.axis_size("tp"))]


def gather_rows(rows, others, orders, ends):
    shared = orders[0][:-2]
    values = [
        jnp.concatenate([value[None], exchange(value[None], shared[0])], axis=0)
        for value in (rows, others)
    ]
    value = jnp.concatenate(values, axis=2)
    for bit in shared[1:]:
        shared_sent = value
        value = jnp.concatenate([value, exchange(value, bit)], axis=0)
    halves = []
    for order, start, end in zip(orders, (0,) + ends, ends):
        part = value[:, :, start:end]
        part = jnp.concatenate([part, exchange(part, order[-2])], axis=0)
        halves.append((part, exchange(part, order[-1])))
    return halves, shared_sent


def places_of(order):
    places = [0]
    for bit in order:
        places = places + [place ^ bit for place in places]
    return places


def join_kernel(spots, ends, count, tp_size, *refs):
    out = refs[-1]
    parts = len(spots)
    rows = out.shape[0] // len(spots[0])
    width = out.shape[1] // tp_size
    index = lax.axis_index("tp")

    def place(tp_index):
        for step in range(tp_size):
            owner = (tp_index - step) % tp_size
            for part in range(parts):
                start, end = ((0,) + ends)[part], ends[part]
                for half in range(2):
                    ref = refs[(step * parts + part) * 2 + half]
                    blocks = ref.shape[0] // rows
                    for block in range(blocks):
                        spot = spots[part][half * blocks + block] * rows
                        out[spot : spot + rows, owner * width + start : owner * width + end] = ref[
                            block * rows : (block + 1) * rows, : end - start
                        ]

    for tp_index in range(tp_size):
        pl.when(index == tp_index)(functools.partial(place, tp_index))


def join_rows(by_step, spots, ends, rows):
    tp_size = len(by_step)
    arrays = [
        half.reshape(-1, half.shape[-1]) for parts in by_step for pair in parts for half in pair
    ]
    shape = jax.ShapeDtypeStruct((len(spots[0]) * rows, ends[-1] * tp_size), jnp.bfloat16)
    return kernel_call(
        functools.partial(join_kernel, spots, ends, len(arrays), tp_size),
        shape,
        arrays,
        flops=0,
        spare=4 << 20,
    )


def scatter_sums(totals, orders, hooks):
    steps = len(orders[0])
    for step in range(steps):
        if step == 2:
            totals = [jnp.concatenate(totals, axis=1)]
        half = totals[0].shape[0] // 2
        sents = [total[half:] for total in totals]
        if step in hooks:
            sents[-1] = hooks[step](sents[-1])
        totals = [
            add_up([total[:half], exchange(sent, order[steps - 1 - step])])
            for total, sent, order in zip(totals, sents, orders)
        ]
    return totals[0]


def add_up(terms):
    total = terms[0].astype(jnp.float32)
    for term in terms[1:]:
        total = total + term.astype(jnp.float32)
    return total.astype(jnp.bfloat16)


def three_parts(value):
    parts = []
    for _ in range(3):
        part = lax.reduce_precision(value, 8, 7)
        parts.append(part.astype(jnp.bfloat16))
        value = value - part
    return parts


def down_kernel(spots, tp_size, cut, width, rows, hidden, weight, *refs):
    parts = len(spots)
    outs, (held, turned, arrived) = refs[:-3], refs[-3:]
    copies = []
    for step in range(tp_size):
        target = lax.rem(lax.axis_index("tp") + step + 1, tp_size)
        for part in range(parts):
            run = step * parts + part
            start = pl.multiple_of((target * parts + part) * cut, cut)
            copies.append(
                pltpu.make_async_copy(
                    weight.at[pl.ds(start, cut)],
                    held.at[pl.ds(run * cut, cut)],
                    arrived.at[run],
                )
            )
    for copy in copies:
        copy.start()
    chunk = min(256, hidden.shape[0])
    for part in range(parts):
        for block, spot in enumerate(spots[part]):
            turned[part, spot * rows : (spot + 1) * rows] = hidden[
                block * rows : (block + 1) * rows
            ]
    for run, copy in enumerate(copies):
        copy.wait()
        for column in range(0, cut, width):
            for row in range(0, hidden.shape[0], chunk):
                outs[run][row : row + chunk, column : column + width] = lax.dot_general(
                    turned[run % parts, row : row + chunk],
                    held[run * cut + column : run * cut + column + width],
                    (((1,), (1,)), ((), ())),
                    preferred_element_type=jnp.float32,
                ).astype(jnp.bfloat16)


def down(hidden, weight, spots, rows):
    parts = len(spots)
    tp_size = lax.axis_size("tp")
    cut = weight.shape[0] // tp_size // parts
    width = 256 if cut % 256 == 0 else 128
    shape = jax.ShapeDtypeStruct((hidden.shape[0], cut), jnp.bfloat16)
    outs = kernel_call(
        functools.partial(down_kernel, spots, tp_size, cut, width, rows),
        [shape] * (parts * tp_size),
        [hidden, weight],
        flops=2 * hidden.size * weight.shape[0],
        spare=weight.size * 2 + (4 << 20),
        in_specs=[WHOLE, pl.BlockSpec(memory_space=pl.ANY)],
        scratch_shapes=[
            pltpu.VMEM(weight.shape, weight.dtype),
            pltpu.VMEM((parts,) + hidden.shape, hidden.dtype),
            pltpu.SemaphoreType.DMA((parts * tp_size,)),
        ],
    )
    return [outs[step * parts : (step + 1) * parts] for step in range(tp_size)]


def order_kernel(index, *refs):
    rows, out = refs[:-1], refs[-1]
    columns = lax.broadcasted_iota(jnp.int32, (out.shape[0], rows[0].shape[0]), 1)
    total = jnp.zeros(out.shape, jnp.float32)
    for step, ref in enumerate(rows):
        hot = (columns == index[:, step : step + 1]).astype(jnp.bfloat16)
        total = total + jnp.dot(hot, ref[...], preferred_element_type=jnp.float32)
    out[...] = total.astype(out.dtype)


def cache_out(latent_cache):
    ep_size = lax.axis_size("ep")
    slots, block_size, latent = latent_cache.shape
    share = slots // lax.axis_size("tp")
    mine = lax.dynamic_slice_in_dim(latent_cache, lax.axis_index("tp") * share, share, axis=0)
    return mine.reshape(share, ep_size, block_size * latent // ep_size).transpose(1, 0, 2)


def cache_turn(pieces, block_source, slots, before):
    ep_size = lax.axis_size("ep")
    tp_size = lax.axis_size("tp")
    tp_index = lax.axis_index("tp")
    share, piece = pieces.shape[1:]
    spread = lax.all_to_all(pieces, "ep", split_axis=0, concat_axis=0, tiled=True)
    spread = tie(spread, before)
    wanted = lax.dynamic_slice_in_dim(
        block_source.reshape(ep_size, tp_size, share), tp_index, 1, axis=1
    ).reshape(-1)
    place = (wanted // slots) * share + wanted % share
    holder = (wanted % slots) // share
    from_step = (tp_index + tp_size - holder) % tp_size
    index = jnp.where(
        from_step[:, None] == jnp.arange(tp_size, dtype=jnp.int32)[None, :], place[:, None], -1
    )
    rows = [part.reshape(-1, piece) for part in [spread] + swap_tp(spread)]
    shape = jax.ShapeDtypeStruct(rows[0].shape, rows[0].dtype)
    ordered = kernel_call(
        order_kernel,
        shape,
        [index] + rows,
        flops=2 * tp_size * rows[0].size * rows[0].shape[0],
        spare=6 << 20,
    )
    return ordered.reshape(ep_size, share, piece)


def cache_in(ordered, block_size, latent):
    share, piece = ordered.shape[1:]
    arrived = lax.all_to_all(ordered, "ep", split_axis=0, concat_axis=0, tiled=True)
    if piece != latent:
        arrived = arrived.transpose(1, 0, 2).reshape(share, block_size, latent).transpose(1, 0, 2)
    return arrived


def attention_kernel(chunk, owner, request, queries, *refs):
    keys, out = refs[:-1], refs[-1]
    for start in range(0, queries.shape[0], chunk):
        row = request[start : start + chunk]
        scores = []
        for step, key in enumerate(keys):
            part = lax.dot_general(
                queries[start : start + chunk],
                key[...],
                (((1,), (1,)), ((), ())),
                preferred_element_type=jnp.float32,
            )
            scores.append(
                jnp.where(row == owner[step : step + 1, :], part * score_scale, -jnp.inf)
            )
        row_max = scores[0].max(axis=1, keepdims=True)
        for part in scores[1:]:
            row_max = jnp.maximum(row_max, part.max(axis=1, keepdims=True))
        terms = [jnp.exp(part - row_max) for part in scores]
        total = 1.0 / sum(term.sum(axis=1, keepdims=True) for term in terms)
        attended = jnp.zeros((chunk, KV), jnp.float32)
        for term, key in zip(terms, keys):
            attended = attended + jnp.dot(
                (term * total).astype(jnp.bfloat16),
                key[:, :KV],
                preferred_element_type=jnp.float32,
            )
        out[start : start + chunk] = attended.astype(out.dtype)


def attend(queries, keys, block_request, block_used):
    tp_size = lax.axis_size("tp")
    row_count, heads, latent = queries.shape
    block_size, share = keys[0].shape[:2]
    within = jnp.arange(block_size, dtype=jnp.int32)[:, None]
    owners = []
    for step in range(tp_size):
        first = ((lax.axis_index("tp") + tp_size - step) % tp_size) * share
        owner = lax.dynamic_slice_in_dim(block_request, first, share)[None, :]
        limit = lax.dynamic_slice_in_dim(block_used, first, share)[None, :]
        owners.append(jnp.where(within < limit, owner, -1).reshape(1, -1))
    keys = [part.reshape(-1, latent) for part in keys]
    rows = queries.reshape(-1, latent)
    request = jnp.repeat(jnp.arange(row_count, dtype=jnp.int32), heads)[:, None]
    shape = jax.ShapeDtypeStruct((rows.shape[0], KV), jnp.bfloat16)
    result = kernel_call(
        functools.partial(attention_kernel, min(256, rows.shape[0])),
        shape,
        [jnp.concatenate(owners, axis=0), request, rows] + keys,
        flops=4 * rows.size * keys[0].shape[0] * tp_size,
        spare=8 << 20,
    )
    return result.reshape(row_count, heads, KV)


def body(
    tokens,
    expert_ids,
    gate_weights,
    expert_gate_up,
    expert_down,
    queries,
    latent_cache,
    block_source,
    block_request,
    block_used,
):
    row_count, top_count = expert_ids.shape
    slot_total, block_size, latent = latent_cache.shape
    ep_size = lax.axis_size("ep")
    tp_size = lax.axis_size("tp")
    tp_index = lax.axis_index("tp")
    bits = ep_bits()
    orders = (bits, bits[:-2] + [bits[-1], bits[-2]])
    parts = len(orders)
    cut = tokens.shape[1] // parts

    expert_range = jnp.arange(ep_size, dtype=jnp.int32)
    dense_gate = jnp.sum(
        jnp.where(
            expert_ids[:, :, None] == expert_range[None, None, :], gate_weights[:, :, None], 0.0
        ),
        axis=1,
    )
    gate_parts = jnp.concatenate(three_parts(dense_gate), axis=1)
    pad = -gate_parts.shape[1] % 128
    gates = jnp.pad(gate_parts, ((0, 0), (0, pad)))
    ends = tuple(cut * part for part in range(1, parts)) + (tokens.shape[1] + gates.shape[1],)
    halves, shared_sent = gather_rows(tokens, gates, orders, ends)
    last_sent = halves[-1][0]
    pieces = tie(cache_out(latent_cache), shared_sent)
    ordered = cache_turn(pieces, block_source, slot_total, last_sent)
    keys = cache_in(ordered, block_size, latent)
    places = [places_of(order) for order in orders]
    to_first = [[places[0].index(place) for place in own] for own in places]
    from_first = [[own.index(place) for place in places[0]] for own in places]

    passed = [tie(early, last_sent) for early, _ in halves[:-1]]
    passed.append(tie(last_sent, halves[0][1]))
    arrived = [
        [(pass_tp(early, step), pass_tp(late, step)) for early, (_, late) in zip(passed, halves)]
        for step in range(1, tp_size)
    ]
    all_rows = join_rows(
        [halves] + arrived, to_first, tuple(cut * part for part in range(1, parts + 1)), row_count
    )
    gate_halves = [half[..., cut : cut + 3 * ep_size] for half in halves[-1]]
    all_gate = jnp.concatenate(gate_halves, axis=0)
    all_gate = jnp.stack([all_gate[block] for block in from_first[-1]]).astype(jnp.float32)
    mine = (jnp.arange(3 * ep_size, dtype=jnp.int32) % ep_size) == lax.axis_index("ep")
    my_gate = jnp.sum(jnp.where(mine, all_gate, 0.0), axis=2).reshape(-1)
    gate_and_up = jnp.einsum(
        "sd,dgf->sgf", all_rows, expert_gate_up[0], preferred_element_type=jnp.float32
    )
    hidden = (
        jax.nn.silu(gate_and_up[:, 0]) * gate_and_up[:, 1] * my_gate[:, None]
    ).astype(jnp.bfloat16)

    by_step = down(hidden, expert_down[0], from_first, row_count)
    sums = list(by_step[-1])
    for part in range(parts):
        others = [pass_tp(by_step[step - 1][part], step) for step in range(1, tp_size)]
        sums[part] = add_up([sums[part]] + others)

    held = {}

    def beside_first_sum(sent):
        sent, near = lax.optimization_barrier((sent, keys))
        held["attended"] = attend(queries, [near] + swap_tp(near), block_request, block_used)
        return sent

    def beside_second_sum(sent):
        sent, held["attended"] = lax.optimization_barrier((sent, held["attended"]))
        return sent

    hooks = {0: beside_first_sum, 1: beside_second_sum}
    return (scatter_sums(sums, orders, hooks), held["attended"])


def solution(mesh):
    placed = (
        P("ep", "tp"),
        P("ep", None),
        P("ep", None),
        P("ep", None, None, "tp"),
        P("ep", None, "tp"),
        P("ep", "tp", None),
        P("ep", None, None),
        P(),
        P("ep"),
        P("ep"),
    )
    return jax.shard_map(
        body,
        mesh=mesh,
        in_specs=placed,
        out_specs=(P("ep", "tp"), P("ep", "tp", None)),
        check_vma=False,
    )
```

```python
import functools

import jax
import jax.numpy as jnp
from jax import lax
from jax.experimental import pallas as pl
from jax.experimental.pallas import tpu as pltpu
from jax.sharding import PartitionSpec as P

KV = 512


score_scale = 192.0 ** (-0.5)

WHOLE = pl.BlockSpec(memory_space=pltpu.VMEM)


def kernel_call(kernel, out_shape, arguments, flops, spare, in_specs=None, scratch_shapes=()):
    held = sum(array.size * array.dtype.itemsize for array in jax.tree.leaves(out_shape))
    for array, spec in zip(arguments, in_specs or [WHOLE] * len(arguments)):
        held += array.size * array.dtype.itemsize if spec is WHOLE else 0
    moved = sum(array.size * array.dtype.itemsize for array in arguments)
    return pl.pallas_call(
        kernel,
        out_shape=out_shape,
        in_specs=in_specs or [WHOLE] * len(arguments),
        out_specs=jax.tree.map(lambda _: WHOLE, out_shape),
        scratch_shapes=scratch_shapes,
        compiler_params=pltpu.CompilerParams(vmem_limit_bytes=held + spare),
        cost_estimate=pl.CostEstimate(
            flops=flops, bytes_accessed=moved + held, transcendentals=0
        ),
    )(*arguments)


def tie(values, others):
    return lax.optimization_barrier((values, others))[0]


def ep_bits():
    ep_size = lax.axis_size("ep")
    return [1 << place for place in reversed(range(ep_size.bit_length() - 1))]


def exchange(value, bit):
    ep_size = lax.axis_size("ep")
    return lax.ppermute(value, "ep", [(index, index ^ bit) for index in range(ep_size)])


def pass_tp(value, step):
    tp_size = lax.axis_size("tp")
    return lax.ppermute(
        value, "tp", [(index, (index + step) % tp_size) for index in range(tp_size)]
    )


def swap_tp(value):
    return [pass_tp(value, step) for step in range(1, lax.axis_size("tp"))]


def gather_rows(rows, others, orders, ends):
    shared = orders[0][:-2]
    values = [
        jnp.concatenate([value[None], exchange(value[None], shared[0])], axis=0)
        for value in (rows, others)
    ]
    value = jnp.concatenate(values, axis=2)
    for bit in shared[1:]:
        value = jnp.concatenate([value, exchange(value, bit)], axis=0)
    halves = []
    for order, start, end in zip(orders, (0,) + ends, ends):
        part = value[:, :, start:end]
        part = jnp.concatenate([part, exchange(part, order[-2])], axis=0)
        halves.append((part, exchange(part, order[-1])))
    return halves


def places_of(order):
    places = [0]
    for bit in order:
        places = places + [place ^ bit for place in places]
    return places


def join_kernel(spots, ends, count, tp_size, *refs):
    out = refs[-1]
    parts = len(spots)
    rows = out.shape[0] // len(spots[0])
    width = out.shape[1] // tp_size
    index = lax.axis_index("tp")

    def place(tp_index):
        for step in range(tp_size):
            owner = (tp_index - step) % tp_size
            for part in range(parts):
                start, end = ((0,) + ends)[part], ends[part]
                for half in range(2):
                    ref = refs[(step * parts + part) * 2 + half]
                    blocks = ref.shape[0] // rows
                    for block in range(blocks):
                        spot = spots[part][half * blocks + block] * rows
                        out[spot : spot + rows, owner * width + start : owner * width + end] = ref[
                            block * rows : (block + 1) * rows, : end - start
                        ]

    for tp_index in range(tp_size):
        pl.when(index == tp_index)(functools.partial(place, tp_index))


def join_rows(by_step, spots, ends, rows):
    tp_size = len(by_step)
    arrays = [
        half.reshape(-1, half.shape[-1]) for parts in by_step for pair in parts for half in pair
    ]
    shape = jax.ShapeDtypeStruct((len(spots[0]) * rows, ends[-1] * tp_size), jnp.bfloat16)
    return kernel_call(
        functools.partial(join_kernel, spots, ends, len(arrays), tp_size),
        shape,
        arrays,
        flops=0,
        spare=4 << 20,
    )


def scatter_sums(totals, orders, hooks):
    steps = len(orders[0])
    for step in range(steps):
        if step == 2:
            totals = [jnp.concatenate(totals, axis=1)]
        half = totals[0].shape[0] // 2
        sents = [total[half:] for total in totals]
        if step in hooks:
            sents[-1] = hooks[step](sents[-1])
        totals = [
            add_up([total[:half], exchange(sent, order[steps - 1 - step])])
            for total, sent, order in zip(totals, sents, orders)
        ]
    return totals[0]


def add_up(terms):
    total = terms[0].astype(jnp.float32)
    for term in terms[1:]:
        total = total + term.astype(jnp.float32)
    return total.astype(jnp.bfloat16)


def three_parts(value):
    parts = []
    for _ in range(3):
        part = lax.reduce_precision(value, 8, 7)
        parts.append(part.astype(jnp.bfloat16))
        value = value - part
    return parts


def down_kernel(spots, tp_size, cut, width, rows, hidden, weight, *refs):
    parts = len(spots)
    outs, (held, turned, arrived) = refs[:-3], refs[-3:]
    copies = []
    for step in range(tp_size):
        target = lax.rem(lax.axis_index("tp") + step + 1, tp_size)
        for part in range(parts):
            run = step * parts + part
            start = pl.multiple_of((target * parts + part) * cut, cut)
            copies.append(
                pltpu.make_async_copy(
                    weight.at[pl.ds(start, cut)],
                    held.at[pl.ds(run * cut, cut)],
                    arrived.at[run],
                )
            )
    for copy in copies:
        copy.start()
    chunk = min(256, hidden.shape[0])
    for part in range(parts):
        for block, spot in enumerate(spots[part]):
            turned[part, spot * rows : (spot + 1) * rows] = hidden[
                block * rows : (block + 1) * rows
            ]
    for run, copy in enumerate(copies):
        copy.wait()
        for column in range(0, cut, width):
            for row in range(0, hidden.shape[0], chunk):
                outs[run][row : row + chunk, column : column + width] = lax.dot_general(
                    turned[run % parts, row : row + chunk],
                    held[run * cut + column : run * cut + column + width],
                    (((1,), (1,)), ((), ())),
                    preferred_element_type=jnp.float32,
                ).astype(jnp.bfloat16)


def down(hidden, weight, spots, rows):
    parts = len(spots)
    tp_size = lax.axis_size("tp")
    cut = weight.shape[0] // tp_size // parts
    width = 256 if cut % 256 == 0 else 128
    shape = jax.ShapeDtypeStruct((hidden.shape[0], cut), jnp.bfloat16)
    outs = kernel_call(
        functools.partial(down_kernel, spots, tp_size, cut, width, rows),
        [shape] * (parts * tp_size),
        [hidden, weight],
        flops=2 * hidden.size * weight.shape[0],
        spare=weight.size * 2 + (4 << 20),
        in_specs=[WHOLE, pl.BlockSpec(memory_space=pl.ANY)],
        scratch_shapes=[
            pltpu.VMEM(weight.shape, weight.dtype),
            pltpu.VMEM((parts,) + hidden.shape, hidden.dtype),
            pltpu.SemaphoreType.DMA((parts * tp_size,)),
        ],
    )
    return [outs[step * parts : (step + 1) * parts] for step in range(tp_size)]


def order_kernel(index, *refs):
    rows, out = refs[:-1], refs[-1]
    columns = lax.broadcasted_iota(jnp.int32, (out.shape[0], rows[0].shape[0]), 1)
    total = jnp.zeros(out.shape, jnp.float32)
    for step, ref in enumerate(rows):
        hot = (columns == index[:, step : step + 1]).astype(jnp.bfloat16)
        total = total + jnp.dot(hot, ref[...], preferred_element_type=jnp.float32)
    out[...] = total.astype(out.dtype)


def cache_out(latent_cache):
    ep_size = lax.axis_size("ep")
    slots, block_size, latent = latent_cache.shape
    share = slots // lax.axis_size("tp")
    mine = lax.dynamic_slice_in_dim(latent_cache, lax.axis_index("tp") * share, share, axis=0)
    return mine.reshape(share, ep_size, block_size * latent // ep_size).transpose(1, 0, 2)


def cache_turn(pieces, block_source, slots, before):
    ep_size = lax.axis_size("ep")
    tp_size = lax.axis_size("tp")
    tp_index = lax.axis_index("tp")
    share, piece = pieces.shape[1:]
    spread = lax.all_to_all(pieces, "ep", split_axis=0, concat_axis=0, tiled=True)
    spread = tie(spread, before)
    wanted = lax.dynamic_slice_in_dim(
        block_source.reshape(ep_size, tp_size, share), tp_index, 1, axis=1
    ).reshape(-1)
    place = (wanted // slots) * share + wanted % share
    holder = (wanted % slots) // share
    from_step = (tp_index + tp_size - holder) % tp_size
    index = jnp.where(
        from_step[:, None] == jnp.arange(tp_size, dtype=jnp.int32)[None, :], place[:, None], -1
    )
    rows = [part.reshape(-1, piece) for part in [spread] + swap_tp(spread)]
    shape = jax.ShapeDtypeStruct(rows[0].shape, rows[0].dtype)
    ordered = kernel_call(
        order_kernel,
        shape,
        [index] + rows,
        flops=2 * tp_size * rows[0].size * rows[0].shape[0],
        spare=6 << 20,
    )
    return ordered.reshape(ep_size, share, piece)


def cache_in(ordered, block_size, latent):
    share, piece = ordered.shape[1:]
    arrived = lax.all_to_all(ordered, "ep", split_axis=0, concat_axis=0, tiled=True)
    if piece != latent:
        arrived = arrived.transpose(1, 0, 2).reshape(share, block_size, latent).transpose(1, 0, 2)
    return arrived


def attention_kernel(chunk, owner, request, queries, *refs):
    keys, out = refs[:-1], refs[-1]
    for start in range(0, queries.shape[0], chunk):
        row = request[start : start + chunk]
        scores = []
        for step, key in enumerate(keys):
            part = lax.dot_general(
                queries[start : start + chunk],
                key[...],
                (((1,), (1,)), ((), ())),
                preferred_element_type=jnp.float32,
            )
            scores.append(
                jnp.where(row == owner[step : step + 1, :], part * score_scale, -jnp.inf)
            )
        row_max = scores[0].max(axis=1, keepdims=True)
        for part in scores[1:]:
            row_max = jnp.maximum(row_max, part.max(axis=1, keepdims=True))
        terms = [jnp.exp(part - row_max) for part in scores]
        total = 1.0 / sum(term.sum(axis=1, keepdims=True) for term in terms)
        attended = jnp.zeros((chunk, KV), jnp.float32)
        for term, key in zip(terms, keys):
            attended = attended + jnp.dot(
                (term * total).astype(jnp.bfloat16),
                key[:, :KV],
                preferred_element_type=jnp.float32,
            )
        out[start : start + chunk] = attended.astype(out.dtype)


def attend(queries, keys, block_request, block_used):
    tp_size = lax.axis_size("tp")
    row_count, heads, latent = queries.shape
    block_size, share = keys[0].shape[:2]
    within = jnp.arange(block_size, dtype=jnp.int32)[:, None]
    owners = []
    for step in range(tp_size):
        first = ((lax.axis_index("tp") + tp_size - step) % tp_size) * share
        owner = lax.dynamic_slice_in_dim(block_request, first, share)[None, :]
        limit = lax.dynamic_slice_in_dim(block_used, first, share)[None, :]
        owners.append(jnp.where(within < limit, owner, -1).reshape(1, -1))
    keys = [part.reshape(-1, latent) for part in keys]
    rows = queries.reshape(-1, latent)
    request = jnp.repeat(jnp.arange(row_count, dtype=jnp.int32), heads)[:, None]
    shape = jax.ShapeDtypeStruct((rows.shape[0], KV), jnp.bfloat16)
    result = kernel_call(
        functools.partial(attention_kernel, min(256, rows.shape[0])),
        shape,
        [jnp.concatenate(owners, axis=0), request, rows] + keys,
        flops=4 * rows.size * keys[0].shape[0] * tp_size,
        spare=8 << 20,
    )
    return result.reshape(row_count, heads, KV)


def body(
    tokens,
    expert_ids,
    gate_weights,
    expert_gate_up,
    expert_down,
    queries,
    latent_cache,
    block_source,
    block_request,
    block_used,
):
    row_count, top_count = expert_ids.shape
    slot_total, block_size, latent = latent_cache.shape
    ep_size = lax.axis_size("ep")
    tp_size = lax.axis_size("tp")
    tp_index = lax.axis_index("tp")
    bits = ep_bits()
    orders = (bits, bits[:-2] + [bits[-1], bits[-2]])
    parts = len(orders)
    cut = tokens.shape[1] // parts

    expert_range = jnp.arange(ep_size, dtype=jnp.int32)
    dense_gate = jnp.sum(
        jnp.where(
            expert_ids[:, :, None] == expert_range[None, None, :], gate_weights[:, :, None], 0.0
        ),
        axis=1,
    )
    gate_parts = jnp.concatenate(three_parts(dense_gate), axis=1)
    pad = -gate_parts.shape[1] % 128
    gates = jnp.pad(gate_parts, ((0, 0), (0, pad)))
    ends = tuple(cut * part for part in range(1, parts)) + (tokens.shape[1] + gates.shape[1],)
    halves = gather_rows(tokens, gates, orders, ends)
    last_sent = halves[-1][0]
    pieces = tie(cache_out(latent_cache), last_sent)
    places = [places_of(order) for order in orders]
    to_first = [[places[0].index(place) for place in own] for own in places]
    from_first = [[own.index(place) for place in places[0]] for own in places]

    passed = [tie(early, last_sent) for early, _ in halves[:-1]]
    passed.append(tie(last_sent, halves[0][1]))
    arrived = [
        [(pass_tp(early, step), pass_tp(late, step)) for early, (_, late) in zip(passed, halves)]
        for step in range(1, tp_size)
    ]
    all_rows = join_rows(
        [halves] + arrived, to_first, tuple(cut * part for part in range(1, parts + 1)), row_count
    )
    ordered = cache_turn(pieces, block_source, slot_total, all_rows)
    gate_halves = [half[..., cut : cut + 3 * ep_size] for half in halves[-1]]
    all_gate = jnp.concatenate(gate_halves, axis=0)
    all_gate = jnp.stack([all_gate[block] for block in from_first[-1]]).astype(jnp.float32)
    mine = (jnp.arange(3 * ep_size, dtype=jnp.int32) % ep_size) == lax.axis_index("ep")
    my_gate = jnp.sum(jnp.where(mine, all_gate, 0.0), axis=2).reshape(-1)
    gate_and_up = jnp.einsum(
        "sd,dgf->sgf", all_rows, expert_gate_up[0], preferred_element_type=jnp.float32
    )
    hidden = (
        jax.nn.silu(gate_and_up[:, 0]) * gate_and_up[:, 1] * my_gate[:, None]
    ).astype(jnp.bfloat16)

    hidden = tie(hidden, ordered)
    by_step = down(hidden, expert_down[0], from_first, row_count)
    sums = list(by_step[-1])
    for part in range(parts):
        others = [pass_tp(by_step[step - 1][part], step) for step in range(1, tp_size)]
        sums[part] = add_up([sums[part]] + others)

    held = {}

    def beside_first_sum(sent):
        held["keys"] = cache_in(tie(ordered, sent), block_size, latent)
        return sent

    def beside_third_sum(sent):
        sent, near = lax.optimization_barrier((sent, held["keys"]))
        held["attended"] = attend(queries, [near] + swap_tp(near), block_request, block_used)
        return sent

    def beside_last_sum(sent):
        sent, held["attended"] = lax.optimization_barrier((sent, held["attended"]))
        return sent

    hooks = {0: beside_first_sum, 2: beside_third_sum, len(bits) - 1: beside_last_sum}
    return (scatter_sums(sums, orders, hooks), held["attended"])


def solution(mesh):
    placed = (
        P("ep", "tp"),
        P("ep", None),
        P("ep", None),
        P("ep", None, None, "tp"),
        P("ep", None, "tp"),
        P("ep", "tp", None),
        P("ep", None, None),
        P(),
        P("ep"),
        P("ep"),
    )
    return jax.shard_map(
        body,
        mesh=mesh,
        in_specs=placed,
        out_specs=(P("ep", "tp"), P("ep", "tp", None)),
        check_vma=False,
    )
```

```python
import functools

import jax
import jax.numpy as jnp
from jax import lax
from jax.experimental import pallas as pl
from jax.experimental.pallas import tpu as pltpu
from jax.sharding import PartitionSpec as P

KV = 512


score_scale = 192.0 ** (-0.5)

WHOLE = pl.BlockSpec(memory_space=pltpu.VMEM)


def kernel_call(kernel, out_shape, arguments, flops, spare, in_specs=None, scratch_shapes=()):
    held = sum(array.size * array.dtype.itemsize for array in jax.tree.leaves(out_shape))
    for array, spec in zip(arguments, in_specs or [WHOLE] * len(arguments)):
        held += array.size * array.dtype.itemsize if spec is WHOLE else 0
    moved = sum(array.size * array.dtype.itemsize for array in arguments)
    return pl.pallas_call(
        kernel,
        out_shape=out_shape,
        in_specs=in_specs or [WHOLE] * len(arguments),
        out_specs=jax.tree.map(lambda _: WHOLE, out_shape),
        scratch_shapes=scratch_shapes,
        compiler_params=pltpu.CompilerParams(vmem_limit_bytes=held + spare),
        cost_estimate=pl.CostEstimate(
            flops=flops, bytes_accessed=moved + held, transcendentals=0
        ),
    )(*arguments)


def tie(values, others):
    return lax.optimization_barrier((values, others))[0]


def ep_bits():
    ep_size = lax.axis_size("ep")
    return [1 << place for place in reversed(range(ep_size.bit_length() - 1))]


def exchange(value, bit):
    ep_size = lax.axis_size("ep")
    return lax.ppermute(value, "ep", [(index, index ^ bit) for index in range(ep_size)])


def pass_tp(value, step):
    tp_size = lax.axis_size("tp")
    return lax.ppermute(
        value, "tp", [(index, (index + step) % tp_size) for index in range(tp_size)]
    )


def swap_tp(value):
    return [pass_tp(value, step) for step in range(1, lax.axis_size("tp"))]


def gather_rows(rows, others, orders, ends):
    shared = orders[0][:-2]
    values = [
        jnp.concatenate([value[None], exchange(value[None], shared[0])], axis=0)
        for value in (rows, others)
    ]
    value = jnp.concatenate(values, axis=2)
    for bit in shared[1:]:
        value = jnp.concatenate([value, exchange(value, bit)], axis=0)
    halves = []
    for order, start, end in zip(orders, (0,) + ends, ends):
        part = value[:, :, start:end]
        part = jnp.concatenate([part, exchange(part, order[-2])], axis=0)
        halves.append((part, exchange(part, order[-1])))
    return halves


def places_of(order):
    places = [0]
    for bit in order:
        places = places + [place ^ bit for place in places]
    return places


def join_kernel(spots, ends, count, tp_size, *refs):
    out = refs[-1]
    parts = len(spots)
    rows = out.shape[0] // len(spots[0])
    width = out.shape[1] // tp_size
    index = lax.axis_index("tp")

    def place(tp_index):
        for step in range(tp_size):
            owner = (tp_index - step) % tp_size
            for part in range(parts):
                start, end = ((0,) + ends)[part], ends[part]
                for half in range(2):
                    ref = refs[(step * parts + part) * 2 + half]
                    blocks = ref.shape[0] // rows
                    for block in range(blocks):
                        spot = spots[part][half * blocks + block] * rows
                        out[spot : spot + rows, owner * width + start : owner * width + end] = ref[
                            block * rows : (block + 1) * rows, : end - start
                        ]

    for tp_index in range(tp_size):
        pl.when(index == tp_index)(functools.partial(place, tp_index))


def join_rows(by_step, spots, ends, rows):
    tp_size = len(by_step)
    arrays = [
        half.reshape(-1, half.shape[-1]) for parts in by_step for pair in parts for half in pair
    ]
    shape = jax.ShapeDtypeStruct((len(spots[0]) * rows, ends[-1] * tp_size), jnp.bfloat16)
    return kernel_call(
        functools.partial(join_kernel, spots, ends, len(arrays), tp_size),
        shape,
        arrays,
        flops=0,
        spare=4 << 20,
    )


def scatter_sums(parts, orders, hooks):
    steps = len(orders[0])
    for step in range(steps):
        half = parts[0][0].shape[0] // 2
        sents = [add_up([term[half:] for term in terms]) for terms in parts]
        kepts = [add_up([term[:half] for term in terms]) for terms in parts]
        if step == 2:
            sents = [jnp.concatenate(sents, axis=1)]
            kepts = [jnp.concatenate(kepts, axis=1)]
        if step in hooks:
            sents[-1] = hooks[step](sents[-1])
        parts = [
            [kept, exchange(sent, order[steps - 1 - step])]
            for kept, sent, order in zip(kepts, sents, orders)
        ]
    return add_up(parts[0])


def add_up(terms):
    total = terms[0].astype(jnp.float32)
    for term in terms[1:]:
        total = total + term.astype(jnp.float32)
    return total.astype(jnp.bfloat16)


def three_parts(value):
    parts = []
    for _ in range(3):
        part = lax.reduce_precision(value, 8, 7)
        parts.append(part.astype(jnp.bfloat16))
        value = value - part
    return parts


def down_kernel(spots, tp_size, cut, width, rows, hidden, weight, *refs):
    parts = len(spots)
    outs, (held, turned, arrived) = refs[:-3], refs[-3:]
    copies = []
    for step in range(tp_size):
        target = lax.rem(lax.axis_index("tp") + step + 1, tp_size)
        for part in range(parts):
            run = step * parts + part
            start = pl.multiple_of((target * parts + part) * cut, cut)
            copies.append(
                pltpu.make_async_copy(
                    weight.at[pl.ds(start, cut)],
                    held.at[pl.ds(run * cut, cut)],
                    arrived.at[run],
                )
            )
    for copy in copies:
        copy.start()
    chunk = min(256, hidden.shape[0])
    for part in range(parts):
        for block, spot in enumerate(spots[part]):
            turned[part, spot * rows : (spot + 1) * rows] = hidden[
                block * rows : (block + 1) * rows
            ]
    for run, copy in enumerate(copies):
        copy.wait()
        for column in range(0, cut, width):
            for row in range(0, hidden.shape[0], chunk):
                outs[run][row : row + chunk, column : column + width] = lax.dot_general(
                    turned[run % parts, row : row + chunk],
                    held[run * cut + column : run * cut + column + width],
                    (((1,), (1,)), ((), ())),
                    preferred_element_type=jnp.float32,
                ).astype(jnp.bfloat16)


def down(hidden, weight, spots, rows):
    parts = len(spots)
    tp_size = lax.axis_size("tp")
    cut = weight.shape[0] // tp_size // parts
    width = 256 if cut % 256 == 0 else 128
    shape = jax.ShapeDtypeStruct((hidden.shape[0], cut), jnp.bfloat16)
    outs = kernel_call(
        functools.partial(down_kernel, spots, tp_size, cut, width, rows),
        [shape] * (parts * tp_size),
        [hidden, weight],
        flops=2 * hidden.size * weight.shape[0],
        spare=weight.size * 2 + (4 << 20),
        in_specs=[WHOLE, pl.BlockSpec(memory_space=pl.ANY)],
        scratch_shapes=[
            pltpu.VMEM(weight.shape, weight.dtype),
            pltpu.VMEM((parts,) + hidden.shape, hidden.dtype),
            pltpu.SemaphoreType.DMA((parts * tp_size,)),
        ],
    )
    return [outs[step * parts : (step + 1) * parts] for step in range(tp_size)]


def order_kernel(index, *refs):
    rows, out = refs[:-1], refs[-1]
    columns = lax.broadcasted_iota(jnp.int32, (out.shape[0], rows[0].shape[0]), 1)
    total = jnp.zeros(out.shape, jnp.float32)
    for step, ref in enumerate(rows):
        hot = (columns == index[:, step : step + 1]).astype(jnp.bfloat16)
        total = total + jnp.dot(hot, ref[...], preferred_element_type=jnp.float32)
    out[...] = total.astype(out.dtype)


def cache_out(latent_cache):
    ep_size = lax.axis_size("ep")
    slots, block_size, latent = latent_cache.shape
    share = slots // lax.axis_size("tp")
    mine = lax.dynamic_slice_in_dim(latent_cache, lax.axis_index("tp") * share, share, axis=0)
    return mine.reshape(share, ep_size, block_size * latent // ep_size).transpose(1, 0, 2)


def cache_turn(pieces, block_source, slots, before):
    ep_size = lax.axis_size("ep")
    tp_size = lax.axis_size("tp")
    tp_index = lax.axis_index("tp")
    share, piece = pieces.shape[1:]
    spread = lax.all_to_all(pieces, "ep", split_axis=0, concat_axis=0, tiled=True)
    spread = tie(spread, before)
    wanted = lax.dynamic_slice_in_dim(
        block_source.reshape(ep_size, tp_size, share), tp_index, 1, axis=1
    ).reshape(-1)
    place = (wanted // slots) * share + wanted % share
    holder = (wanted % slots) // share
    from_step = (tp_index + tp_size - holder) % tp_size
    index = jnp.where(
        from_step[:, None] == jnp.arange(tp_size, dtype=jnp.int32)[None, :], place[:, None], -1
    )
    rows = [part.reshape(-1, piece) for part in [spread] + swap_tp(spread)]
    shape = jax.ShapeDtypeStruct(rows[0].shape, rows[0].dtype)
    ordered = kernel_call(
        order_kernel,
        shape,
        [index] + rows,
        flops=2 * tp_size * rows[0].size * rows[0].shape[0],
        spare=6 << 20,
    )
    return ordered.reshape(ep_size, share, piece)


def cache_in(ordered, block_size, latent):
    share, piece = ordered.shape[1:]
    arrived = lax.all_to_all(ordered, "ep", split_axis=0, concat_axis=0, tiled=True)
    if piece != latent:
        arrived = arrived.transpose(1, 0, 2).reshape(share, block_size, latent).transpose(1, 0, 2)
    return arrived


def attention_kernel(chunk, owner, request, queries, *refs):
    keys, out = refs[:-1], refs[-1]
    for start in range(0, queries.shape[0], chunk):
        row = request[start : start + chunk]
        scores = []
        for step, key in enumerate(keys):
            part = lax.dot_general(
                queries[start : start + chunk],
                key[...],
                (((1,), (1,)), ((), ())),
                preferred_element_type=jnp.float32,
            )
            scores.append(
                jnp.where(row == owner[step : step + 1, :], part * score_scale, -jnp.inf)
            )
        row_max = scores[0].max(axis=1, keepdims=True)
        for part in scores[1:]:
            row_max = jnp.maximum(row_max, part.max(axis=1, keepdims=True))
        terms = [jnp.exp(part - row_max) for part in scores]
        total = 1.0 / sum(term.sum(axis=1, keepdims=True) for term in terms)
        attended = jnp.zeros((chunk, KV), jnp.float32)
        for term, key in zip(terms, keys):
            attended = attended + jnp.dot(
                (term * total).astype(jnp.bfloat16),
                key[:, :KV],
                preferred_element_type=jnp.float32,
            )
        out[start : start + chunk] = attended.astype(out.dtype)


def attend(queries, keys, block_request, block_used):
    tp_size = lax.axis_size("tp")
    row_count, heads, latent = queries.shape
    block_size, share = keys[0].shape[:2]
    within = jnp.arange(block_size, dtype=jnp.int32)[:, None]
    owners = []
    for step in range(tp_size):
        first = ((lax.axis_index("tp") + tp_size - step) % tp_size) * share
        owner = lax.dynamic_slice_in_dim(block_request, first, share)[None, :]
        limit = lax.dynamic_slice_in_dim(block_used, first, share)[None, :]
        owners.append(jnp.where(within < limit, owner, -1).reshape(1, -1))
    keys = [part.reshape(-1, latent) for part in keys]
    rows = queries.reshape(-1, latent)
    request = jnp.repeat(jnp.arange(row_count, dtype=jnp.int32), heads)[:, None]
    shape = jax.ShapeDtypeStruct((rows.shape[0], KV), jnp.bfloat16)
    result = kernel_call(
        functools.partial(attention_kernel, min(256, rows.shape[0])),
        shape,
        [jnp.concatenate(owners, axis=0), request, rows] + keys,
        flops=4 * rows.size * keys[0].shape[0] * tp_size,
        spare=8 << 20,
    )
    return result.reshape(row_count, heads, KV)


def body(
    tokens,
    expert_ids,
    gate_weights,
    expert_gate_up,
    expert_down,
    queries,
    latent_cache,
    block_source,
    block_request,
    block_used,
):
    row_count, top_count = expert_ids.shape
    slot_total, block_size, latent = latent_cache.shape
    ep_size = lax.axis_size("ep")
    tp_size = lax.axis_size("tp")
    tp_index = lax.axis_index("tp")
    bits = ep_bits()
    orders = (bits, bits[:-2] + [bits[-1], bits[-2]])
    parts = len(orders)
    cut = tokens.shape[1] // parts

    expert_range = jnp.arange(ep_size, dtype=jnp.int32)
    dense_gate = jnp.sum(
        jnp.where(
            expert_ids[:, :, None] == expert_range[None, None, :], gate_weights[:, :, None], 0.0
        ),
        axis=1,
    )
    gate_parts = jnp.concatenate(three_parts(dense_gate), axis=1)
    pad = -gate_parts.shape[1] % 128
    gates = jnp.pad(gate_parts, ((0, 0), (0, pad)))
    ends = tuple(cut * part for part in range(1, parts)) + (tokens.shape[1] + gates.shape[1],)
    halves = gather_rows(tokens, gates, orders, ends)
    last_sent = halves[-1][0]
    pieces = tie(cache_out(latent_cache), last_sent)
    places = [places_of(order) for order in orders]
    to_first = [[places[0].index(place) for place in own] for own in places]
    from_first = [[own.index(place) for place in places[0]] for own in places]

    passed = [tie(early, last_sent) for early, _ in halves[:-1]]
    passed.append(tie(last_sent, halves[0][1]))
    arrived = [
        [(pass_tp(early, step), pass_tp(late, step)) for early, (_, late) in zip(passed, halves)]
        for step in range(1, tp_size)
    ]
    all_rows = join_rows(
        [halves] + arrived, to_first, tuple(cut * part for part in range(1, parts + 1)), row_count
    )
    gate_halves = [half[..., cut : cut + 3 * ep_size] for half in halves[-1]]
    all_gate = jnp.concatenate(gate_halves, axis=0)
    all_gate = jnp.stack([all_gate[block] for block in from_first[-1]]).astype(jnp.float32)
    mine = (jnp.arange(3 * ep_size, dtype=jnp.int32) % ep_size) == lax.axis_index("ep")
    my_gate = jnp.sum(jnp.where(mine, all_gate, 0.0), axis=2).reshape(-1)
    gate_and_up = jnp.einsum(
        "sd,dgf->sgf", all_rows, expert_gate_up[0], preferred_element_type=jnp.float32
    )
    hidden = (
        jax.nn.silu(gate_and_up[:, 0]) * gate_and_up[:, 1] * my_gate[:, None]
    ).astype(jnp.bfloat16)

    ordered = cache_turn(pieces, block_source, slot_total, hidden)
    down_weight = pltpu.with_memory_space_constraint(expert_down[0], pltpu.HBM)
    by_step = down(hidden, down_weight, from_first, row_count)
    sums = [[own] for own in by_step[-1]]
    for part in range(parts):
        for step in range(1, tp_size):
            sums[part].append(pass_tp(by_step[step - 1][part], step))

    held = {}

    def beside_first_sum(sent):
        held["keys"] = cache_in(tie(ordered, sent), block_size, latent)
        return sent

    def beside_third_sum(sent):
        sent, near = lax.optimization_barrier((sent, held["keys"]))
        held["attended"] = attend(queries, [near] + swap_tp(near), block_request, block_used)
        return sent

    def beside_last_sum(sent):
        sent, held["attended"] = lax.optimization_barrier((sent, held["attended"]))
        return sent

    hooks = {0: beside_first_sum, 2: beside_third_sum, len(bits) - 1: beside_last_sum}
    return (scatter_sums(sums, orders, hooks), held["attended"])


def solution(mesh):
    placed = (
        P("ep", "tp"),
        P("ep", None),
        P("ep", None),
        P("ep", None, None, "tp"),
        P("ep", None, "tp"),
        P("ep", "tp", None),
        P("ep", None, None),
        P(),
        P("ep"),
        P("ep"),
    )
    return jax.shard_map(
        body,
        mesh=mesh,
        in_specs=placed,
        out_specs=(P("ep", "tp"), P("ep", "tp", None)),
        check_vma=False,
    )
```

```python
import functools

import jax
import jax.numpy as jnp
from jax import lax
from jax.experimental import pallas as pl
from jax.experimental.pallas import tpu as pltpu
from jax.sharding import PartitionSpec as P

KV = 512


score_scale = 192.0 ** (-0.5)

WHOLE = pl.BlockSpec(memory_space=pltpu.VMEM)


def kernel_call(kernel, out_shape, arguments, flops, spare, in_specs=None, scratch_shapes=()):
    held = sum(array.size * array.dtype.itemsize for array in jax.tree.leaves(out_shape))
    for array, spec in zip(arguments, in_specs or [WHOLE] * len(arguments)):
        held += array.size * array.dtype.itemsize if spec is WHOLE else 0
    moved = sum(array.size * array.dtype.itemsize for array in arguments)
    return pl.pallas_call(
        kernel,
        out_shape=out_shape,
        in_specs=in_specs or [WHOLE] * len(arguments),
        out_specs=jax.tree.map(lambda _: WHOLE, out_shape),
        scratch_shapes=scratch_shapes,
        compiler_params=pltpu.CompilerParams(vmem_limit_bytes=held + spare),
        cost_estimate=pl.CostEstimate(
            flops=flops, bytes_accessed=moved + held, transcendentals=0
        ),
    )(*arguments)


def tie(values, others):
    return lax.optimization_barrier((values, others))[0]


def ep_bits():
    ep_size = lax.axis_size("ep")
    return [1 << place for place in reversed(range(ep_size.bit_length() - 1))]


def exchange(value, bit):
    ep_size = lax.axis_size("ep")
    return lax.ppermute(value, "ep", [(index, index ^ bit) for index in range(ep_size)])


def pass_tp(value, step):
    tp_size = lax.axis_size("tp")
    return lax.ppermute(
        value, "tp", [(index, (index + step) % tp_size) for index in range(tp_size)]
    )


def swap_tp(value):
    return [pass_tp(value, step) for step in range(1, lax.axis_size("tp"))]


def gather_rows(rows, others, orders, ends, beside, ahead):
    shared = orders[0][:-2]
    values = [
        jnp.concatenate([value[None], exchange(value[None], shared[0])], axis=0)
        for value in (rows, others)
    ]
    value = jnp.concatenate(values, axis=2)
    for bit in shared[1:]:
        if bit == shared[-1]:
            beside(value)
        value = jnp.concatenate([value, exchange(value, bit)], axis=0)
    halves = []
    for order, start, end in zip(orders, (0,) + ends, ends):
        part = value[:, :, start:end]
        part = jnp.concatenate([part, exchange(part, order[-2])], axis=0)
        if end == ends[-1]:
            part = ahead(part)
        halves.append((part, exchange(part, order[-1])))
    return halves


def places_of(order):
    places = [0]
    for bit in order:
        places = places + [place ^ bit for place in places]
    return places


def join_kernel(spots, ends, count, tp_size, *refs):
    out = refs[-1]
    parts = len(spots)
    rows = out.shape[0] // len(spots[0])
    width = out.shape[1] // tp_size
    index = lax.axis_index("tp")

    def place(tp_index):
        for step in range(tp_size):
            owner = (tp_index - step) % tp_size
            for part in range(parts):
                start, end = ((0,) + ends)[part], ends[part]
                for half in range(2):
                    ref = refs[(step * parts + part) * 2 + half]
                    blocks = ref.shape[0] // rows
                    for block in range(blocks):
                        spot = spots[part][half * blocks + block] * rows
                        out[spot : spot + rows, owner * width + start : owner * width + end] = ref[
                            block * rows : (block + 1) * rows, : end - start
                        ]

    for tp_index in range(tp_size):
        pl.when(index == tp_index)(functools.partial(place, tp_index))


def join_rows(by_step, spots, ends, rows):
    tp_size = len(by_step)
    arrays = [
        half.reshape(-1, half.shape[-1]) for parts in by_step for pair in parts for half in pair
    ]
    shape = jax.ShapeDtypeStruct((len(spots[0]) * rows, ends[-1] * tp_size), jnp.bfloat16)
    return kernel_call(
        functools.partial(join_kernel, spots, ends, len(arrays), tp_size),
        shape,
        arrays,
        flops=0,
        spare=4 << 20,
    )


def scatter_sums(parts, orders, hooks):
    steps = len(orders[0])
    for step in range(steps):
        half = parts[0][0].shape[0] // 2
        sents = [add_up([term[half:] for term in terms]) for terms in parts]
        kepts = [add_up([term[:half] for term in terms]) for terms in parts]
        if step == 2:
            sents = [jnp.concatenate(sents, axis=1)]
            kepts = [jnp.concatenate(kepts, axis=1)]
        if step in hooks:
            sents[-1] = hooks[step](sents[-1])
        parts = [
            [kept, exchange(sent, order[steps - 1 - step])]
            for kept, sent, order in zip(kepts, sents, orders)
        ]
    return add_up(parts[0])


def add_up(terms):
    total = terms[0].astype(jnp.float32)
    for term in terms[1:]:
        total = total + term.astype(jnp.float32)
    return total.astype(jnp.bfloat16)


def three_parts(value):
    parts = []
    for _ in range(3):
        part = lax.reduce_precision(value, 8, 7)
        parts.append(part.astype(jnp.bfloat16))
        value = value - part
    return parts


def down_kernel(spots, tp_size, cut, width, rows, hidden, weight, *refs):
    parts = len(spots)
    outs, (held, turned, arrived) = refs[:-3], refs[-3:]
    copies = []
    for step in range(tp_size):
        target = lax.rem(lax.axis_index("tp") + step + 1, tp_size)
        for part in range(parts):
            run = step * parts + part
            start = pl.multiple_of((target * parts + part) * cut, cut)
            copies.append(
                pltpu.make_async_copy(
                    weight.at[pl.ds(start, cut)],
                    held.at[pl.ds(run * cut, cut)],
                    arrived.at[run],
                )
            )
    for copy in copies:
        copy.start()
    chunk = min(256, hidden.shape[0])
    for part in range(parts):
        for block, spot in enumerate(spots[part]):
            turned[part, spot * rows : (spot + 1) * rows] = hidden[
                block * rows : (block + 1) * rows
            ]
    for run, copy in enumerate(copies):
        copy.wait()
        for column in range(0, cut, width):
            for row in range(0, hidden.shape[0], chunk):
                outs[run][row : row + chunk, column : column + width] = lax.dot_general(
                    turned[run % parts, row : row + chunk],
                    held[run * cut + column : run * cut + column + width],
                    (((1,), (1,)), ((), ())),
                    preferred_element_type=jnp.float32,
                ).astype(jnp.bfloat16)


def down(hidden, weight, spots, rows):
    parts = len(spots)
    tp_size = lax.axis_size("tp")
    cut = weight.shape[0] // tp_size // parts
    width = 256 if cut % 256 == 0 else 128
    shape = jax.ShapeDtypeStruct((hidden.shape[0], cut), jnp.bfloat16)
    outs = kernel_call(
        functools.partial(down_kernel, spots, tp_size, cut, width, rows),
        [shape] * (parts * tp_size),
        [hidden, weight],
        flops=2 * hidden.size * weight.shape[0],
        spare=weight.size * 2 + (4 << 20),
        in_specs=[WHOLE, pl.BlockSpec(memory_space=pl.ANY)],
        scratch_shapes=[
            pltpu.VMEM(weight.shape, weight.dtype),
            pltpu.VMEM((parts,) + hidden.shape, hidden.dtype),
            pltpu.SemaphoreType.DMA((parts * tp_size,)),
        ],
    )
    return [outs[step * parts : (step + 1) * parts] for step in range(tp_size)]


def order_kernel(index, *refs):
    rows, out = refs[:-1], refs[-1]
    columns = lax.broadcasted_iota(jnp.int32, (out.shape[0], rows[0].shape[0]), 1)
    total = jnp.zeros(out.shape, jnp.float32)
    for step, ref in enumerate(rows):
        hot = (columns == index[:, step : step + 1]).astype(jnp.bfloat16)
        total = total + jnp.dot(hot, ref[...], preferred_element_type=jnp.float32)
    out[...] = total.astype(out.dtype)


def cache_out(latent_cache):
    ep_size = lax.axis_size("ep")
    slots, block_size, latent = latent_cache.shape
    share = slots // lax.axis_size("tp")
    mine = lax.dynamic_slice_in_dim(latent_cache, lax.axis_index("tp") * share, share, axis=0)
    return mine.reshape(share, ep_size, block_size * latent // ep_size).transpose(1, 0, 2)


def cache_turn(spread, block_source, slots):
    ep_size = lax.axis_size("ep")
    tp_size = lax.axis_size("tp")
    tp_index = lax.axis_index("tp")
    share, piece = spread.shape[1:]
    wanted = lax.dynamic_slice_in_dim(
        block_source.reshape(ep_size, tp_size, share), tp_index, 1, axis=1
    ).reshape(-1)
    place = (wanted // slots) * share + wanted % share
    holder = (wanted % slots) // share
    from_step = (tp_index + tp_size - holder) % tp_size
    index = jnp.where(
        from_step[:, None] == jnp.arange(tp_size, dtype=jnp.int32)[None, :], place[:, None], -1
    )
    rows = [part.reshape(-1, piece) for part in [spread] + swap_tp(spread)]
    shape = jax.ShapeDtypeStruct(rows[0].shape, rows[0].dtype)
    ordered = kernel_call(
        order_kernel,
        shape,
        [index] + rows,
        flops=2 * tp_size * rows[0].size * rows[0].shape[0],
        spare=6 << 20,
    )
    return ordered.reshape(ep_size, share, piece)


def cache_in(ordered, block_size, latent):
    share, piece = ordered.shape[1:]
    arrived = lax.all_to_all(ordered, "ep", split_axis=0, concat_axis=0, tiled=True)
    if piece != latent:
        arrived = arrived.transpose(1, 0, 2).reshape(share, block_size, latent).transpose(1, 0, 2)
    return arrived


def attention_kernel(chunk, owner, request, queries, *refs):
    keys, out = refs[:-1], refs[-1]
    for start in range(0, queries.shape[0], chunk):
        row = request[start : start + chunk]
        scores = []
        for step, key in enumerate(keys):
            part = lax.dot_general(
                queries[start : start + chunk],
                key[...],
                (((1,), (1,)), ((), ())),
                preferred_element_type=jnp.float32,
            )
            scores.append(
                jnp.where(row == owner[step : step + 1, :], part * score_scale, -jnp.inf)
            )
        row_max = scores[0].max(axis=1, keepdims=True)
        for part in scores[1:]:
            row_max = jnp.maximum(row_max, part.max(axis=1, keepdims=True))
        terms = [jnp.exp(part - row_max) for part in scores]
        total = 1.0 / sum(term.sum(axis=1, keepdims=True) for term in terms)
        attended = jnp.zeros((chunk, KV), jnp.float32)
        for term, key in zip(terms, keys):
            attended = attended + jnp.dot(
                (term * total).astype(jnp.bfloat16),
                key[:, :KV],
                preferred_element_type=jnp.float32,
            )
        out[start : start + chunk] = attended.astype(out.dtype)


def attend(queries, keys, block_request, block_used):
    tp_size = lax.axis_size("tp")
    row_count, heads, latent = queries.shape
    block_size, share = keys[0].shape[:2]
    within = jnp.arange(block_size, dtype=jnp.int32)[:, None]
    owners = []
    for step in range(tp_size):
        first = ((lax.axis_index("tp") + tp_size - step) % tp_size) * share
        owner = lax.dynamic_slice_in_dim(block_request, first, share)[None, :]
        limit = lax.dynamic_slice_in_dim(block_used, first, share)[None, :]
        owners.append(jnp.where(within < limit, owner, -1).reshape(1, -1))
    keys = [part.reshape(-1, latent) for part in keys]
    rows = queries.reshape(-1, latent)
    request = jnp.repeat(jnp.arange(row_count, dtype=jnp.int32), heads)[:, None]
    shape = jax.ShapeDtypeStruct((rows.shape[0], KV), jnp.bfloat16)
    result = kernel_call(
        functools.partial(attention_kernel, min(256, rows.shape[0])),
        shape,
        [jnp.concatenate(owners, axis=0), request, rows] + keys,
        flops=4 * rows.size * keys[0].shape[0] * tp_size,
        spare=8 << 20,
    )
    return result.reshape(row_count, heads, KV)


def body(
    tokens,
    expert_ids,
    gate_weights,
    expert_gate_up,
    expert_down,
    queries,
    latent_cache,
    block_source,
    block_request,
    block_used,
):
    row_count, top_count = expert_ids.shape
    slot_total, block_size, latent = latent_cache.shape
    ep_size = lax.axis_size("ep")
    tp_size = lax.axis_size("tp")
    tp_index = lax.axis_index("tp")
    bits = ep_bits()
    orders = (bits, bits[:-2] + [bits[-1], bits[-2]])
    parts = len(orders)
    cut = tokens.shape[1] // parts

    expert_range = jnp.arange(ep_size, dtype=jnp.int32)
    dense_gate = jnp.sum(
        jnp.where(
            expert_ids[:, :, None] == expert_range[None, None, :], gate_weights[:, :, None], 0.0
        ),
        axis=1,
    )
    gate_parts = jnp.concatenate(three_parts(dense_gate), axis=1)
    pad = -gate_parts.shape[1] % 128
    gates = jnp.pad(gate_parts, ((0, 0), (0, pad)))
    ends = tuple(cut * part for part in range(1, parts)) + (tokens.shape[1] + gates.shape[1],)
    held = {}

    def beside_shared(sent):
        pieces = tie(cache_out(latent_cache), sent)
        held["spread"] = lax.all_to_all(pieces, "ep", split_axis=0, concat_axis=0, tiled=True)

    def ahead_of_last(sent):
        sent, held["spread"] = lax.optimization_barrier((sent, held["spread"]))
        return sent

    halves = gather_rows(tokens, gates, orders, ends, beside_shared, ahead_of_last)
    last_sent, last_late = halves[-1]
    ordered = cache_turn(held["spread"], block_source, slot_total)
    last_late, ordered = lax.optimization_barrier((last_late, ordered))
    halves[-1] = (last_sent, last_late)
    places = [places_of(order) for order in orders]
    to_first = [[places[0].index(place) for place in own] for own in places]
    from_first = [[own.index(place) for place in places[0]] for own in places]

    passed = [tie(early, last_sent) for early, _ in halves[:-1]]
    passed.append(tie(last_sent, halves[0][1]))
    arrived = [
        [(pass_tp(early, step), pass_tp(late, step)) for early, (_, late) in zip(passed, halves)]
        for step in range(1, tp_size)
    ]
    all_rows = join_rows(
        [halves] + arrived, to_first, tuple(cut * part for part in range(1, parts + 1)), row_count
    )
    gate_halves = [half[..., cut : cut + 3 * ep_size] for half in halves[-1]]
    all_gate = jnp.concatenate(gate_halves, axis=0)
    all_gate = jnp.stack([all_gate[block] for block in from_first[-1]]).astype(jnp.float32)
    mine = (jnp.arange(3 * ep_size, dtype=jnp.int32) % ep_size) == lax.axis_index("ep")
    my_gate = jnp.sum(jnp.where(mine, all_gate, 0.0), axis=2).reshape(-1)
    gate_and_up = jnp.einsum(
        "sd,dgf->sgf", all_rows, expert_gate_up[0], preferred_element_type=jnp.float32
    )
    hidden = (
        jax.nn.silu(gate_and_up[:, 0]) * gate_and_up[:, 1] * my_gate[:, None]
    ).astype(jnp.bfloat16)

    down_weight = pltpu.with_memory_space_constraint(expert_down[0], pltpu.HBM)
    by_step = down(hidden, down_weight, from_first, row_count)
    sums = [[own] for own in by_step[-1]]
    for part in range(parts):
        for step in range(1, tp_size):
            sums[part].append(pass_tp(by_step[step - 1][part], step))

    def beside_first_sum(sent):
        held["keys"] = cache_in(tie(ordered, sent), block_size, latent)
        return sent

    def beside_third_sum(sent):
        near = tie(held["keys"], sent)
        held["keys"] = [near] + swap_tp(near)
        return sent

    def beside_last_sum(sent):
        keys = tie(held["keys"], sent)
        held["attended"] = attend(queries, keys, block_request, block_used)
        return sent

    hooks = {0: beside_first_sum, 2: beside_third_sum, len(bits) - 1: beside_last_sum}
    return (scatter_sums(sums, orders, hooks), held["attended"])


def solution(mesh):
    placed = (
        P("ep", "tp"),
        P("ep", None),
        P("ep", None),
        P("ep", None, None, "tp"),
        P("ep", None, "tp"),
        P("ep", "tp", None),
        P("ep", None, None),
        P(),
        P("ep"),
        P("ep"),
    )
    return jax.shard_map(
        body,
        mesh=mesh,
        in_specs=placed,
        out_specs=(P("ep", "tp"), P("ep", "tp", None)),
        check_vma=False,
    )
```

```python
import functools

import jax
import jax.numpy as jnp
from jax import lax
from jax.experimental import pallas as pl
from jax.experimental.pallas import tpu as pltpu
from jax.sharding import PartitionSpec as P

KV = 512


score_scale = 192.0 ** (-0.5)

WHOLE = pl.BlockSpec(memory_space=pltpu.VMEM)


def kernel_call(kernel, out_shape, arguments, flops, spare, in_specs=None, scratch_shapes=()):
    held = sum(array.size * array.dtype.itemsize for array in jax.tree.leaves(out_shape))
    for array, spec in zip(arguments, in_specs or [WHOLE] * len(arguments)):
        held += array.size * array.dtype.itemsize if spec is WHOLE else 0
    moved = sum(array.size * array.dtype.itemsize for array in arguments)
    return pl.pallas_call(
        kernel,
        out_shape=out_shape,
        in_specs=in_specs or [WHOLE] * len(arguments),
        out_specs=jax.tree.map(lambda _: WHOLE, out_shape),
        scratch_shapes=scratch_shapes,
        compiler_params=pltpu.CompilerParams(vmem_limit_bytes=held + spare),
        cost_estimate=pl.CostEstimate(
            flops=flops, bytes_accessed=moved + held, transcendentals=0
        ),
    )(*arguments)


def tie(values, others):
    return lax.optimization_barrier((values, others))[0]


def ep_bits():
    ep_size = lax.axis_size("ep")
    return [1 << place for place in reversed(range(ep_size.bit_length() - 1))]


def exchange(value, bit):
    ep_size = lax.axis_size("ep")
    return lax.ppermute(value, "ep", [(index, index ^ bit) for index in range(ep_size)])


def pass_tp(value, step):
    tp_size = lax.axis_size("tp")
    return lax.ppermute(
        value, "tp", [(index, (index + step) % tp_size) for index in range(tp_size)]
    )


def swap_tp(value):
    return [pass_tp(value, step) for step in range(1, lax.axis_size("tp"))]


def gather_rows(rows, others, orders, ends, beside, ahead):
    shared = orders[0][:-2]
    values = [
        jnp.concatenate([value[None], exchange(value[None], shared[0])], axis=0)
        for value in (rows, others)
    ]
    value = jnp.concatenate(values, axis=2)
    for bit in shared[1:]:
        if bit == shared[-1]:
            beside(value)
        value = jnp.concatenate([value, exchange(value, bit)], axis=0)
    halves = []
    for order, start, end in zip(orders, (0,) + ends, ends):
        part = value[:, :, start:end]
        part = jnp.concatenate([part, exchange(part, order[-2])], axis=0)
        if end == ends[-1]:
            part = ahead(part)
        halves.append((part, exchange(part, order[-1])))
    return halves


def places_of(order):
    places = [0]
    for bit in order:
        places = places + [place ^ bit for place in places]
    return places


def join_kernel(spots, ends, count, tp_size, *refs):
    out = refs[-1]
    parts = len(spots)
    rows = out.shape[0] // len(spots[0])
    width = out.shape[1] // tp_size
    index = lax.axis_index("tp")

    def place(tp_index):
        for step in range(tp_size):
            owner = (tp_index - step) % tp_size
            for part in range(parts):
                start, end = ((0,) + ends)[part], ends[part]
                for half in range(2):
                    ref = refs[(step * parts + part) * 2 + half]
                    blocks = ref.shape[0] // rows
                    for block in range(blocks):
                        spot = spots[part][half * blocks + block] * rows
                        out[spot : spot + rows, owner * width + start : owner * width + end] = ref[
                            block * rows : (block + 1) * rows, : end - start
                        ]

    for tp_index in range(tp_size):
        pl.when(index == tp_index)(functools.partial(place, tp_index))


def join_rows(by_step, spots, ends, rows):
    tp_size = len(by_step)
    arrays = [
        half.reshape(-1, half.shape[-1]) for parts in by_step for pair in parts for half in pair
    ]
    shape = jax.ShapeDtypeStruct((len(spots[0]) * rows, ends[-1] * tp_size), jnp.bfloat16)
    return kernel_call(
        functools.partial(join_kernel, spots, ends, len(arrays), tp_size),
        shape,
        arrays,
        flops=0,
        spare=4 << 20,
    )


def scatter_sums(parts, orders, hooks):
    steps = len(orders[0])
    for step in range(steps):
        half = parts[0][0].shape[0] // 2
        sents = [add_up([term[half:] for term in terms]) for terms in parts]
        kepts = [add_up([term[:half] for term in terms]) for terms in parts]
        if step == 2:
            sents = [jnp.concatenate(sents, axis=1)]
            kepts = [jnp.concatenate(kepts, axis=1)]
        if step in hooks:
            sents[-1] = hooks[step](sents[-1])
        parts = [
            [kept, exchange(sent, order[steps - 1 - step])]
            for kept, sent, order in zip(kepts, sents, orders)
        ]
    return add_up(parts[0])


def add_up(terms):
    total = terms[0].astype(jnp.float32)
    for term in terms[1:]:
        total = total + term.astype(jnp.float32)
    return total.astype(jnp.bfloat16)


def three_parts(value):
    parts = []
    for _ in range(3):
        part = lax.reduce_precision(value, 8, 7)
        parts.append(part.astype(jnp.bfloat16))
        value = value - part
    return parts


def down_kernel(spots, tp_size, cut, width, rows, hidden, weight, *refs):
    parts = len(spots)
    outs, (held, turned, arrived) = refs[:-3], refs[-3:]
    copies = []
    for step in range(tp_size):
        target = lax.rem(lax.axis_index("tp") + step + 1, tp_size)
        for part in range(parts):
            run = step * parts + part
            start = pl.multiple_of((target * parts + part) * cut, cut)
            copies.append(
                pltpu.make_async_copy(
                    weight.at[pl.ds(start, cut)],
                    held.at[pl.ds(run * cut, cut)],
                    arrived.at[run],
                )
            )
    for copy in copies:
        copy.start()
    chunk = min(256, hidden.shape[0])
    for part in range(parts):
        for block, spot in enumerate(spots[part]):
            turned[part, spot * rows : (spot + 1) * rows] = hidden[
                block * rows : (block + 1) * rows
            ]
    for run, copy in enumerate(copies):
        copy.wait()
        for column in range(0, cut, width):
            for row in range(0, hidden.shape[0], chunk):
                outs[run][row : row + chunk, column : column + width] = lax.dot_general(
                    turned[run % parts, row : row + chunk],
                    held[run * cut + column : run * cut + column + width],
                    (((1,), (1,)), ((), ())),
                    preferred_element_type=jnp.float32,
                ).astype(jnp.bfloat16)


def down(hidden, weight, spots, rows):
    parts = len(spots)
    tp_size = lax.axis_size("tp")
    cut = weight.shape[0] // tp_size // parts
    width = cut
    shape = jax.ShapeDtypeStruct((hidden.shape[0], cut), jnp.bfloat16)
    outs = kernel_call(
        functools.partial(down_kernel, spots, tp_size, cut, width, rows),
        [shape] * (parts * tp_size),
        [hidden, weight],
        flops=2 * hidden.size * weight.shape[0],
        spare=weight.size * 2 + (8 << 20),
        in_specs=[WHOLE, pl.BlockSpec(memory_space=pl.ANY)],
        scratch_shapes=[
            pltpu.VMEM(weight.shape, weight.dtype),
            pltpu.VMEM((parts,) + hidden.shape, hidden.dtype),
            pltpu.SemaphoreType.DMA((parts * tp_size,)),
        ],
    )
    return [outs[step * parts : (step + 1) * parts] for step in range(tp_size)]


def order_kernel(index, *refs):
    rows, out = refs[:-1], refs[-1]
    columns = lax.broadcasted_iota(jnp.int32, (out.shape[0], rows[0].shape[0]), 1)
    total = jnp.zeros(out.shape, jnp.float32)
    for step, ref in enumerate(rows):
        hot = (columns == index[:, step : step + 1]).astype(jnp.bfloat16)
        total = total + jnp.dot(hot, ref[...], preferred_element_type=jnp.float32)
    out[...] = total.astype(out.dtype)


def cache_out(latent_cache):
    ep_size = lax.axis_size("ep")
    slots, block_size, latent = latent_cache.shape
    share = slots // lax.axis_size("tp")
    mine = lax.dynamic_slice_in_dim(latent_cache, lax.axis_index("tp") * share, share, axis=0)
    return mine.reshape(share, ep_size, block_size * latent // ep_size).transpose(1, 0, 2)


def cache_turn(spread, block_source, slots):
    ep_size = lax.axis_size("ep")
    tp_size = lax.axis_size("tp")
    tp_index = lax.axis_index("tp")
    share, piece = spread.shape[1:]
    wanted = lax.dynamic_slice_in_dim(
        block_source.reshape(ep_size, tp_size, share), tp_index, 1, axis=1
    ).reshape(-1)
    place = (wanted // slots) * share + wanted % share
    holder = (wanted % slots) // share
    from_step = (tp_index + tp_size - holder) % tp_size
    index = jnp.where(
        from_step[:, None] == jnp.arange(tp_size, dtype=jnp.int32)[None, :], place[:, None], -1
    )
    rows = [part.reshape(-1, piece) for part in [spread] + swap_tp(spread)]
    shape = jax.ShapeDtypeStruct(rows[0].shape, rows[0].dtype)
    ordered = kernel_call(
        order_kernel,
        shape,
        [index] + rows,
        flops=2 * tp_size * rows[0].size * rows[0].shape[0],
        spare=6 << 20,
    )
    return ordered.reshape(ep_size, share, piece)


def cache_in(ordered, block_size, latent):
    share, piece = ordered.shape[1:]
    arrived = lax.all_to_all(ordered, "ep", split_axis=0, concat_axis=0, tiled=True)
    if piece != latent:
        arrived = arrived.transpose(1, 0, 2).reshape(share, block_size, latent).transpose(1, 0, 2)
    return arrived


def attention_kernel(chunk, owner, request, queries, *refs):
    keys, out = refs[:-1], refs[-1]
    for start in range(0, queries.shape[0], chunk):
        row = request[start : start + chunk]
        scores = []
        for step, key in enumerate(keys):
            part = lax.dot_general(
                queries[start : start + chunk],
                key[...],
                (((1,), (1,)), ((), ())),
                preferred_element_type=jnp.float32,
            )
            scores.append(
                jnp.where(row == owner[step : step + 1, :], part * score_scale, -jnp.inf)
            )
        row_max = scores[0].max(axis=1, keepdims=True)
        for part in scores[1:]:
            row_max = jnp.maximum(row_max, part.max(axis=1, keepdims=True))
        terms = [jnp.exp(part - row_max) for part in scores]
        total = 1.0 / sum(term.sum(axis=1, keepdims=True) for term in terms)
        attended = jnp.zeros((chunk, KV), jnp.float32)
        for term, key in zip(terms, keys):
            attended = attended + jnp.dot(
                (term * total).astype(jnp.bfloat16),
                key[:, :KV],
                preferred_element_type=jnp.float32,
            )
        out[start : start + chunk] = attended.astype(out.dtype)


def attend(queries, keys, block_request, block_used):
    tp_size = lax.axis_size("tp")
    row_count, heads, latent = queries.shape
    block_size, share = keys[0].shape[:2]
    within = jnp.arange(block_size, dtype=jnp.int32)[:, None]
    owners = []
    for step in range(tp_size):
        first = ((lax.axis_index("tp") + tp_size - step) % tp_size) * share
        owner = lax.dynamic_slice_in_dim(block_request, first, share)[None, :]
        limit = lax.dynamic_slice_in_dim(block_used, first, share)[None, :]
        owners.append(jnp.where(within < limit, owner, -1).reshape(1, -1))
    keys = [part.reshape(-1, latent) for part in keys]
    rows = queries.reshape(-1, latent)
    request = jnp.repeat(jnp.arange(row_count, dtype=jnp.int32), heads)[:, None]
    shape = jax.ShapeDtypeStruct((rows.shape[0], KV), jnp.bfloat16)
    result = kernel_call(
        functools.partial(attention_kernel, min(256, rows.shape[0])),
        shape,
        [jnp.concatenate(owners, axis=0), request, rows] + keys,
        flops=4 * rows.size * keys[0].shape[0] * tp_size,
        spare=8 << 20,
    )
    return result.reshape(row_count, heads, KV)


def body(
    tokens,
    expert_ids,
    gate_weights,
    expert_gate_up,
    expert_down,
    queries,
    latent_cache,
    block_source,
    block_request,
    block_used,
):
    row_count, top_count = expert_ids.shape
    slot_total, block_size, latent = latent_cache.shape
    ep_size = lax.axis_size("ep")
    tp_size = lax.axis_size("tp")
    tp_index = lax.axis_index("tp")
    bits = ep_bits()
    orders = (bits, bits[:-2] + [bits[-1], bits[-2]])
    parts = len(orders)
    cut = tokens.shape[1] // parts

    expert_range = jnp.arange(ep_size, dtype=jnp.int32)
    dense_gate = jnp.sum(
        jnp.where(
            expert_ids[:, :, None] == expert_range[None, None, :], gate_weights[:, :, None], 0.0
        ),
        axis=1,
    )
    gate_parts = jnp.concatenate(three_parts(dense_gate), axis=1)
    pad = -gate_parts.shape[1] % 128
    gates = jnp.pad(gate_parts, ((0, 0), (0, pad)))
    ends = tuple(cut * part for part in range(1, parts)) + (tokens.shape[1] + gates.shape[1],)
    held = {}

    def beside_shared(sent):
        pieces = tie(cache_out(latent_cache), sent)
        held["spread"] = lax.all_to_all(pieces, "ep", split_axis=0, concat_axis=0, tiled=True)

    def ahead_of_last(sent):
        sent, held["spread"] = lax.optimization_barrier((sent, held["spread"]))
        return sent

    halves = gather_rows(tokens, gates, orders, ends, beside_shared, ahead_of_last)
    last_sent = halves[-1][0]
    ordered = cache_turn(held["spread"], block_source, slot_total)
    first_late, ordered = lax.optimization_barrier((halves[0][1], ordered))
    halves[0] = (halves[0][0], first_late)
    places = [places_of(order) for order in orders]
    to_first = [[places[0].index(place) for place in own] for own in places]
    from_first = [[own.index(place) for place in places[0]] for own in places]

    passed = [tie(early, last_sent) for early, _ in halves[:-1]]
    passed.append(tie(last_sent, halves[0][1]))
    arrived = [
        [(pass_tp(early, step), pass_tp(late, step)) for early, (_, late) in zip(passed, halves)]
        for step in range(1, tp_size)
    ]
    all_rows = join_rows(
        [halves] + arrived, to_first, tuple(cut * part for part in range(1, parts + 1)), row_count
    )
    gate_halves = [half[..., cut : cut + 3 * ep_size] for half in halves[-1]]
    all_gate = jnp.concatenate(gate_halves, axis=0)
    all_gate = jnp.stack([all_gate[block] for block in from_first[-1]]).astype(jnp.float32)
    mine = (jnp.arange(3 * ep_size, dtype=jnp.int32) % ep_size) == lax.axis_index("ep")
    my_gate = jnp.sum(jnp.where(mine, all_gate, 0.0), axis=2).reshape(-1)
    gate_and_up = jnp.einsum(
        "sd,dgf->sgf", all_rows, expert_gate_up[0], preferred_element_type=jnp.float32
    )
    hidden = (
        jax.nn.silu(gate_and_up[:, 0]) * gate_and_up[:, 1] * my_gate[:, None]
    ).astype(jnp.bfloat16)

    down_weight = pltpu.with_memory_space_constraint(expert_down[0], pltpu.HBM)
    by_step = down(hidden, down_weight, from_first, row_count)
    sums = [[own] for own in by_step[-1]]
    for part in range(parts):
        for step in range(1, tp_size):
            sums[part].append(pass_tp(by_step[step - 1][part], step))

    def beside_first_sum(sent):
        held["keys"] = cache_in(tie(ordered, sent), block_size, latent)
        return sent

    def beside_third_sum(sent):
        sent, near = lax.optimization_barrier((sent, held["keys"]))
        held["keys"] = [near] + swap_tp(near)
        return sent

    def beside_last_sum(sent):
        keys = tie(held["keys"], sent)
        held["attended"] = attend(queries, keys, block_request, block_used)
        return sent

    hooks = {0: beside_first_sum, 2: beside_third_sum, len(bits) - 1: beside_last_sum}
    return (scatter_sums(sums, orders, hooks), held["attended"])


def solution(mesh):
    placed = (
        P("ep", "tp"),
        P("ep", None),
        P("ep", None),
        P("ep", None, None, "tp"),
        P("ep", None, "tp"),
        P("ep", "tp", None),
        P("ep", None, None),
        P(),
        P("ep"),
        P("ep"),
    )
    return jax.shard_map(
        body,
        mesh=mesh,
        in_specs=placed,
        out_specs=(P("ep", "tp"), P("ep", "tp", None)),
        check_vma=False,
    )
```

```python
import functools

import jax
import jax.numpy as jnp
from jax import lax
from jax.experimental import pallas as pl
from jax.experimental.pallas import tpu as pltpu
from jax.sharding import PartitionSpec as P

KV = 512


score_scale = 192.0 ** (-0.5)

WHOLE = pl.BlockSpec(memory_space=pltpu.VMEM)


def kernel_call(kernel, out_shape, arguments, flops, spare, in_specs=None, scratch_shapes=()):
    held = sum(array.size * array.dtype.itemsize for array in jax.tree.leaves(out_shape))
    for array, spec in zip(arguments, in_specs or [WHOLE] * len(arguments)):
        held += array.size * array.dtype.itemsize if spec is WHOLE else 0
    moved = sum(array.size * array.dtype.itemsize for array in arguments)
    return pl.pallas_call(
        kernel,
        out_shape=out_shape,
        in_specs=in_specs or [WHOLE] * len(arguments),
        out_specs=jax.tree.map(lambda _: WHOLE, out_shape),
        scratch_shapes=scratch_shapes,
        compiler_params=pltpu.CompilerParams(vmem_limit_bytes=held + spare),
        cost_estimate=pl.CostEstimate(
            flops=flops, bytes_accessed=moved + held, transcendentals=0
        ),
    )(*arguments)


def tie(values, others):
    return lax.optimization_barrier((values, others))[0]


def ep_bits():
    ep_size = lax.axis_size("ep")
    return [1 << place for place in reversed(range(ep_size.bit_length() - 1))]


def exchange(value, bit):
    ep_size = lax.axis_size("ep")
    return lax.ppermute(value, "ep", [(index, index ^ bit) for index in range(ep_size)])


def pass_tp(value, step):
    tp_size = lax.axis_size("tp")
    return lax.ppermute(
        value, "tp", [(index, (index + step) % tp_size) for index in range(tp_size)]
    )


def swap_tp(value):
    return [pass_tp(value, step) for step in range(1, lax.axis_size("tp"))]


def gather_rows(rows, others, orders, ends, beside, ahead):
    shared = orders[0][:-2]
    values = [
        jnp.concatenate([value[None], exchange(value[None], shared[0])], axis=0)
        for value in (rows, others)
    ]
    value = jnp.concatenate(values, axis=2)
    for bit in shared[1:]:
        if bit == shared[-1]:
            beside(value)
        value = jnp.concatenate([value, exchange(value, bit)], axis=0)
    halves = []
    for order, start, end in zip(orders, (0,) + ends, ends):
        part = value[:, :, start:end]
        part = jnp.concatenate([part, exchange(part, order[-2])], axis=0)
        if end == ends[-1]:
            part = ahead(part)
        halves.append((part, exchange(part, order[-1])))
    return halves


def places_of(order):
    places = [0]
    for bit in order:
        places = places + [place ^ bit for place in places]
    return places


def join_kernel(spots, ends, count, tp_size, *refs):
    out = refs[-1]
    parts = len(spots)
    rows = out.shape[0] // len(spots[0])
    width = out.shape[1] // tp_size
    index = lax.axis_index("tp")

    def place(tp_index):
        for step in range(tp_size):
            owner = (tp_index - step) % tp_size
            for part in range(parts):
                start, end = ((0,) + ends)[part], ends[part]
                for half in range(2):
                    ref = refs[(step * parts + part) * 2 + half]
                    blocks = ref.shape[0] // rows
                    for block in range(blocks):
                        spot = spots[part][half * blocks + block] * rows
                        out[spot : spot + rows, owner * width + start : owner * width + end] = ref[
                            block * rows : (block + 1) * rows, : end - start
                        ]

    for tp_index in range(tp_size):
        pl.when(index == tp_index)(functools.partial(place, tp_index))


def join_rows(by_step, spots, ends, rows):
    tp_size = len(by_step)
    arrays = [
        half.reshape(-1, half.shape[-1]) for parts in by_step for pair in parts for half in pair
    ]
    shape = jax.ShapeDtypeStruct((len(spots[0]) * rows, ends[-1] * tp_size), jnp.bfloat16)
    return kernel_call(
        functools.partial(join_kernel, spots, ends, len(arrays), tp_size),
        shape,
        arrays,
        flops=0,
        spare=4 << 20,
    )


def scatter_sums(parts, orders, hooks):
    steps = len(orders[0])
    for step in range(steps):
        half = parts[0][0].shape[0] // 2
        sents = [add_up([term[half:] for term in terms]) for terms in parts]
        kepts = [[term[:half] for term in terms] for terms in parts]
        if step > 0:
            kepts = [[add_up(terms)] for terms in kepts]
        if step == 2:
            sents = [jnp.concatenate(sents, axis=1)]
            kepts = [[jnp.concatenate([kept for kept, in kepts], axis=1)]]
        if step in hooks:
            sents[-1] = hooks[step](sents[-1])
        parts = [
            kept + [exchange(sent, order[steps - 1 - step])]
            for kept, sent, order in zip(kepts, sents, orders)
        ]
    parts[0][-1] = hooks[-1](parts[0][-1])
    return add_up(parts[0])


def add_up(terms):
    total = terms[0].astype(jnp.float32)
    for term in terms[1:]:
        total = total + term.astype(jnp.float32)
    return total.astype(jnp.bfloat16)


def three_parts(value):
    parts = []
    for _ in range(3):
        part = lax.reduce_precision(value, 8, 7)
        parts.append(part.astype(jnp.bfloat16))
        value = value - part
    return parts


def down_kernel(spots, tp_size, cut, width, rows, hidden, weight, *refs):
    parts = len(spots)
    outs, (held, turned, arrived) = refs[:-3], refs[-3:]
    copies = []
    for step in range(tp_size):
        target = lax.rem(lax.axis_index("tp") + step + 1, tp_size)
        for part in range(parts):
            run = step * parts + part
            start = pl.multiple_of((target * parts + part) * cut, cut)
            copies.append(
                pltpu.make_async_copy(
                    weight.at[pl.ds(start, cut)],
                    held.at[pl.ds(run * cut, cut)],
                    arrived.at[run],
                )
            )
    for copy in copies:
        copy.start()
    chunk = min(256, hidden.shape[0])
    for part in range(parts):
        for block, spot in enumerate(spots[part]):
            turned[part, spot * rows : (spot + 1) * rows] = hidden[
                block * rows : (block + 1) * rows
            ]
    for run, copy in enumerate(copies):
        copy.wait()
        for column in range(0, cut, width):
            for row in range(0, hidden.shape[0], chunk):
                outs[run][row : row + chunk, column : column + width] = lax.dot_general(
                    turned[run % parts, row : row + chunk],
                    held[run * cut + column : run * cut + column + width],
                    (((1,), (1,)), ((), ())),
                    preferred_element_type=jnp.float32,
                ).astype(jnp.bfloat16)


def down(hidden, weight, spots, rows):
    parts = len(spots)
    tp_size = lax.axis_size("tp")
    cut = weight.shape[0] // tp_size // parts
    width = cut
    shape = jax.ShapeDtypeStruct((hidden.shape[0], cut), jnp.bfloat16)
    outs = kernel_call(
        functools.partial(down_kernel, spots, tp_size, cut, width, rows),
        [shape] * (parts * tp_size),
        [hidden, weight],
        flops=2 * hidden.size * weight.shape[0],
        spare=weight.size * 2 + (8 << 20),
        in_specs=[WHOLE, pl.BlockSpec(memory_space=pl.ANY)],
        scratch_shapes=[
            pltpu.VMEM(weight.shape, weight.dtype),
            pltpu.VMEM((parts,) + hidden.shape, hidden.dtype),
            pltpu.SemaphoreType.DMA((parts * tp_size,)),
        ],
    )
    return [outs[step * parts : (step + 1) * parts] for step in range(tp_size)]


def order_kernel(index, *refs):
    rows, out = refs[:-1], refs[-1]
    columns = lax.broadcasted_iota(jnp.int32, (out.shape[0], rows[0].shape[0]), 1)
    total = jnp.zeros(out.shape, jnp.float32)
    for step, ref in enumerate(rows):
        hot = (columns == index[:, step : step + 1]).astype(jnp.bfloat16)
        total = total + jnp.dot(hot, ref[...], preferred_element_type=jnp.float32)
    out[...] = total.astype(out.dtype)


def cache_out(latent_cache):
    ep_size = lax.axis_size("ep")
    slots, block_size, latent = latent_cache.shape
    share = slots // lax.axis_size("tp")
    mine = lax.dynamic_slice_in_dim(latent_cache, lax.axis_index("tp") * share, share, axis=0)
    return mine.reshape(share, ep_size, block_size * latent // ep_size).transpose(1, 0, 2)


def cache_turn(spread, block_source, slots):
    ep_size = lax.axis_size("ep")
    tp_size = lax.axis_size("tp")
    tp_index = lax.axis_index("tp")
    share, piece = spread.shape[1:]
    wanted = lax.dynamic_slice_in_dim(
        block_source.reshape(ep_size, tp_size, share), tp_index, 1, axis=1
    ).reshape(-1)
    place = (wanted // slots) * share + wanted % share
    holder = (wanted % slots) // share
    from_step = (tp_index + tp_size - holder) % tp_size
    index = jnp.where(
        from_step[:, None] == jnp.arange(tp_size, dtype=jnp.int32)[None, :], place[:, None], -1
    )
    rows = [part.reshape(-1, piece) for part in [spread] + swap_tp(spread)]
    shape = jax.ShapeDtypeStruct(rows[0].shape, rows[0].dtype)
    ordered = kernel_call(
        order_kernel,
        shape,
        [index] + rows,
        flops=2 * tp_size * rows[0].size * rows[0].shape[0],
        spare=6 << 20,
    )
    return ordered.reshape(ep_size, share, piece)


def cache_in(ordered, block_size, latent):
    share, piece = ordered.shape[1:]
    arrived = lax.all_to_all(ordered, "ep", split_axis=0, concat_axis=0, tiled=True)
    if piece != latent:
        arrived = arrived.transpose(1, 0, 2).reshape(share, block_size, latent).transpose(1, 0, 2)
    return arrived


def attention_kernel(heads, chunk, owner, queries, *refs):
    keys, out = refs[:-1], refs[-1]
    for start in range(0, queries.shape[0], chunk):
        row = lax.broadcasted_iota(jnp.int32, (chunk, keys[0].shape[0]), 0) + start
        if heads & (heads - 1):
            row = row // heads
        else:
            row = row >> (heads.bit_length() - 1)
        scores = []
        for step, key in enumerate(keys):
            part = lax.dot_general(
                queries[start : start + chunk],
                key[...],
                (((1,), (1,)), ((), ())),
                preferred_element_type=jnp.float32,
            )
            scores.append(
                jnp.where(row == owner[step : step + 1, :], part * score_scale, -jnp.inf)
            )
        row_max = scores[0].max(axis=1, keepdims=True)
        for part in scores[1:]:
            row_max = jnp.maximum(row_max, part.max(axis=1, keepdims=True))
        terms = [jnp.exp(part - row_max) for part in scores]
        total = 1.0 / sum(term.sum(axis=1, keepdims=True) for term in terms)
        attended = jnp.zeros((chunk, KV), jnp.float32)
        for term, key in zip(terms, keys):
            attended = attended + jnp.dot(
                (term * total).astype(jnp.bfloat16),
                key[:, :KV],
                preferred_element_type=jnp.float32,
            )
        out[start : start + chunk] = attended.astype(out.dtype)


def attend(queries, keys, block_request, block_used):
    tp_size = lax.axis_size("tp")
    row_count, heads, latent = queries.shape
    block_size, share = keys[0].shape[:2]
    within = jnp.arange(block_size, dtype=jnp.int32)[:, None]
    owners = []
    for step in range(tp_size):
        first = ((lax.axis_index("tp") + tp_size - step) % tp_size) * share
        owner = lax.dynamic_slice_in_dim(block_request, first, share)[None, :]
        limit = lax.dynamic_slice_in_dim(block_used, first, share)[None, :]
        owners.append(jnp.where(within < limit, owner, -1).reshape(1, -1))
    keys = [part.reshape(-1, latent) for part in keys]
    rows = queries.reshape(-1, latent)
    shape = jax.ShapeDtypeStruct((rows.shape[0], KV), jnp.bfloat16)
    result = kernel_call(
        functools.partial(attention_kernel, heads, min(256, rows.shape[0])),
        shape,
        [jnp.concatenate(owners, axis=0), rows] + keys,
        flops=4 * rows.size * keys[0].shape[0] * tp_size,
        spare=8 << 20,
    )
    return result.reshape(row_count, heads, KV)


def body(
    tokens,
    expert_ids,
    gate_weights,
    expert_gate_up,
    expert_down,
    queries,
    latent_cache,
    block_source,
    block_request,
    block_used,
):
    row_count, top_count = expert_ids.shape
    slot_total, block_size, latent = latent_cache.shape
    ep_size = lax.axis_size("ep")
    tp_size = lax.axis_size("tp")
    tp_index = lax.axis_index("tp")
    bits = ep_bits()
    orders = (bits, bits[:-2] + [bits[-1], bits[-2]])
    parts = len(orders)
    cut = tokens.shape[1] // parts

    expert_range = jnp.arange(ep_size, dtype=jnp.int32)
    dense_gate = jnp.sum(
        jnp.where(
            expert_ids[:, :, None] == expert_range[None, None, :], gate_weights[:, :, None], 0.0
        ),
        axis=1,
    )
    gate_parts = jnp.concatenate(three_parts(dense_gate), axis=1)
    pad = -gate_parts.shape[1] % 128
    gates = jnp.pad(gate_parts, ((0, 0), (0, pad)))
    ends = tuple(cut * part for part in range(1, parts)) + (tokens.shape[1] + gates.shape[1],)
    held = {}

    def beside_shared(sent):
        pieces = tie(cache_out(latent_cache), sent)
        held["spread"] = lax.all_to_all(pieces, "ep", split_axis=0, concat_axis=0, tiled=True)

    def ahead_of_last(sent):
        sent, held["spread"] = lax.optimization_barrier((sent, held["spread"]))
        return sent

    halves = gather_rows(tokens, gates, orders, ends, beside_shared, ahead_of_last)
    last_sent = halves[-1][0]
    ordered = cache_turn(held["spread"], tie(block_source, last_sent), slot_total)
    first_late, ordered = lax.optimization_barrier((halves[0][1], ordered))
    halves[0] = (halves[0][0], first_late)
    places = [places_of(order) for order in orders]
    to_first = [[places[0].index(place) for place in own] for own in places]
    from_first = [[own.index(place) for place in places[0]] for own in places]

    passed = [tie(early, last_sent) for early, _ in halves[:-1]]
    passed.append(tie(last_sent, halves[0][1]))
    arrived = [
        [(pass_tp(early, step), pass_tp(late, step)) for early, (_, late) in zip(passed, halves)]
        for step in range(1, tp_size)
    ]
    all_rows = join_rows(
        [halves] + arrived, to_first, tuple(cut * part for part in range(1, parts + 1)), row_count
    )
    gate_halves = [half[..., cut : cut + 3 * ep_size] for half in halves[-1]]
    all_gate = jnp.concatenate(gate_halves, axis=0)
    all_gate = jnp.stack([all_gate[block] for block in from_first[-1]]).astype(jnp.float32)
    mine = (jnp.arange(3 * ep_size, dtype=jnp.int32) % ep_size) == lax.axis_index("ep")
    my_gate = jnp.sum(jnp.where(mine, all_gate, 0.0), axis=2).reshape(-1)
    gate_and_up = jnp.einsum(
        "sd,dgf->sgf", all_rows, expert_gate_up[0], preferred_element_type=jnp.float32
    )
    hidden = (
        jax.nn.silu(gate_and_up[:, 0]) * gate_and_up[:, 1] * my_gate[:, None]
    ).astype(jnp.bfloat16)

    down_weight = pltpu.with_memory_space_constraint(expert_down[0], pltpu.HBM)
    by_step = down(hidden, down_weight, from_first, row_count)
    sums = [[own] for own in by_step[-1]]
    for part in range(parts):
        for step in range(1, tp_size):
            sums[part].append(pass_tp(by_step[step - 1][part], step))

    def beside_first_sum(sent):
        held["keys"] = cache_in(tie(ordered, sent), block_size, latent)
        return sent

    def beside_third_sum(sent):
        sent, near = lax.optimization_barrier((sent, held["keys"]))
        held["keys"] = [near] + swap_tp(near)
        return sent

    def beside_last_sum(sent):
        sent, keys = lax.optimization_barrier((sent, held["keys"]))
        held["attended"] = attend(queries, keys, block_request, block_used)
        return sent

    def ahead_of_end(arrived):
        arrived, held["attended"] = lax.optimization_barrier((arrived, held["attended"]))
        return arrived

    hooks = {
        0: beside_first_sum,
        2: beside_third_sum,
        len(bits) - 1: beside_last_sum,
        -1: ahead_of_end,
    }
    return (scatter_sums(sums, orders, hooks), held["attended"])


def solution(mesh):
    placed = (
        P("ep", "tp"),
        P("ep", None),
        P("ep", None),
        P("ep", None, None, "tp"),
        P("ep", None, "tp"),
        P("ep", "tp", None),
        P("ep", None, None),
        P(),
        P("ep"),
        P("ep"),
    )
    return jax.shard_map(
        body,
        mesh=mesh,
        in_specs=placed,
        out_specs=(P("ep", "tp"), P("ep", "tp", None)),
        check_vma=False,
    )
```

```python
import functools

import jax
import jax.numpy as jnp
from jax import lax
from jax.experimental import pallas as pl
from jax.experimental.pallas import tpu as pltpu
from jax.sharding import PartitionSpec as P

KV = 512


score_scale = 192.0 ** (-0.5)

WHOLE = pl.BlockSpec(memory_space=pltpu.VMEM)


def kernel_call(kernel, out_shape, arguments, flops, spare, in_specs=None, scratch_shapes=()):
    held = sum(array.size * array.dtype.itemsize for array in jax.tree.leaves(out_shape))
    for array, spec in zip(arguments, in_specs or [WHOLE] * len(arguments)):
        held += array.size * array.dtype.itemsize if spec is WHOLE else 0
    moved = sum(array.size * array.dtype.itemsize for array in arguments)
    return pl.pallas_call(
        kernel,
        out_shape=out_shape,
        in_specs=in_specs or [WHOLE] * len(arguments),
        out_specs=jax.tree.map(lambda _: WHOLE, out_shape),
        scratch_shapes=scratch_shapes,
        compiler_params=pltpu.CompilerParams(vmem_limit_bytes=held + spare),
        cost_estimate=pl.CostEstimate(
            flops=flops, bytes_accessed=moved + held, transcendentals=0
        ),
    )(*arguments)


def tie(values, others):
    return lax.optimization_barrier((values, others))[0]


def ep_bits():
    ep_size = lax.axis_size("ep")
    return [1 << place for place in reversed(range(ep_size.bit_length() - 1))]


def exchange(value, bit):
    ep_size = lax.axis_size("ep")
    return lax.ppermute(value, "ep", [(index, index ^ bit) for index in range(ep_size)])


def pass_tp(value, step):
    tp_size = lax.axis_size("tp")
    return lax.ppermute(
        value, "tp", [(index, (index + step) % tp_size) for index in range(tp_size)]
    )


def swap_tp(value):
    return [pass_tp(value, step) for step in range(1, lax.axis_size("tp"))]


def gather_rows(rows, others, orders, ends, beside, ahead):
    shared = orders[0][:-2]
    values = [
        jnp.concatenate([value[None], exchange(value[None], shared[0])], axis=0)
        for value in (rows, others)
    ]
    value = jnp.concatenate(values, axis=2)
    for bit in shared[1:]:
        if bit == shared[-1]:
            beside(value)
        value = jnp.concatenate([value, exchange(value, bit)], axis=0)
    halves = []
    for order, start, end in zip(orders, (0,) + ends, ends):
        part = value[:, :, start:end]
        part = jnp.concatenate([part, exchange(part, order[-2])], axis=0)
        if end == ends[-1]:
            part = ahead(part)
        halves.append((part, exchange(part, order[-1])))
    return halves


def places_of(order):
    places = [0]
    for bit in order:
        places = places + [place ^ bit for place in places]
    return places


def join_kernel(spots, ends, count, tp_size, *refs):
    out = refs[-1]
    parts = len(spots)
    rows = out.shape[0] // len(spots[0])
    width = out.shape[1] // tp_size
    index = lax.axis_index("tp")

    def place(tp_index):
        for step in range(tp_size):
            owner = (tp_index - step) % tp_size
            for part in range(parts):
                start, end = ((0,) + ends)[part], ends[part]
                for half in range(2):
                    ref = refs[(step * parts + part) * 2 + half]
                    blocks = ref.shape[0] // rows
                    for block in range(blocks):
                        spot = spots[part][half * blocks + block] * rows
                        out[spot : spot + rows, owner * width + start : owner * width + end] = ref[
                            block * rows : (block + 1) * rows, : end - start
                        ]

    for tp_index in range(tp_size):
        pl.when(index == tp_index)(functools.partial(place, tp_index))


def join_rows(by_step, spots, ends, rows):
    tp_size = len(by_step)
    arrays = [
        half.reshape(-1, half.shape[-1]) for parts in by_step for pair in parts for half in pair
    ]
    shape = jax.ShapeDtypeStruct((len(spots[0]) * rows, ends[-1] * tp_size), jnp.bfloat16)
    return kernel_call(
        functools.partial(join_kernel, spots, ends, len(arrays), tp_size),
        shape,
        arrays,
        flops=0,
        spare=4 << 20,
    )


def scatter_sums(sums, orders, hooks):
    steps = len(orders[0])
    kepts, sents = zip(*sums)
    kepts, sents = list(kepts), list(sents)
    for step in range(steps):
        if step in hooks:
            sents[-1] = hooks[step](sents[-1])
        terms = [
            [kept, exchange(sent, order[steps - 1 - step])]
            for kept, sent, order in zip(kepts, sents, orders)
        ]
        if step == steps - 1:
            break
        half = kepts[0].shape[0] // 2
        sents = [add_up([term[half:] for term in pair]) for pair in terms]
        kepts = [add_up([term[:half] for term in pair]) for pair in terms]
        if step == 1:
            sents = [jnp.concatenate(sents, axis=1)]
            kepts = [jnp.concatenate(kepts, axis=1)]
    kept, arrived = terms[0]
    return add_up([kept, hooks[-1](arrived)])


def add_up(terms):
    total = terms[0].astype(jnp.float32)
    for term in terms[1:]:
        total = total + term.astype(jnp.float32)
    return total.astype(jnp.bfloat16)


def three_parts(value):
    parts = []
    for _ in range(3):
        part = lax.reduce_precision(value, 8, 7)
        parts.append(part.astype(jnp.bfloat16))
        value = value - part
    return parts


def turn_rows(hidden, turned, spots, rows):
    for block, spot in enumerate(spots):
        turned[spot * rows : (spot + 1) * rows] = hidden[block * rows : (block + 1) * rows]


def down_product(turned, weight, row, chunk, column, width):
    return lax.dot_general(
        turned[row : row + chunk],
        weight[column : column + width],
        (((1,), (1,)), ((), ())),
        preferred_element_type=jnp.float32,
    )


def others_kernel(step, spots, tp_size, cut, rows, hidden, weight, *refs):
    parts = len(spots)
    outs, (held, turned, arrived) = refs[:parts], refs[parts:]
    target = lax.rem(lax.axis_index("tp") + step, tp_size)
    copies = []
    for part in range(parts):
        start = pl.multiple_of((target * parts + part) * cut, cut)
        copies.append(
            pltpu.make_async_copy(
                weight.at[pl.ds(start, cut)], held.at[part], arrived.at[part]
            )
        )
    for copy in copies:
        copy.start()
    chunk = min(256, hidden.shape[0])
    for part, copy in enumerate(copies):
        turn_rows(hidden, turned.at[part], spots[part], rows)
        copy.wait()
        for row in range(0, hidden.shape[0], chunk):
            outs[part][row : row + chunk] = down_product(
                turned.at[part], held.at[part], row, chunk, 0, cut
            ).astype(jnp.bfloat16)


def down_others(hidden, weight, step, spots, rows):
    parts = len(spots)
    tp_size = lax.axis_size("tp")
    cut = weight.shape[0] // tp_size // parts
    shape = jax.ShapeDtypeStruct((hidden.shape[0], cut), jnp.bfloat16)
    return kernel_call(
        functools.partial(others_kernel, step, spots, tp_size, cut, rows),
        [shape] * parts,
        [hidden, weight],
        flops=2 * hidden.size * cut * parts,
        spare=parts * cut * weight.shape[1] * 2 + (8 << 20),
        in_specs=[WHOLE, pl.BlockSpec(memory_space=pl.ANY)],
        scratch_shapes=[
            pltpu.VMEM((parts, cut, weight.shape[1]), weight.dtype),
            pltpu.VMEM((parts,) + hidden.shape, hidden.dtype),
            pltpu.SemaphoreType.DMA((parts,)),
        ],
    )


def own_kernel(part, parts, spots, cut, rows, count, hidden, weight, *refs):
    others, (kept, sent, held, turned, passed, arrived) = refs[:count], refs[count:]
    start = pl.multiple_of((lax.axis_index("tp") * parts + part) * cut, cut)
    copies = [pltpu.make_async_copy(weight.at[pl.ds(start, cut)], held, arrived.at[count])]
    for index, other in enumerate(others):
        copies.append(pltpu.make_async_copy(other, passed.at[index], arrived.at[index]))
    for copy in copies:
        copy.start()
    turn_rows(hidden, turned, spots, rows)
    for copy in copies:
        copy.wait()
    half = hidden.shape[0] // 2
    chunk = min(256, hidden.shape[0])
    width = cut // 2 if cut % 256 == 0 else cut
    for column in range(0, cut, width):
        for row in range(0, hidden.shape[0], chunk):
            total = down_product(turned, held, row, chunk, column, width)
            for index in range(count):
                total = total + passed[
                    index, row : row + chunk, column : column + width
                ].astype(jnp.float32)
            total = total.astype(jnp.bfloat16)
            for first in range(row, row + chunk, min(chunk, half)):
                out = kept if first < half else sent
                place = first % half
                piece = total[first - row : first - row + min(chunk, half)]
                out[place : place + piece.shape[0], column : column + width] = piece


def down_own(hidden, weight, part, parts, spots, rows, others):
    cut = weight.shape[0] // lax.axis_size("tp") // parts
    shape = jax.ShapeDtypeStruct((hidden.shape[0] // 2, cut), jnp.bfloat16)
    anywhere = pl.BlockSpec(memory_space=pl.ANY)
    return kernel_call(
        functools.partial(own_kernel, part, parts, spots, cut, rows, len(others)),
        [shape, shape],
        [hidden, weight] + others,
        flops=2 * hidden.size * cut,
        spare=(cut * weight.shape[1] + hidden.shape[0] * cut * len(others)) * 2 + (8 << 20),
        in_specs=[WHOLE] + [anywhere] * (1 + len(others)),
        scratch_shapes=[
            pltpu.VMEM((cut, weight.shape[1]), weight.dtype),
            pltpu.VMEM(hidden.shape, hidden.dtype),
            pltpu.VMEM((len(others), hidden.shape[0], cut), jnp.bfloat16),
            pltpu.SemaphoreType.DMA((1 + len(others),)),
        ],
    )


def order_kernel(index, *refs):
    rows, out = refs[:-1], refs[-1]
    columns = lax.broadcasted_iota(jnp.int32, (out.shape[0], rows[0].shape[0]), 1)
    total = jnp.zeros(out.shape, jnp.float32)
    for step, ref in enumerate(rows):
        hot = (columns == index[:, step : step + 1]).astype(jnp.bfloat16)
        total = total + jnp.dot(hot, ref[...], preferred_element_type=jnp.float32)
    out[...] = total.astype(out.dtype)


def cache_out(latent_cache):
    ep_size = lax.axis_size("ep")
    slots, block_size, latent = latent_cache.shape
    share = slots // lax.axis_size("tp")
    mine = lax.dynamic_slice_in_dim(latent_cache, lax.axis_index("tp") * share, share, axis=0)
    return mine.reshape(share, ep_size, block_size * latent // ep_size).transpose(1, 0, 2)


def cache_turn(spread, block_source, slots):
    ep_size = lax.axis_size("ep")
    tp_size = lax.axis_size("tp")
    tp_index = lax.axis_index("tp")
    share, piece = spread.shape[1:]
    wanted = lax.dynamic_slice_in_dim(
        block_source.reshape(ep_size, tp_size, share), tp_index, 1, axis=1
    ).reshape(-1)
    place = (wanted // slots) * share + wanted % share
    holder = (wanted % slots) // share
    from_step = (tp_index + tp_size - holder) % tp_size
    index = jnp.where(
        from_step[:, None] == jnp.arange(tp_size, dtype=jnp.int32)[None, :], place[:, None], -1
    )
    rows = [part.reshape(-1, piece) for part in [spread] + swap_tp(spread)]
    shape = jax.ShapeDtypeStruct(rows[0].shape, rows[0].dtype)
    ordered = kernel_call(
        order_kernel,
        shape,
        [index] + rows,
        flops=2 * tp_size * rows[0].size * rows[0].shape[0],
        spare=6 << 20,
    )
    return ordered.reshape(ep_size, share, piece)


def cache_in(ordered, block_size, latent):
    share, piece = ordered.shape[1:]
    arrived = lax.all_to_all(ordered, "ep", split_axis=0, concat_axis=0, tiled=True)
    if piece != latent:
        arrived = arrived.transpose(1, 0, 2).reshape(share, block_size, latent).transpose(1, 0, 2)
    return arrived


def attention_kernel(heads, chunk, owner, queries, *refs):
    keys, out = refs[:-1], refs[-1]
    for start in range(0, queries.shape[0], chunk):
        row = lax.broadcasted_iota(jnp.int32, (chunk, keys[0].shape[0]), 0) + start
        if heads & (heads - 1):
            row = row // heads
        else:
            row = row >> (heads.bit_length() - 1)
        scores = []
        for step, key in enumerate(keys):
            part = lax.dot_general(
                queries[start : start + chunk],
                key[...],
                (((1,), (1,)), ((), ())),
                preferred_element_type=jnp.float32,
            )
            scores.append(
                jnp.where(row == owner[step : step + 1, :], part * score_scale, -jnp.inf)
            )
        row_max = scores[0].max(axis=1, keepdims=True)
        for part in scores[1:]:
            row_max = jnp.maximum(row_max, part.max(axis=1, keepdims=True))
        terms = [jnp.exp(part - row_max) for part in scores]
        total = 1.0 / sum(term.sum(axis=1, keepdims=True) for term in terms)
        attended = jnp.zeros((chunk, KV), jnp.float32)
        for term, key in zip(terms, keys):
            attended = attended + jnp.dot(
                (term * total).astype(jnp.bfloat16),
                key[:, :KV],
                preferred_element_type=jnp.float32,
            )
        out[start : start + chunk] = attended.astype(out.dtype)


def attend(queries, keys, block_request, block_used):
    tp_size = lax.axis_size("tp")
    row_count, heads, latent = queries.shape
    block_size, share = keys[0].shape[:2]
    within = jnp.arange(block_size, dtype=jnp.int32)[:, None]
    owners = []
    for step in range(tp_size):
        first = ((lax.axis_index("tp") + tp_size - step) % tp_size) * share
        owner = lax.dynamic_slice_in_dim(block_request, first, share)[None, :]
        limit = lax.dynamic_slice_in_dim(block_used, first, share)[None, :]
        owners.append(jnp.where(within < limit, owner, -1).reshape(1, -1))
    keys = [part.reshape(-1, latent) for part in keys]
    rows = queries.reshape(-1, latent)
    shape = jax.ShapeDtypeStruct((rows.shape[0], KV), jnp.bfloat16)
    result = kernel_call(
        functools.partial(attention_kernel, heads, min(256, rows.shape[0])),
        shape,
        [jnp.concatenate(owners, axis=0), rows] + keys,
        flops=4 * rows.size * keys[0].shape[0] * tp_size,
        spare=8 << 20,
    )
    return result.reshape(row_count, heads, KV)


def body(
    tokens,
    expert_ids,
    gate_weights,
    expert_gate_up,
    expert_down,
    queries,
    latent_cache,
    block_source,
    block_request,
    block_used,
):
    row_count, top_count = expert_ids.shape
    slot_total, block_size, latent = latent_cache.shape
    ep_size = lax.axis_size("ep")
    tp_size = lax.axis_size("tp")
    tp_index = lax.axis_index("tp")
    bits = ep_bits()
    orders = (bits, bits[:-2] + [bits[-1], bits[-2]])
    parts = len(orders)
    cut = tokens.shape[1] // parts

    expert_range = jnp.arange(ep_size, dtype=jnp.int32)
    dense_gate = jnp.sum(
        jnp.where(
            expert_ids[:, :, None] == expert_range[None, None, :], gate_weights[:, :, None], 0.0
        ),
        axis=1,
    )
    gate_parts = jnp.concatenate(three_parts(dense_gate), axis=1)
    pad = -gate_parts.shape[1] % 128
    gates = jnp.pad(gate_parts, ((0, 0), (0, pad)))
    ends = tuple(cut * part for part in range(1, parts)) + (tokens.shape[1] + gates.shape[1],)
    held = {}

    def beside_shared(sent):
        pieces = tie(cache_out(latent_cache), sent)
        held["spread"] = lax.all_to_all(pieces, "ep", split_axis=0, concat_axis=0, tiled=True)

    def ahead_of_last(sent):
        sent, held["spread"] = lax.optimization_barrier((sent, held["spread"]))
        return sent

    halves = gather_rows(tokens, gates, orders, ends, beside_shared, ahead_of_last)
    last_sent = halves[-1][0]
    ordered = cache_turn(held["spread"], tie(block_source, last_sent), slot_total)
    first_late, ordered = lax.optimization_barrier((halves[0][1], ordered))
    halves[0] = (halves[0][0], first_late)
    places = [places_of(order) for order in orders]
    to_first = [[places[0].index(place) for place in own] for own in places]
    from_first = [[own.index(place) for place in places[0]] for own in places]

    passed = [tie(early, last_sent) for early, _ in halves[:-1]]
    passed.append(tie(last_sent, halves[0][1]))
    arrived = [
        [(pass_tp(early, step), pass_tp(late, step)) for early, (_, late) in zip(passed, halves)]
        for step in range(1, tp_size)
    ]
    all_rows = join_rows(
        [halves] + arrived, to_first, tuple(cut * part for part in range(1, parts + 1)), row_count
    )
    gate_halves = [half[..., cut : cut + 3 * ep_size] for half in halves[-1]]
    all_gate = jnp.concatenate(gate_halves, axis=0)
    all_gate = jnp.stack([all_gate[block] for block in from_first[-1]]).astype(jnp.float32)
    mine = (jnp.arange(3 * ep_size, dtype=jnp.int32) % ep_size) == lax.axis_index("ep")
    my_gate = jnp.sum(jnp.where(mine, all_gate, 0.0), axis=2).reshape(-1)
    gate_and_up = jnp.einsum(
        "sd,dgf->sgf", all_rows, expert_gate_up[0], preferred_element_type=jnp.float32
    )
    hidden = (
        jax.nn.silu(gate_and_up[:, 0]) * gate_and_up[:, 1] * my_gate[:, None]
    ).astype(jnp.bfloat16)

    down_weight = pltpu.with_memory_space_constraint(expert_down[0], pltpu.HBM)
    passed = [[] for _ in range(parts)]
    for step in range(1, tp_size):
        others = down_others(hidden, down_weight, step, from_first, row_count)
        for part in range(parts):
            passed[part].append(pass_tp(others[part], step))
    sums = [
        down_own(hidden, down_weight, part, parts, from_first[part], row_count, passed[part])
        for part in range(parts)
    ]

    def beside_first_sum(sent):
        held["keys"] = cache_in(tie(ordered, sent), block_size, latent)
        return sent

    def beside_third_sum(sent):
        sent, near = lax.optimization_barrier((sent, held["keys"]))
        held["keys"] = [near] + swap_tp(near)
        return sent

    def beside_last_sum(sent):
        sent, keys = lax.optimization_barrier((sent, held["keys"]))
        held["attended"] = attend(queries, keys, block_request, block_used)
        return sent

    def ahead_of_end(arrived):
        arrived, held["attended"] = lax.optimization_barrier((arrived, held["attended"]))
        return arrived

    hooks = {
        0: beside_first_sum,
        2: beside_third_sum,
        len(bits) - 1: beside_last_sum,
        -1: ahead_of_end,
    }
    return (scatter_sums(sums, orders, hooks), held["attended"])


def solution(mesh):
    placed = (
        P("ep", "tp"),
        P("ep", None),
        P("ep", None),
        P("ep", None, None, "tp"),
        P("ep", None, "tp"),
        P("ep", "tp", None),
        P("ep", None, None),
        P(),
        P("ep"),
        P("ep"),
    )
    return jax.shard_map(
        body,
        mesh=mesh,
        in_specs=placed,
        out_specs=(P("ep", "tp"), P("ep", "tp", None)),
        check_vma=False,
    )
```

```python
import functools

import jax
import jax.numpy as jnp
from jax import lax
from jax.experimental import pallas as pl
from jax.experimental.pallas import tpu as pltpu
from jax.sharding import PartitionSpec as P

KV = 512


score_scale = 192.0 ** (-0.5)

WHOLE = pl.BlockSpec(memory_space=pltpu.VMEM)


def kernel_call(kernel, out_shape, arguments, flops, spare, in_specs=None, scratch_shapes=()):
    held = sum(array.size * array.dtype.itemsize for array in jax.tree.leaves(out_shape))
    for array, spec in zip(arguments, in_specs or [WHOLE] * len(arguments)):
        held += array.size * array.dtype.itemsize if spec is WHOLE else 0
    moved = sum(array.size * array.dtype.itemsize for array in arguments)
    return pl.pallas_call(
        kernel,
        out_shape=out_shape,
        in_specs=in_specs or [WHOLE] * len(arguments),
        out_specs=jax.tree.map(lambda _: WHOLE, out_shape),
        scratch_shapes=scratch_shapes,
        compiler_params=pltpu.CompilerParams(vmem_limit_bytes=held + spare),
        cost_estimate=pl.CostEstimate(
            flops=flops, bytes_accessed=moved + held, transcendentals=0
        ),
    )(*arguments)


def tie(values, others):
    return lax.optimization_barrier((values, others))[0]


def ep_bits():
    ep_size = lax.axis_size("ep")
    return [1 << place for place in reversed(range(ep_size.bit_length() - 1))]


def exchange(value, bit):
    ep_size = lax.axis_size("ep")
    return lax.ppermute(value, "ep", [(index, index ^ bit) for index in range(ep_size)])


def pass_tp(value, step):
    tp_size = lax.axis_size("tp")
    return lax.ppermute(
        value, "tp", [(index, (index + step) % tp_size) for index in range(tp_size)]
    )


def swap_tp(value):
    return [pass_tp(value, step) for step in range(1, lax.axis_size("tp"))]


def gather_rows(rows, others, orders, ends, beside, ahead):
    shared = orders[0][:-2]
    values = [
        jnp.concatenate([value[None], exchange(value[None], shared[0])], axis=0)
        for value in (rows, others)
    ]
    value = jnp.concatenate(values, axis=2)
    for bit in shared[1:]:
        if bit == shared[-1]:
            beside(value)
        value = jnp.concatenate([value, exchange(value, bit)], axis=0)
    halves = []
    for order, start, end in zip(orders, (0,) + ends, ends):
        part = value[:, :, start:end]
        part = jnp.concatenate([part, exchange(part, order[-2])], axis=0)
        if end == ends[-1]:
            part = ahead(part)
        halves.append((part, exchange(part, order[-1])))
    return halves


def places_of(order):
    places = [0]
    for bit in order:
        places = places + [place ^ bit for place in places]
    return places


def join_kernel(spots, ends, count, tp_size, *refs):
    out = refs[-1]
    parts = len(spots)
    rows = out.shape[0] // len(spots[0])
    width = out.shape[1] // tp_size
    index = lax.axis_index("tp")

    def place(tp_index):
        for step in range(tp_size):
            owner = (tp_index - step) % tp_size
            for part in range(parts):
                start, end = ((0,) + ends)[part], ends[part]
                for half in range(2):
                    ref = refs[(step * parts + part) * 2 + half]
                    blocks = ref.shape[0] // rows
                    for block in range(blocks):
                        spot = spots[part][half * blocks + block] * rows
                        out[spot : spot + rows, owner * width + start : owner * width + end] = ref[
                            block * rows : (block + 1) * rows, : end - start
                        ]

    for tp_index in range(tp_size):
        pl.when(index == tp_index)(functools.partial(place, tp_index))


def join_rows(by_step, spots, ends, rows):
    tp_size = len(by_step)
    arrays = [
        half.reshape(-1, half.shape[-1]) for parts in by_step for pair in parts for half in pair
    ]
    shape = jax.ShapeDtypeStruct((len(spots[0]) * rows, ends[-1] * tp_size), jnp.bfloat16)
    return kernel_call(
        functools.partial(join_kernel, spots, ends, len(arrays), tp_size),
        shape,
        arrays,
        flops=0,
        spare=4 << 20,
    )


def scatter_sums(kepts, sents, orders, hooks):
    steps = len(orders[0])
    sents = list(sents)
    for step in range(steps):
        if step in hooks:
            sents[-1] = hooks[step](sents[-1])
        terms = [
            [kept, exchange(sent, order[steps - 1 - step])]
            for kept, sent, order in zip(kepts, sents, orders)
        ]
        if step == steps - 1:
            break
        half = kepts[0].shape[0] // 2
        sents = [add_up([term[half:] for term in pair]) for pair in terms]
        kepts = [add_up([term[:half] for term in pair]) for pair in terms]
        if step == 1:
            sents = [jnp.concatenate(sents, axis=1)]
            kepts = [jnp.concatenate(kepts, axis=1)]
    kept, arrived = terms[0]
    return add_up([kept, hooks[-1](arrived)])


def add_up(terms):
    total = terms[0].astype(jnp.float32)
    for term in terms[1:]:
        total = total + term.astype(jnp.float32)
    return total.astype(jnp.bfloat16)


def three_parts(value):
    parts = []
    for _ in range(3):
        part = lax.reduce_precision(value, 8, 7)
        parts.append(part.astype(jnp.bfloat16))
        value = value - part
    return parts


def turn_rows(hidden, turned, spots, rows):
    for block, spot in enumerate(spots):
        turned[spot * rows : (spot + 1) * rows] = hidden[block * rows : (block + 1) * rows]


def down_product(turned, weight, row, chunk, column, width):
    return lax.dot_general(
        turned[row : row + chunk],
        weight[column : column + width],
        (((1,), (1,)), ((), ())),
        preferred_element_type=jnp.float32,
    )


def group_kernel(step, spots, tp_size, cut, rows, hidden, weight, *refs):
    parts = len(spots)
    outs, (held, turned, arrived) = refs[:parts], refs[parts:]
    target = lax.rem(lax.axis_index("tp") + step, tp_size)
    copies = []
    for part in range(parts):
        start = pl.multiple_of((target * parts + part) * cut, cut)
        copies.append(
            pltpu.make_async_copy(
                weight.at[pl.ds(start, cut)], held.at[part], arrived.at[part]
            )
        )
    for copy in copies:
        copy.start()
    chunk = min(256, hidden.shape[0])
    for part, copy in enumerate(copies):
        turn_rows(hidden, turned.at[part], spots[part], rows)
        copy.wait()
        for row in range(0, hidden.shape[0], chunk):
            outs[part][row : row + chunk] = down_product(
                turned.at[part], held.at[part], row, chunk, 0, cut
            ).astype(jnp.bfloat16)


def down_group(hidden, weight, step, spots, rows):
    parts = len(spots)
    tp_size = lax.axis_size("tp")
    cut = weight.shape[0] // tp_size // parts
    shape = jax.ShapeDtypeStruct((hidden.shape[0], cut), jnp.bfloat16)
    return kernel_call(
        functools.partial(group_kernel, step, spots, tp_size, cut, rows),
        [shape] * parts,
        [hidden, weight],
        flops=2 * hidden.size * cut * parts,
        spare=parts * cut * weight.shape[1] * 2 + (8 << 20),
        in_specs=[WHOLE, pl.BlockSpec(memory_space=pl.ANY)],
        scratch_shapes=[
            pltpu.VMEM((parts, cut, weight.shape[1]), weight.dtype),
            pltpu.VMEM((parts,) + hidden.shape, hidden.dtype),
            pltpu.SemaphoreType.DMA((parts,)),
        ],
    )


def halves_kernel(parts, first, *refs):
    outs, (held, arrived) = refs[-2 - parts : -2], refs[-2:]
    terms = refs[: -2 - parts]
    count = len(terms) // parts
    half, rows = outs[0].shape[0], 16
    copies = [
        pltpu.make_async_copy(term.at[pl.ds(first, half)], held.at[index], arrived.at[index])
        for index, term in enumerate(terms)
    ]
    for copy in copies:
        copy.start()
    for part in range(parts):
        for index in range(part * count, (part + 1) * count):
            copies[index].wait()
        for row in range(0, half, rows):
            total = held[part * count, row : row + rows].astype(jnp.float32)
            for index in range(part * count + 1, (part + 1) * count):
                total = total + held[index, row : row + rows].astype(jnp.float32)
            outs[part][row : row + rows] = total.astype(jnp.bfloat16)


def add_halves(terms, second):
    parts = len(terms)
    flat = [term for part in terms for term in part]
    half, cut = flat[0].shape[0] // 2, flat[0].shape[1]
    return kernel_call(
        functools.partial(halves_kernel, parts, half if second else 0),
        [jax.ShapeDtypeStruct((half, cut), jnp.bfloat16)] * parts,
        flat,
        flops=half * cut * len(flat),
        spare=half * cut * len(flat) * 2 + (2 << 20),
        in_specs=[pl.BlockSpec(memory_space=pl.ANY)] * len(flat),
        scratch_shapes=[
            pltpu.VMEM((len(flat), half, cut), jnp.bfloat16),
            pltpu.SemaphoreType.DMA((len(flat),)),
        ],
    )


def order_kernel(index, *refs):
    rows, out = refs[:-1], refs[-1]
    columns = lax.broadcasted_iota(jnp.int32, (out.shape[0], rows[0].shape[0]), 1)
    total = jnp.zeros(out.shape, jnp.float32)
    for step, ref in enumerate(rows):
        hot = (columns == index[:, step : step + 1]).astype(jnp.bfloat16)
        total = total + jnp.dot(hot, ref[...], preferred_element_type=jnp.float32)
    out[...] = total.astype(out.dtype)


def cache_out(latent_cache):
    ep_size = lax.axis_size("ep")
    slots, block_size, latent = latent_cache.shape
    share = slots // lax.axis_size("tp")
    mine = lax.dynamic_slice_in_dim(latent_cache, lax.axis_index("tp") * share, share, axis=0)
    return mine.reshape(share, ep_size, block_size * latent // ep_size).transpose(1, 0, 2)


def cache_turn(spread, block_source, slots):
    ep_size = lax.axis_size("ep")
    tp_size = lax.axis_size("tp")
    tp_index = lax.axis_index("tp")
    share, piece = spread.shape[1:]
    wanted = lax.dynamic_slice_in_dim(
        block_source.reshape(ep_size, tp_size, share), tp_index, 1, axis=1
    ).reshape(-1)
    place = (wanted // slots) * share + wanted % share
    holder = (wanted % slots) // share
    from_step = (tp_index + tp_size - holder) % tp_size
    index = jnp.where(
        from_step[:, None] == jnp.arange(tp_size, dtype=jnp.int32)[None, :], place[:, None], -1
    )
    rows = [part.reshape(-1, piece) for part in [spread] + swap_tp(spread)]
    shape = jax.ShapeDtypeStruct(rows[0].shape, rows[0].dtype)
    ordered = kernel_call(
        order_kernel,
        shape,
        [index] + rows,
        flops=2 * tp_size * rows[0].size * rows[0].shape[0],
        spare=6 << 20,
    )
    return ordered.reshape(ep_size, share, piece)


def cache_in(ordered, block_size, latent):
    share, piece = ordered.shape[1:]
    arrived = lax.all_to_all(ordered, "ep", split_axis=0, concat_axis=0, tiled=True)
    if piece != latent:
        arrived = arrived.transpose(1, 0, 2).reshape(share, block_size, latent).transpose(1, 0, 2)
    return arrived


def attention_kernel(heads, chunk, owner, queries, *refs):
    keys, out = refs[:-1], refs[-1]
    for start in range(0, queries.shape[0], chunk):
        row = lax.broadcasted_iota(jnp.int32, (chunk, keys[0].shape[0]), 0) + start
        if heads & (heads - 1):
            row = row // heads
        else:
            row = row >> (heads.bit_length() - 1)
        scores = []
        for step, key in enumerate(keys):
            part = lax.dot_general(
                queries[start : start + chunk],
                key[...],
                (((1,), (1,)), ((), ())),
                preferred_element_type=jnp.float32,
            )
            scores.append(
                jnp.where(row == owner[step : step + 1, :], part * score_scale, -jnp.inf)
            )
        row_max = scores[0].max(axis=1, keepdims=True)
        for part in scores[1:]:
            row_max = jnp.maximum(row_max, part.max(axis=1, keepdims=True))
        terms = [jnp.exp(part - row_max) for part in scores]
        total = 1.0 / sum(term.sum(axis=1, keepdims=True) for term in terms)
        attended = jnp.zeros((chunk, KV), jnp.float32)
        for term, key in zip(terms, keys):
            attended = attended + jnp.dot(
                (term * total).astype(jnp.bfloat16),
                key[:, :KV],
                preferred_element_type=jnp.float32,
            )
        out[start : start + chunk] = attended.astype(out.dtype)


def attend(queries, keys, block_request, block_used):
    tp_size = lax.axis_size("tp")
    row_count, heads, latent = queries.shape
    block_size, share = keys[0].shape[:2]
    within = jnp.arange(block_size, dtype=jnp.int32)[:, None]
    owners = []
    for step in range(tp_size):
        first = ((lax.axis_index("tp") + tp_size - step) % tp_size) * share
        owner = lax.dynamic_slice_in_dim(block_request, first, share)[None, :]
        limit = lax.dynamic_slice_in_dim(block_used, first, share)[None, :]
        owners.append(jnp.where(within < limit, owner, -1).reshape(1, -1))
    keys = [part.reshape(-1, latent) for part in keys]
    rows = queries.reshape(-1, latent)
    shape = jax.ShapeDtypeStruct((rows.shape[0], KV), jnp.bfloat16)
    result = kernel_call(
        functools.partial(attention_kernel, heads, min(256, rows.shape[0])),
        shape,
        [jnp.concatenate(owners, axis=0), rows] + keys,
        flops=4 * rows.size * keys[0].shape[0] * tp_size,
        spare=8 << 20,
    )
    return result.reshape(row_count, heads, KV)


def body(
    tokens,
    expert_ids,
    gate_weights,
    expert_gate_up,
    expert_down,
    queries,
    latent_cache,
    block_source,
    block_request,
    block_used,
):
    row_count, top_count = expert_ids.shape
    slot_total, block_size, latent = latent_cache.shape
    ep_size = lax.axis_size("ep")
    tp_size = lax.axis_size("tp")
    tp_index = lax.axis_index("tp")
    bits = ep_bits()
    orders = (bits, bits[:-2] + [bits[-1], bits[-2]])
    parts = len(orders)
    cut = tokens.shape[1] // parts

    expert_range = jnp.arange(ep_size, dtype=jnp.int32)
    dense_gate = jnp.sum(
        jnp.where(
            expert_ids[:, :, None] == expert_range[None, None, :], gate_weights[:, :, None], 0.0
        ),
        axis=1,
    )
    gate_parts = jnp.concatenate(three_parts(dense_gate), axis=1)
    pad = -gate_parts.shape[1] % 128
    gates = jnp.pad(gate_parts, ((0, 0), (0, pad)))
    ends = tuple(cut * part for part in range(1, parts)) + (tokens.shape[1] + gates.shape[1],)
    held = {}

    def beside_shared(sent):
        pieces = tie(cache_out(latent_cache), sent)
        held["spread"] = lax.all_to_all(pieces, "ep", split_axis=0, concat_axis=0, tiled=True)

    def ahead_of_last(sent):
        sent, held["spread"] = lax.optimization_barrier((sent, held["spread"]))
        return sent

    halves = gather_rows(tokens, gates, orders, ends, beside_shared, ahead_of_last)
    last_sent = halves[-1][0]
    ordered = cache_turn(held["spread"], tie(block_source, last_sent), slot_total)
    first_late, ordered = lax.optimization_barrier((halves[0][1], ordered))
    halves[0] = (halves[0][0], first_late)
    places = [places_of(order) for order in orders]
    to_first = [[places[0].index(place) for place in own] for own in places]
    from_first = [[own.index(place) for place in places[0]] for own in places]

    passed = [tie(early, last_sent) for early, _ in halves[:-1]]
    passed.append(tie(last_sent, halves[0][1]))
    arrived = [
        [(pass_tp(early, step), pass_tp(late, step)) for early, (_, late) in zip(passed, halves)]
        for step in range(1, tp_size)
    ]
    all_rows = join_rows(
        [halves] + arrived, to_first, tuple(cut * part for part in range(1, parts + 1)), row_count
    )
    gate_halves = [half[..., cut : cut + 3 * ep_size] for half in halves[-1]]
    all_gate = jnp.concatenate(gate_halves, axis=0)
    all_gate = jnp.stack([all_gate[block] for block in from_first[-1]]).astype(jnp.float32)
    mine = (jnp.arange(3 * ep_size, dtype=jnp.int32) % ep_size) == lax.axis_index("ep")
    my_gate = jnp.sum(jnp.where(mine, all_gate, 0.0), axis=2).reshape(-1)
    gate_and_up = jnp.einsum(
        "sd,dgf->sgf", all_rows, expert_gate_up[0], preferred_element_type=jnp.float32
    )
    hidden = (
        jax.nn.silu(gate_and_up[:, 0]) * gate_and_up[:, 1] * my_gate[:, None]
    ).astype(jnp.bfloat16)

    down_weight = pltpu.with_memory_space_constraint(expert_down[0], pltpu.HBM)
    terms = [[] for _ in range(parts)]
    for step in range(1, tp_size):
        others = down_group(hidden, down_weight, step, from_first, row_count)
        for part in range(parts):
            terms[part].append(pass_tp(others[part], step))
    own = down_group(hidden, down_weight, 0, from_first, row_count)
    terms = [[own[part]] + terms[part] for part in range(parts)]
    sents, kepts = add_halves(terms, True), add_halves(terms, False)

    def beside_first_sum(sent):
        held["keys"] = cache_in(tie(ordered, sent), block_size, latent)
        return sent

    def beside_third_sum(sent):
        sent, near = lax.optimization_barrier((sent, held["keys"]))
        held["keys"] = [near] + swap_tp(near)
        return sent

    def beside_last_sum(sent):
        sent, keys = lax.optimization_barrier((sent, held["keys"]))
        held["attended"] = attend(queries, keys, block_request, block_used)
        return sent

    def ahead_of_end(arrived):
        arrived, held["attended"] = lax.optimization_barrier((arrived, held["attended"]))
        return arrived

    hooks = {
        0: beside_first_sum,
        2: beside_third_sum,
        len(bits) - 1: beside_last_sum,
        -1: ahead_of_end,
    }
    return (scatter_sums(kepts, sents, orders, hooks), held["attended"])


def solution(mesh):
    placed = (
        P("ep", "tp"),
        P("ep", None),
        P("ep", None),
        P("ep", None, None, "tp"),
        P("ep", None, "tp"),
        P("ep", "tp", None),
        P("ep", None, None),
        P(),
        P("ep"),
        P("ep"),
    )
    return jax.shard_map(
        body,
        mesh=mesh,
        in_specs=placed,
        out_specs=(P("ep", "tp"), P("ep", "tp", None)),
        check_vma=False,
    )
```

```python
import functools

import jax
import jax.numpy as jnp
from jax import lax
from jax.experimental import pallas as pl
from jax.experimental.pallas import tpu as pltpu
from jax.sharding import PartitionSpec as P

KV = 512


score_scale = 192.0 ** (-0.5)

WHOLE = pl.BlockSpec(memory_space=pltpu.VMEM)


def kernel_call(kernel, out_shape, arguments, flops, spare, in_specs=None, scratch_shapes=()):
    held = sum(array.size * array.dtype.itemsize for array in jax.tree.leaves(out_shape))
    for array, spec in zip(arguments, in_specs or [WHOLE] * len(arguments)):
        held += array.size * array.dtype.itemsize if spec is WHOLE else 0
    moved = sum(array.size * array.dtype.itemsize for array in arguments)
    return pl.pallas_call(
        kernel,
        out_shape=out_shape,
        in_specs=in_specs or [WHOLE] * len(arguments),
        out_specs=jax.tree.map(lambda _: WHOLE, out_shape),
        scratch_shapes=scratch_shapes,
        compiler_params=pltpu.CompilerParams(vmem_limit_bytes=held + spare),
        cost_estimate=pl.CostEstimate(
            flops=flops, bytes_accessed=moved + held, transcendentals=0
        ),
    )(*arguments)


def tie(values, others):
    return lax.optimization_barrier((values, others))[0]


def ep_bits():
    ep_size = lax.axis_size("ep")
    return [1 << place for place in reversed(range(ep_size.bit_length() - 1))]


def exchange(value, bit):
    ep_size = lax.axis_size("ep")
    return lax.ppermute(value, "ep", [(index, index ^ bit) for index in range(ep_size)])


def pass_tp(value, step):
    tp_size = lax.axis_size("tp")
    return lax.ppermute(
        value, "tp", [(index, (index + step) % tp_size) for index in range(tp_size)]
    )


def swap_tp(value):
    return [pass_tp(value, step) for step in range(1, lax.axis_size("tp"))]


def gather_rows(rows, others, orders, ends, beside, ahead):
    shared = orders[0][:-2]
    values = [
        jnp.concatenate([value[None], exchange(value[None], shared[0])], axis=0)
        for value in (rows, others)
    ]
    value = jnp.concatenate(values, axis=2)
    for bit in shared[1:]:
        if bit == shared[-1]:
            beside(value)
        value = jnp.concatenate([value, exchange(value, bit)], axis=0)
    halves = []
    for order, start, end in zip(orders, (0,) + ends, ends):
        part = value[:, :, start:end]
        part = jnp.concatenate([part, exchange(part, order[-2])], axis=0)
        if end == ends[-1]:
            part = ahead(part)
        halves.append((part, exchange(part, order[-1])))
    return halves


def places_of(order):
    places = [0]
    for bit in order:
        places = places + [place ^ bit for place in places]
    return places


def join_kernel(spots, ends, count, tp_size, *refs):
    out = refs[-1]
    parts = len(spots)
    rows = out.shape[0] // len(spots[0])
    width = out.shape[1] // tp_size
    index = lax.axis_index("tp")

    def place(tp_index):
        for step in range(tp_size):
            owner = (tp_index - step) % tp_size
            for part in range(parts):
                start, end = ((0,) + ends)[part], ends[part]
                for half in range(2):
                    ref = refs[(step * parts + part) * 2 + half]
                    blocks = ref.shape[0] // rows
                    for block in range(blocks):
                        spot = spots[part][half * blocks + block] * rows
                        out[spot : spot + rows, owner * width + start : owner * width + end] = ref[
                            block * rows : (block + 1) * rows, : end - start
                        ]

    for tp_index in range(tp_size):
        pl.when(index == tp_index)(functools.partial(place, tp_index))


def join_rows(by_step, spots, ends, rows):
    tp_size = len(by_step)
    arrays = [
        half.reshape(-1, half.shape[-1]) for parts in by_step for pair in parts for half in pair
    ]
    shape = jax.ShapeDtypeStruct((len(spots[0]) * rows, ends[-1] * tp_size), jnp.bfloat16)
    return kernel_call(
        functools.partial(join_kernel, spots, ends, len(arrays), tp_size),
        shape,
        arrays,
        flops=0,
        spare=4 << 20,
    )


def scatter_sums(kepts, sents, orders, hooks):
    steps = len(orders[0])
    sents = list(sents)
    for step in range(steps):
        if step in hooks:
            sents[-1] = hooks[step](sents[-1])
        terms = [
            [kept, exchange(sent, order[steps - 1 - step])]
            for kept, sent, order in zip(kepts, sents, orders)
        ]
        if step == steps - 1:
            break
        half = kepts[0].shape[0] // 2
        sents = [add_up([term[half:] for term in pair]) for pair in terms]
        kepts = [add_up([term[:half] for term in pair]) for pair in terms]
        if step == 1:
            sents = [jnp.concatenate(sents, axis=1)]
            kepts = [jnp.concatenate(kepts, axis=1)]
    kept, arrived = terms[0]
    return add_up([kept, hooks[-1](arrived)])


def add_up(terms):
    total = terms[0].astype(jnp.float32)
    for term in terms[1:]:
        total = total + term.astype(jnp.float32)
    return total.astype(jnp.bfloat16)


def three_parts(value):
    parts = []
    for _ in range(3):
        part = lax.reduce_precision(value, 8, 7)
        parts.append(part.astype(jnp.bfloat16))
        value = value - part
    return parts


def turn_rows(hidden, turned, spots, rows):
    for block, spot in enumerate(spots):
        turned[spot * rows : (spot + 1) * rows] = hidden[block * rows : (block + 1) * rows]


def down_product(turned, weight, row, chunk, column, width):
    return lax.dot_general(
        turned[row : row + chunk],
        weight[column : column + width],
        (((1,), (1,)), ((), ())),
        preferred_element_type=jnp.float32,
    )


def group_kernel(step, chosen, spots, tp_size, cut, rows, hidden, weight, *refs):
    outs, (held, turned, arrived) = refs[: len(chosen)], refs[len(chosen) :]
    target = lax.rem(lax.axis_index("tp") + step, tp_size)
    copies = []
    for index, part in enumerate(chosen):
        start = pl.multiple_of((target * len(spots) + part) * cut, cut)
        copies.append(
            pltpu.make_async_copy(
                weight.at[pl.ds(start, cut)], held.at[index], arrived.at[index]
            )
        )
    for copy in copies:
        copy.start()
    chunk = min(256, hidden.shape[0])
    for index, part in enumerate(chosen):
        turn_rows(hidden, turned.at[index], spots[part], rows)
        copies[index].wait()
        for row in range(0, hidden.shape[0], chunk):
            outs[index][row : row + chunk] = down_product(
                turned.at[index], held.at[index], row, chunk, 0, cut
            ).astype(jnp.bfloat16)


def down_group(hidden, weight, step, chosen, spots, rows):
    count = len(chosen)
    tp_size = lax.axis_size("tp")
    cut = weight.shape[0] // tp_size // len(spots)
    shape = jax.ShapeDtypeStruct((hidden.shape[0], cut), jnp.bfloat16)
    return kernel_call(
        functools.partial(group_kernel, step, chosen, spots, tp_size, cut, rows),
        [shape] * count,
        [hidden, weight],
        flops=2 * hidden.size * cut * count,
        spare=count * cut * weight.shape[1] * 2 + (8 << 20),
        in_specs=[WHOLE, pl.BlockSpec(memory_space=pl.ANY)],
        scratch_shapes=[
            pltpu.VMEM((count, cut, weight.shape[1]), weight.dtype),
            pltpu.VMEM((count,) + hidden.shape, hidden.dtype),
            pltpu.SemaphoreType.DMA((count,)),
        ],
    )


def own_kernel(part, parts, spots, cut, rows, count, hidden, weight, *refs):
    others, (kept, sent, held, turned, passed, arrived) = refs[:count], refs[count:]
    start = pl.multiple_of((lax.axis_index("tp") * parts + part) * cut, cut)
    copies = [pltpu.make_async_copy(weight.at[pl.ds(start, cut)], held, arrived.at[count])]
    for index, other in enumerate(others):
        copies.append(pltpu.make_async_copy(other, passed.at[index], arrived.at[index]))
    for copy in copies:
        copy.start()
    turn_rows(hidden, turned, spots, rows)
    for copy in copies:
        copy.wait()
    half = hidden.shape[0] // 2
    chunk = min(256, hidden.shape[0])
    width = cut // 2 if cut % 256 == 0 else cut
    for column in range(0, cut, width):
        for row in range(0, hidden.shape[0], chunk):
            total = down_product(turned, held, row, chunk, column, width)
            for index in range(count):
                total = total + passed[
                    index, row : row + chunk, column : column + width
                ].astype(jnp.float32)
            total = total.astype(jnp.bfloat16)
            for first in range(row, row + chunk, min(chunk, half)):
                out = kept if first < half else sent
                place = first % half
                piece = total[first - row : first - row + min(chunk, half)]
                out[place : place + piece.shape[0], column : column + width] = piece


def down_own(hidden, weight, part, parts, spots, rows, others):
    cut = weight.shape[0] // lax.axis_size("tp") // parts
    shape = jax.ShapeDtypeStruct((hidden.shape[0] // 2, cut), jnp.bfloat16)
    anywhere = pl.BlockSpec(memory_space=pl.ANY)
    return kernel_call(
        functools.partial(own_kernel, part, parts, spots, cut, rows, len(others)),
        [shape, shape],
        [hidden, weight] + others,
        flops=2 * hidden.size * cut,
        spare=(cut * weight.shape[1] + hidden.shape[0] * cut * len(others)) * 2 + (8 << 20),
        in_specs=[WHOLE] + [anywhere] * (1 + len(others)),
        scratch_shapes=[
            pltpu.VMEM((cut, weight.shape[1]), weight.dtype),
            pltpu.VMEM(hidden.shape, hidden.dtype),
            pltpu.VMEM((len(others), hidden.shape[0], cut), jnp.bfloat16),
            pltpu.SemaphoreType.DMA((1 + len(others),)),
        ],
    )


def halves_kernel(parts, first, *refs):
    outs, (held, arrived) = refs[-2 - parts : -2], refs[-2:]
    terms = refs[: -2 - parts]
    count = len(terms) // parts
    half, rows = outs[0].shape[0], 16
    copies = [
        pltpu.make_async_copy(term.at[pl.ds(first, half)], held.at[index], arrived.at[index])
        for index, term in enumerate(terms)
    ]
    for copy in copies:
        copy.start()
    for part in range(parts):
        for index in range(part * count, (part + 1) * count):
            copies[index].wait()
        for row in range(0, half, rows):
            total = held[part * count, row : row + rows].astype(jnp.float32)
            for index in range(part * count + 1, (part + 1) * count):
                total = total + held[index, row : row + rows].astype(jnp.float32)
            outs[part][row : row + rows] = total.astype(jnp.bfloat16)


def add_halves(terms, second):
    parts = len(terms)
    flat = [term for part in terms for term in part]
    half, cut = flat[0].shape[0] // 2, flat[0].shape[1]
    return kernel_call(
        functools.partial(halves_kernel, parts, half if second else 0),
        [jax.ShapeDtypeStruct((half, cut), jnp.bfloat16)] * parts,
        flat,
        flops=half * cut * len(flat),
        spare=half * cut * len(flat) * 2 + (2 << 20),
        in_specs=[pl.BlockSpec(memory_space=pl.ANY)] * len(flat),
        scratch_shapes=[
            pltpu.VMEM((len(flat), half, cut), jnp.bfloat16),
            pltpu.SemaphoreType.DMA((len(flat),)),
        ],
    )


def order_kernel(index, *refs):
    rows, out = refs[:-1], refs[-1]
    columns = lax.broadcasted_iota(jnp.int32, (out.shape[0], rows[0].shape[0]), 1)
    total = jnp.zeros(out.shape, jnp.float32)
    for step, ref in enumerate(rows):
        hot = (columns == index[:, step : step + 1]).astype(jnp.bfloat16)
        total = total + jnp.dot(hot, ref[...], preferred_element_type=jnp.float32)
    out[...] = total.astype(out.dtype)


def cache_out(latent_cache):
    ep_size = lax.axis_size("ep")
    slots, block_size, latent = latent_cache.shape
    share = slots // lax.axis_size("tp")
    mine = lax.dynamic_slice_in_dim(latent_cache, lax.axis_index("tp") * share, share, axis=0)
    return mine.reshape(share, ep_size, block_size * latent // ep_size).transpose(1, 0, 2)


def cache_turn(spread, block_source, slots):
    ep_size = lax.axis_size("ep")
    tp_size = lax.axis_size("tp")
    tp_index = lax.axis_index("tp")
    share, piece = spread.shape[1:]
    wanted = lax.dynamic_slice_in_dim(
        block_source.reshape(ep_size, tp_size, share), tp_index, 1, axis=1
    ).reshape(-1)
    place = (wanted // slots) * share + wanted % share
    holder = (wanted % slots) // share
    from_step = (tp_index + tp_size - holder) % tp_size
    index = jnp.where(
        from_step[:, None] == jnp.arange(tp_size, dtype=jnp.int32)[None, :], place[:, None], -1
    )
    rows = [part.reshape(-1, piece) for part in [spread] + swap_tp(spread)]
    shape = jax.ShapeDtypeStruct(rows[0].shape, rows[0].dtype)
    ordered = kernel_call(
        order_kernel,
        shape,
        [index] + rows,
        flops=2 * tp_size * rows[0].size * rows[0].shape[0],
        spare=6 << 20,
    )
    return ordered.reshape(ep_size, share, piece)


def cache_in(ordered, block_size, latent):
    share, piece = ordered.shape[1:]
    arrived = lax.all_to_all(ordered, "ep", split_axis=0, concat_axis=0, tiled=True)
    if piece != latent:
        arrived = arrived.transpose(1, 0, 2).reshape(share, block_size, latent).transpose(1, 0, 2)
    return arrived


def attention_kernel(heads, chunk, owner, queries, *refs):
    keys, out = refs[:-1], refs[-1]
    for start in range(0, queries.shape[0], chunk):
        row = lax.broadcasted_iota(jnp.int32, (chunk, keys[0].shape[0]), 0) + start
        if heads & (heads - 1):
            row = row // heads
        else:
            row = row >> (heads.bit_length() - 1)
        scores = []
        for step, key in enumerate(keys):
            part = lax.dot_general(
                queries[start : start + chunk],
                key[...],
                (((1,), (1,)), ((), ())),
                preferred_element_type=jnp.float32,
            )
            scores.append(
                jnp.where(row == owner[step : step + 1, :], part * score_scale, -jnp.inf)
            )
        row_max = scores[0].max(axis=1, keepdims=True)
        for part in scores[1:]:
            row_max = jnp.maximum(row_max, part.max(axis=1, keepdims=True))
        terms = [jnp.exp(part - row_max) for part in scores]
        total = 1.0 / sum(term.sum(axis=1, keepdims=True) for term in terms)
        attended = jnp.zeros((chunk, KV), jnp.float32)
        for term, key in zip(terms, keys):
            attended = attended + jnp.dot(
                (term * total).astype(jnp.bfloat16),
                key[:, :KV],
                preferred_element_type=jnp.float32,
            )
        out[start : start + chunk] = attended.astype(out.dtype)


def token_owners(block_request, block_used, block_size):
    tp_size = lax.axis_size("tp")
    share = block_request.shape[0] // tp_size
    within = jnp.arange(block_size, dtype=jnp.int32)[:, None]
    owners = []
    for step in range(tp_size):
        first = ((lax.axis_index("tp") + tp_size - step) % tp_size) * share
        owner = lax.dynamic_slice_in_dim(block_request, first, share)[None, :]
        limit = lax.dynamic_slice_in_dim(block_used, first, share)[None, :]
        owners.append(jnp.where(within < limit, owner, -1).reshape(1, -1))
    return jnp.concatenate(owners, axis=0)


def attend(queries, keys, owners):
    row_count, heads, latent = queries.shape
    keys = [part.reshape(-1, latent) for part in keys]
    rows = queries.reshape(-1, latent)
    shape = jax.ShapeDtypeStruct((rows.shape[0], KV), jnp.bfloat16)
    result = kernel_call(
        functools.partial(attention_kernel, heads, min(256, rows.shape[0])),
        shape,
        [owners, rows] + keys,
        flops=4 * rows.size * keys[0].shape[0] * len(keys),
        spare=8 << 20,
    )
    return result.reshape(row_count, heads, KV)


def body(
    tokens,
    expert_ids,
    gate_weights,
    expert_gate_up,
    expert_down,
    queries,
    latent_cache,
    block_source,
    block_request,
    block_used,
):
    row_count, top_count = expert_ids.shape
    slot_total, block_size, latent = latent_cache.shape
    ep_size = lax.axis_size("ep")
    tp_size = lax.axis_size("tp")
    tp_index = lax.axis_index("tp")
    bits = ep_bits()
    orders = (bits, bits[:-2] + [bits[-1], bits[-2]])
    parts = len(orders)
    cut = tokens.shape[1] // parts

    expert_range = jnp.arange(ep_size, dtype=jnp.int32)
    dense_gate = jnp.sum(
        jnp.where(
            expert_ids[:, :, None] == expert_range[None, None, :], gate_weights[:, :, None], 0.0
        ),
        axis=1,
    )
    gate_parts = jnp.concatenate(three_parts(dense_gate), axis=1)
    pad = -gate_parts.shape[1] % 128
    gates = jnp.pad(gate_parts, ((0, 0), (0, pad)))
    ends = tuple(cut * part for part in range(1, parts)) + (tokens.shape[1] + gates.shape[1],)
    held = {}

    def beside_shared(sent):
        pieces = tie(cache_out(latent_cache), sent)
        held["spread"] = lax.all_to_all(pieces, "ep", split_axis=0, concat_axis=0, tiled=True)

    def ahead_of_last(sent):
        sent, held["spread"] = lax.optimization_barrier((sent, held["spread"]))
        return sent

    halves = gather_rows(tokens, gates, orders, ends, beside_shared, ahead_of_last)
    last_sent = halves[-1][0]
    ordered = cache_turn(held["spread"], tie(block_source, last_sent), slot_total)
    owners = token_owners(block_request, block_used, block_size)
    first_late, ordered, owners = lax.optimization_barrier((halves[0][1], ordered, owners))
    halves[0] = (halves[0][0], first_late)
    places = [places_of(order) for order in orders]
    to_first = [[places[0].index(place) for place in own] for own in places]
    from_first = [[own.index(place) for place in places[0]] for own in places]

    passed = [tie(early, last_sent) for early, _ in halves[:-1]]
    passed.append(tie(last_sent, halves[0][1]))
    arrived = [
        [(pass_tp(early, step), pass_tp(late, step)) for early, (_, late) in zip(passed, halves)]
        for step in range(1, tp_size)
    ]
    all_rows = join_rows(
        [halves] + arrived, to_first, tuple(cut * part for part in range(1, parts + 1)), row_count
    )
    gate_halves = [half[..., cut : cut + 3 * ep_size] for half in halves[-1]]
    all_gate = jnp.concatenate(gate_halves, axis=0)
    all_gate = jnp.stack([all_gate[block] for block in from_first[-1]]).astype(jnp.float32)
    mine = (jnp.arange(3 * ep_size, dtype=jnp.int32) % ep_size) == lax.axis_index("ep")
    my_gate = jnp.sum(jnp.where(mine, all_gate, 0.0), axis=2).reshape(-1)
    gate_and_up = jnp.einsum(
        "sd,dgf->sgf", all_rows, expert_gate_up[0], preferred_element_type=jnp.float32
    )
    hidden = (
        jax.nn.silu(gate_and_up[:, 0]) * gate_and_up[:, 1] * my_gate[:, None]
    ).astype(jnp.bfloat16)

    down_weight = pltpu.with_memory_space_constraint(expert_down[0], pltpu.HBM)
    passed = [[] for _ in range(parts)]
    for step in range(1, tp_size):
        others = down_group(hidden, down_weight, step, range(parts), from_first, row_count)
        for part in range(parts):
            passed[part].append(pass_tp(others[part], step))
    later = down_group(hidden, down_weight, 0, range(1, parts), from_first, row_count)
    later = [[own] + others for own, others in zip(later, passed[1:])]
    kept, sent = down_own(hidden, down_weight, 0, parts, from_first[0], row_count, passed[0])
    sents = [sent, *add_halves(later, True)]
    kepts = [kept, *add_halves(later, False)]

    def beside_first_sum(sent):
        held["keys"] = cache_in(tie(ordered, sent), block_size, latent)
        return sent

    def beside_third_sum(sent):
        sent, near = lax.optimization_barrier((sent, held["keys"]))
        held["keys"] = [near] + swap_tp(near)
        return sent

    def beside_last_sum(sent):
        sent, keys = lax.optimization_barrier((sent, held["keys"]))
        held["attended"] = attend(queries, keys, owners)
        return sent

    def ahead_of_end(arrived):
        arrived, held["attended"] = lax.optimization_barrier((arrived, held["attended"]))
        return arrived

    hooks = {
        0: beside_first_sum,
        2: beside_third_sum,
        len(bits) - 1: beside_last_sum,
        -1: ahead_of_end,
    }
    return (scatter_sums(kepts, sents, orders, hooks), held["attended"])


def solution(mesh):
    placed = (
        P("ep", "tp"),
        P("ep", None),
        P("ep", None),
        P("ep", None, None, "tp"),
        P("ep", None, "tp"),
        P("ep", "tp", None),
        P("ep", None, None),
        P(),
        P("ep"),
        P("ep"),
    )
    return jax.shard_map(
        body,
        mesh=mesh,
        in_specs=placed,
        out_specs=(P("ep", "tp"), P("ep", "tp", None)),
        check_vma=False,
    )
```

```python
import functools

import jax
import jax.numpy as jnp
from jax import lax
from jax.experimental import pallas as pl
from jax.experimental.pallas import tpu as pltpu
from jax.sharding import PartitionSpec as P

KV = 512


score_scale = 192.0 ** (-0.5)

WHOLE = pl.BlockSpec(memory_space=pltpu.VMEM)


def kernel_call(
    kernel, out_shape, arguments, flops, spare, in_specs=None, scratch_shapes=(), counted=True
):
    held = sum(array.size * array.dtype.itemsize for array in jax.tree.leaves(out_shape))
    for array, spec in zip(arguments, in_specs or [WHOLE] * len(arguments)):
        held += array.size * array.dtype.itemsize if spec is WHOLE else 0
    moved = sum(array.size * array.dtype.itemsize for array in arguments)
    return pl.pallas_call(
        kernel,
        out_shape=out_shape,
        in_specs=in_specs or [WHOLE] * len(arguments),
        out_specs=jax.tree.map(lambda _: WHOLE, out_shape),
        scratch_shapes=scratch_shapes,
        compiler_params=pltpu.CompilerParams(vmem_limit_bytes=held + spare),
        cost_estimate=pl.CostEstimate(
            flops=flops, bytes_accessed=(moved + held) * counted, transcendentals=0
        ),
    )(*arguments)


def tie(values, others):
    return lax.optimization_barrier((values, others))[0]


def ep_bits():
    ep_size = lax.axis_size("ep")
    return [1 << place for place in reversed(range(ep_size.bit_length() - 1))]


def exchange(value, bit):
    ep_size = lax.axis_size("ep")
    return lax.ppermute(value, "ep", [(index, index ^ bit) for index in range(ep_size)])


def pass_tp(value, step):
    tp_size = lax.axis_size("tp")
    return lax.ppermute(
        value, "tp", [(index, (index + step) % tp_size) for index in range(tp_size)]
    )


def swap_tp(value):
    return [pass_tp(value, step) for step in range(1, lax.axis_size("tp"))]


def gather_rows(rows, others, orders, ends, beside, ahead):
    shared = orders[0][:-2]
    values = [
        jnp.concatenate([value[None], exchange(value[None], shared[0])], axis=0)
        for value in (rows, others)
    ]
    value = jnp.concatenate(values, axis=2)
    for bit in shared[1:]:
        if bit == shared[-1]:
            beside(value)
        value = jnp.concatenate([value, exchange(value, bit)], axis=0)
    halves = []
    for order, start, end in zip(orders, (0,) + ends, ends):
        part = value[:, :, start:end]
        part = jnp.concatenate([part, exchange(part, order[-2])], axis=0)
        if end == ends[-1]:
            part = ahead(part)
        halves.append((part, exchange(part, order[-1])))
    return halves


def places_of(order):
    places = [0]
    for bit in order:
        places = places + [place ^ bit for place in places]
    return places


def join_kernel(spots, ends, count, tp_size, *refs):
    out = refs[-1]
    parts = len(spots)
    rows = out.shape[0] // len(spots[0])
    width = out.shape[1] // tp_size
    index = lax.axis_index("tp")

    def place(tp_index):
        for step in range(tp_size):
            owner = (tp_index - step) % tp_size
            for part in range(parts):
                start, end = ((0,) + ends)[part], ends[part]
                for half in range(2):
                    ref = refs[(step * parts + part) * 2 + half]
                    blocks = ref.shape[0] // rows
                    for block in range(blocks):
                        spot = spots[part][half * blocks + block] * rows
                        out[spot : spot + rows, owner * width + start : owner * width + end] = ref[
                            block * rows : (block + 1) * rows, : end - start
                        ]

    for tp_index in range(tp_size):
        pl.when(index == tp_index)(functools.partial(place, tp_index))


def join_rows(by_step, spots, ends, rows):
    tp_size = len(by_step)
    arrays = [
        half.reshape(-1, half.shape[-1]) for parts in by_step for pair in parts for half in pair
    ]
    shape = jax.ShapeDtypeStruct((len(spots[0]) * rows, ends[-1] * tp_size), jnp.bfloat16)
    return kernel_call(
        functools.partial(join_kernel, spots, ends, len(arrays), tp_size),
        shape,
        arrays,
        flops=0,
        spare=4 << 20,
        counted=False,
    )


def scatter_sums(kepts, sents, orders, hooks):
    steps = len(orders[0])
    sents = list(sents)
    for step in range(steps):
        if step in hooks:
            sents[-1] = hooks[step](sents[-1])
        terms = [
            [kept, exchange(sent, order[steps - 1 - step])]
            for kept, sent, order in zip(kepts, sents, orders)
        ]
        if step == steps - 1:
            break
        half = kepts[0].shape[0] // 2
        sents = [add_up([term[half:] for term in pair]) for pair in terms]
        kepts = [add_up([term[:half] for term in pair]) for pair in terms]
        if step == 1:
            sents = [jnp.concatenate(sents, axis=1)]
            kepts = [jnp.concatenate(kepts, axis=1)]
    kept, arrived = terms[0]
    return add_up([kept, arrived])


def add_up(terms):
    total = terms[0].astype(jnp.float32)
    for term in terms[1:]:
        total = total + term.astype(jnp.float32)
    return total.astype(jnp.bfloat16)


def three_parts(value):
    parts = []
    for _ in range(3):
        part = lax.reduce_precision(value, 8, 7)
        parts.append(part.astype(jnp.bfloat16))
        value = value - part
    return parts


def turn_rows(hidden, turned, spots, rows):
    for block, spot in enumerate(spots):
        turned[spot * rows : (spot + 1) * rows] = hidden[block * rows : (block + 1) * rows]


def down_product(turned, weight, row, chunk, column, width):
    return lax.dot_general(
        turned[row : row + chunk],
        weight[column : column + width],
        (((1,), (1,)), ((), ())),
        preferred_element_type=jnp.float32,
    )


def group_kernel(step, chosen, spots, tp_size, cut, rows, hidden, weight, *refs):
    outs, (held, turned, arrived) = refs[: len(chosen)], refs[len(chosen) :]
    target = lax.rem(lax.axis_index("tp") + step, tp_size)
    copies = []
    for index, part in enumerate(chosen):
        start = pl.multiple_of((target * len(spots) + part) * cut, cut)
        copies.append(
            pltpu.make_async_copy(
                weight.at[pl.ds(start, cut)], held.at[index], arrived.at[index]
            )
        )
    for copy in copies:
        copy.start()
    chunk = min(256, hidden.shape[0])
    for index, part in enumerate(chosen):
        turn_rows(hidden, turned.at[index], spots[part], rows)
        copies[index].wait()
        for row in range(0, hidden.shape[0], chunk):
            outs[index][row : row + chunk] = down_product(
                turned.at[index], held.at[index], row, chunk, 0, cut
            ).astype(jnp.bfloat16)


def down_group(hidden, weight, step, chosen, spots, rows):
    count = len(chosen)
    tp_size = lax.axis_size("tp")
    cut = weight.shape[0] // tp_size // len(spots)
    shape = jax.ShapeDtypeStruct((hidden.shape[0], cut), jnp.bfloat16)
    return kernel_call(
        functools.partial(group_kernel, step, chosen, spots, tp_size, cut, rows),
        [shape] * count,
        [hidden, weight],
        flops=2 * hidden.size * cut * count,
        spare=count * cut * weight.shape[1] * 2 + (8 << 20),
        in_specs=[WHOLE, pl.BlockSpec(memory_space=pl.ANY)],
        scratch_shapes=[
            pltpu.VMEM((count, cut, weight.shape[1]), weight.dtype),
            pltpu.VMEM((count,) + hidden.shape, hidden.dtype),
            pltpu.SemaphoreType.DMA((count,)),
        ],
    )


def own_kernel(part, parts, spots, cut, rows, count, hidden, weight, *refs):
    others, (kept, sent, held, turned, passed, arrived) = refs[:count], refs[count:]
    start = pl.multiple_of((lax.axis_index("tp") * parts + part) * cut, cut)
    copies = [pltpu.make_async_copy(weight.at[pl.ds(start, cut)], held, arrived.at[count])]
    for index, other in enumerate(others):
        copies.append(pltpu.make_async_copy(other, passed.at[index], arrived.at[index]))
    for copy in copies:
        copy.start()
    turn_rows(hidden, turned, spots, rows)
    for copy in copies:
        copy.wait()
    half = hidden.shape[0] // 2
    chunk = min(256, hidden.shape[0])
    width = cut // 2 if cut % 256 == 0 else cut
    for column in range(0, cut, width):
        for row in range(0, hidden.shape[0], chunk):
            total = down_product(turned, held, row, chunk, column, width)
            for index in range(count):
                total = total + passed[
                    index, row : row + chunk, column : column + width
                ].astype(jnp.float32)
            total = total.astype(jnp.bfloat16)
            for first in range(row, row + chunk, min(chunk, half)):
                out = kept if first < half else sent
                place = first % half
                piece = total[first - row : first - row + min(chunk, half)]
                out[place : place + piece.shape[0], column : column + width] = piece


def down_own(hidden, weight, part, parts, spots, rows, others):
    cut = weight.shape[0] // lax.axis_size("tp") // parts
    shape = jax.ShapeDtypeStruct((hidden.shape[0] // 2, cut), jnp.bfloat16)
    anywhere = pl.BlockSpec(memory_space=pl.ANY)
    return kernel_call(
        functools.partial(own_kernel, part, parts, spots, cut, rows, len(others)),
        [shape, shape],
        [hidden, weight] + others,
        flops=2 * hidden.size * cut,
        spare=(cut * weight.shape[1] + hidden.shape[0] * cut * len(others)) * 2 + (8 << 20),
        in_specs=[WHOLE] + [anywhere] * (1 + len(others)),
        scratch_shapes=[
            pltpu.VMEM((cut, weight.shape[1]), weight.dtype),
            pltpu.VMEM(hidden.shape, hidden.dtype),
            pltpu.VMEM((len(others), hidden.shape[0], cut), jnp.bfloat16),
            pltpu.SemaphoreType.DMA((1 + len(others),)),
        ],
    )


def halves_kernel(parts, first, *refs):
    outs, (held, arrived) = refs[-2 - parts : -2], refs[-2:]
    terms = refs[: -2 - parts]
    count = len(terms) // parts
    half, rows = outs[0].shape[0], 16
    copies = [
        pltpu.make_async_copy(term.at[pl.ds(first, half)], held.at[index], arrived.at[index])
        for index, term in enumerate(terms)
    ]
    for copy in copies:
        copy.start()
    for part in range(parts):
        for index in range(part * count, (part + 1) * count):
            copies[index].wait()
        for row in range(0, half, rows):
            total = held[part * count, row : row + rows].astype(jnp.float32)
            for index in range(part * count + 1, (part + 1) * count):
                total = total + held[index, row : row + rows].astype(jnp.float32)
            outs[part][row : row + rows] = total.astype(jnp.bfloat16)


def add_halves(terms, second):
    parts = len(terms)
    flat = [term for part in terms for term in part]
    half, cut = flat[0].shape[0] // 2, flat[0].shape[1]
    return kernel_call(
        functools.partial(halves_kernel, parts, half if second else 0),
        [jax.ShapeDtypeStruct((half, cut), jnp.bfloat16)] * parts,
        flat,
        flops=half * cut * len(flat),
        spare=half * cut * len(flat) * 2 + (2 << 20),
        in_specs=[pl.BlockSpec(memory_space=pl.ANY)] * len(flat),
        scratch_shapes=[
            pltpu.VMEM((len(flat), half, cut), jnp.bfloat16),
            pltpu.SemaphoreType.DMA((len(flat),)),
        ],
    )


def order_kernel(index, *refs):
    rows, out = refs[:-1], refs[-1]
    columns = lax.broadcasted_iota(jnp.int32, (out.shape[0], rows[0].shape[0]), 1)
    total = jnp.zeros(out.shape, jnp.float32)
    for step, ref in enumerate(rows):
        hot = (columns == index[:, step : step + 1]).astype(jnp.bfloat16)
        total = total + jnp.dot(hot, ref[...], preferred_element_type=jnp.float32)
    out[...] = total.astype(out.dtype)


def cache_out(latent_cache):
    ep_size = lax.axis_size("ep")
    slots, block_size, latent = latent_cache.shape
    share = slots // lax.axis_size("tp")
    mine = lax.dynamic_slice_in_dim(latent_cache, lax.axis_index("tp") * share, share, axis=0)
    return mine.reshape(share, ep_size, block_size * latent // ep_size).transpose(1, 0, 2)


def cache_turn(spread, block_source, slots):
    ep_size = lax.axis_size("ep")
    tp_size = lax.axis_size("tp")
    tp_index = lax.axis_index("tp")
    share, piece = spread.shape[1:]
    wanted = lax.dynamic_slice_in_dim(
        block_source.reshape(ep_size, tp_size, share), tp_index, 1, axis=1
    ).reshape(-1)
    place = (wanted // slots) * share + wanted % share
    holder = (wanted % slots) // share
    from_step = (tp_index + tp_size - holder) % tp_size
    index = jnp.where(
        from_step[:, None] == jnp.arange(tp_size, dtype=jnp.int32)[None, :], place[:, None], -1
    )
    rows = [part.reshape(-1, piece) for part in [spread] + swap_tp(spread)]
    shape = jax.ShapeDtypeStruct(rows[0].shape, rows[0].dtype)
    ordered = kernel_call(
        order_kernel,
        shape,
        [index] + rows,
        flops=2 * tp_size * rows[0].size * rows[0].shape[0],
        spare=6 << 20,
    )
    return ordered.reshape(ep_size, share, piece)


def cache_in(ordered, block_size, latent):
    share, piece = ordered.shape[1:]
    arrived = lax.all_to_all(ordered, "ep", split_axis=0, concat_axis=0, tiled=True)
    if piece != latent:
        arrived = arrived.transpose(1, 0, 2).reshape(share, block_size, latent).transpose(1, 0, 2)
    return arrived


def attention_kernel(heads, chunk, owner, queries, *refs):
    keys, out = refs[:-1], refs[-1]
    for start in range(0, queries.shape[0], chunk):
        row = lax.broadcasted_iota(jnp.int32, (chunk, keys[0].shape[0]), 0) + start
        if heads & (heads - 1):
            row = row // heads
        else:
            row = row >> (heads.bit_length() - 1)
        scores = []
        for step, key in enumerate(keys):
            part = lax.dot_general(
                queries[start : start + chunk],
                key[...],
                (((1,), (1,)), ((), ())),
                preferred_element_type=jnp.float32,
            )
            scores.append(
                jnp.where(row == owner[step : step + 1, :], part * score_scale, -jnp.inf)
            )
        row_max = scores[0].max(axis=1, keepdims=True)
        for part in scores[1:]:
            row_max = jnp.maximum(row_max, part.max(axis=1, keepdims=True))
        terms = [jnp.exp(part - row_max) for part in scores]
        total = 1.0 / sum(term.sum(axis=1, keepdims=True) for term in terms)
        attended = jnp.zeros((chunk, KV), jnp.float32)
        for term, key in zip(terms, keys):
            attended = attended + jnp.dot(
                (term * total).astype(jnp.bfloat16),
                key[:, :KV],
                preferred_element_type=jnp.float32,
            )
        out[start : start + chunk] = attended.astype(out.dtype)


def token_owners(block_request, block_used, block_size):
    tp_size = lax.axis_size("tp")
    share = block_request.shape[0] // tp_size
    within = jnp.arange(block_size, dtype=jnp.int32)[:, None]
    owners = []
    for step in range(tp_size):
        first = ((lax.axis_index("tp") + tp_size - step) % tp_size) * share
        owner = lax.dynamic_slice_in_dim(block_request, first, share)[None, :]
        limit = lax.dynamic_slice_in_dim(block_used, first, share)[None, :]
        owners.append(jnp.where(within < limit, owner, -1).reshape(1, -1))
    return jnp.concatenate(owners, axis=0)


def attend(queries, keys, owners):
    row_count, heads, latent = queries.shape
    keys = [part.reshape(-1, latent) for part in keys]
    rows = queries.reshape(-1, latent)
    shape = jax.ShapeDtypeStruct((rows.shape[0], KV), jnp.bfloat16)
    result = kernel_call(
        functools.partial(attention_kernel, heads, min(256, rows.shape[0])),
        shape,
        [owners, rows] + keys,
        flops=4 * rows.size * keys[0].shape[0] * len(keys),
        spare=8 << 20,
    )
    return result.reshape(row_count, heads, KV)


def body(
    tokens,
    expert_ids,
    gate_weights,
    expert_gate_up,
    expert_down,
    queries,
    latent_cache,
    block_source,
    block_request,
    block_used,
):
    row_count, top_count = expert_ids.shape
    slot_total, block_size, latent = latent_cache.shape
    ep_size = lax.axis_size("ep")
    tp_size = lax.axis_size("tp")
    tp_index = lax.axis_index("tp")
    bits = ep_bits()
    orders = (bits, bits[:-2] + [bits[-1], bits[-2]])
    parts = len(orders)
    cut = tokens.shape[1] // parts

    expert_range = jnp.arange(ep_size, dtype=jnp.int32)
    dense_gate = jnp.sum(
        jnp.where(
            expert_ids[:, :, None] == expert_range[None, None, :], gate_weights[:, :, None], 0.0
        ),
        axis=1,
    )
    gate_parts = jnp.concatenate(three_parts(dense_gate), axis=1)
    pad = -gate_parts.shape[1] % 128
    gates = jnp.pad(gate_parts, ((0, 0), (0, pad)))
    ends = tuple(cut * part for part in range(1, parts)) + (tokens.shape[1] + gates.shape[1],)
    held = {}

    def beside_shared(sent):
        pieces = tie(cache_out(latent_cache), sent)
        held["spread"] = lax.all_to_all(pieces, "ep", split_axis=0, concat_axis=0, tiled=True)

    def ahead_of_last(sent):
        sent, held["spread"] = lax.optimization_barrier((sent, held["spread"]))
        return sent

    halves = gather_rows(tokens, gates, orders, ends, beside_shared, ahead_of_last)
    last_sent = halves[-1][0]
    ordered = cache_turn(held["spread"], tie(block_source, last_sent), slot_total)
    keys = cache_in(ordered, block_size, latent)
    owners = token_owners(block_request, block_used, block_size)
    first_late, ordered, owners = lax.optimization_barrier((halves[0][1], ordered, owners))
    halves[0] = (halves[0][0], first_late)
    places = [places_of(order) for order in orders]
    to_first = [[places[0].index(place) for place in own] for own in places]
    from_first = [[own.index(place) for place in places[0]] for own in places]

    passed = [tie(early, last_sent) for early, _ in halves[:-1]]
    passed.append(tie(last_sent, halves[0][1]))
    arrived = [
        [(pass_tp(early, step), pass_tp(late, step)) for early, (_, late) in zip(passed, halves)]
        for step in range(1, tp_size)
    ]
    all_rows = join_rows(
        [halves] + arrived, to_first, tuple(cut * part for part in range(1, parts + 1)), row_count
    )
    gate_halves = [half[..., cut : cut + 3 * ep_size] for half in halves[-1]]
    all_gate = jnp.concatenate(gate_halves, axis=0)
    all_gate = jnp.stack([all_gate[block] for block in from_first[-1]]).astype(jnp.float32)
    mine = (jnp.arange(3 * ep_size, dtype=jnp.int32) % ep_size) == lax.axis_index("ep")
    my_gate = jnp.sum(jnp.where(mine, all_gate, 0.0), axis=2).reshape(-1)
    gate_and_up = jnp.einsum(
        "sd,dgf->sgf", all_rows, expert_gate_up[0], preferred_element_type=jnp.float32
    )
    hidden = (
        jax.nn.silu(gate_and_up[:, 0]) * gate_and_up[:, 1] * my_gate[:, None]
    ).astype(jnp.bfloat16)

    hidden, keys = lax.optimization_barrier((hidden, keys))
    down_weight = pltpu.with_memory_space_constraint(expert_down[0], pltpu.HBM)
    passed = [[] for _ in range(parts)]
    for step in range(1, tp_size):
        others = down_group(hidden, down_weight, step, range(parts), from_first, row_count)
        for part in range(parts):
            passed[part].append(pass_tp(others[part], step))
    later = down_group(hidden, down_weight, 0, range(1, parts), from_first, row_count)
    later = [[own] + others for own, others in zip(later, passed[1:])]
    kept, sent = down_own(hidden, down_weight, 0, parts, from_first[0], row_count, passed[0])
    sents = [sent, *add_halves(later, True)]
    kepts = [kept, *add_halves(later, False)]

    def beside_first_sum(sent):
        near = tie(keys, sent)
        held["attended"] = attend(queries, [near] + swap_tp(near), owners)
        return sent

    def beside_second_sum(sent):
        sent, held["attended"] = lax.optimization_barrier((sent, held["attended"]))
        return sent

    hooks = {0: beside_first_sum, 1: beside_second_sum}
    return (scatter_sums(kepts, sents, orders, hooks), held["attended"])


def solution(mesh):
    placed = (
        P("ep", "tp"),
        P("ep", None),
        P("ep", None),
        P("ep", None, None, "tp"),
        P("ep", None, "tp"),
        P("ep", "tp", None),
        P("ep", None, None),
        P(),
        P("ep"),
        P("ep"),
    )
    return jax.shard_map(
        body,
        mesh=mesh,
        in_specs=placed,
        out_specs=(P("ep", "tp"), P("ep", "tp", None)),
        check_vma=False,
    )
```

```python
import functools

import jax
import jax.numpy as jnp
from jax import lax
from jax.experimental import pallas as pl
from jax.experimental.pallas import tpu as pltpu
from jax.sharding import PartitionSpec as P

KV = 512


score_scale = 192.0 ** (-0.5)

WHOLE = pl.BlockSpec(memory_space=pltpu.VMEM)


def kernel_call(
    kernel, out_shape, arguments, flops, spare, in_specs=None, scratch_shapes=(), counted=True
):
    held = sum(array.size * array.dtype.itemsize for array in jax.tree.leaves(out_shape))
    for array, spec in zip(arguments, in_specs or [WHOLE] * len(arguments)):
        held += array.size * array.dtype.itemsize if spec is WHOLE else 0
    moved = sum(array.size * array.dtype.itemsize for array in arguments)
    return pl.pallas_call(
        kernel,
        out_shape=out_shape,
        in_specs=in_specs or [WHOLE] * len(arguments),
        out_specs=jax.tree.map(lambda _: WHOLE, out_shape),
        scratch_shapes=scratch_shapes,
        compiler_params=pltpu.CompilerParams(vmem_limit_bytes=held + spare),
        cost_estimate=pl.CostEstimate(
            flops=flops, bytes_accessed=(moved + held) * counted, transcendentals=0
        ),
    )(*arguments)


def tie(values, others):
    return lax.optimization_barrier((values, others))[0]


def ep_bits():
    ep_size = lax.axis_size("ep")
    return [1 << place for place in reversed(range(ep_size.bit_length() - 1))]


def exchange(value, bit):
    ep_size = lax.axis_size("ep")
    return lax.ppermute(value, "ep", [(index, index ^ bit) for index in range(ep_size)])


def pass_tp(value, step):
    tp_size = lax.axis_size("tp")
    return lax.ppermute(
        value, "tp", [(index, (index + step) % tp_size) for index in range(tp_size)]
    )


def swap_tp(value):
    return [pass_tp(value, step) for step in range(1, lax.axis_size("tp"))]


def gather_rows(rows, others, orders, ends, beside, ahead):
    shared = orders[0][:-2]
    values = [
        jnp.concatenate([value[None], exchange(value[None], shared[0])], axis=0)
        for value in (rows, others)
    ]
    value = jnp.concatenate(values, axis=2)
    for bit in shared[1:]:
        if bit == shared[-1]:
            beside(value)
        value = jnp.concatenate([value, exchange(value, bit)], axis=0)
    halves = []
    for order, start, end in zip(orders, (0,) + ends, ends):
        part = value[:, :, start:end]
        part = jnp.concatenate([part, exchange(part, order[-2])], axis=0)
        if end == ends[-1]:
            part = ahead(part)
        halves.append((part, exchange(part, order[-1])))
    return halves


def places_of(order):
    places = [0]
    for bit in order:
        places = places + [place ^ bit for place in places]
    return places


def join_kernel(spots, ends, count, tp_size, *refs):
    out = refs[-1]
    parts = len(spots)
    rows = out.shape[0] // len(spots[0])
    width = out.shape[1] // tp_size
    index = lax.axis_index("tp")

    def place(tp_index):
        for step in range(tp_size):
            owner = (tp_index - step) % tp_size
            for part in range(parts):
                start, end = ((0,) + ends)[part], ends[part]
                for half in range(2):
                    ref = refs[(step * parts + part) * 2 + half]
                    blocks = ref.shape[0] // rows
                    for block in range(blocks):
                        spot = spots[part][half * blocks + block] * rows
                        out[spot : spot + rows, owner * width + start : owner * width + end] = ref[
                            block * rows : (block + 1) * rows, : end - start
                        ]

    for tp_index in range(tp_size):
        pl.when(index == tp_index)(functools.partial(place, tp_index))


def join_rows(by_step, spots, ends, rows):
    tp_size = len(by_step)
    arrays = [
        half.reshape(-1, half.shape[-1]) for parts in by_step for pair in parts for half in pair
    ]
    shape = jax.ShapeDtypeStruct((len(spots[0]) * rows, ends[-1] * tp_size), jnp.bfloat16)
    return kernel_call(
        functools.partial(join_kernel, spots, ends, len(arrays), tp_size),
        shape,
        arrays,
        flops=0,
        spare=4 << 20,
        counted=False,
    )


def scatter_sums(kepts, sents, orders, hooks):
    steps = len(orders[0])
    sents = list(sents)
    for step in range(steps):
        if step in hooks:
            sents[-1] = hooks[step](sents[-1])
        terms = [
            [kept, exchange(sent, order[steps - 1 - step])]
            for kept, sent, order in zip(kepts, sents, orders)
        ]
        if step == steps - 1:
            break
        half = kepts[0].shape[0] // 2
        sents = [add_up([term[half:] for term in pair]) for pair in terms]
        kepts = [add_up([term[:half] for term in pair]) for pair in terms]
        if step == 1:
            sents = [jnp.concatenate(sents, axis=1)]
            kepts = [jnp.concatenate(kepts, axis=1)]
    kept, arrived = terms[0]
    return add_up([kept, arrived])


def add_up(terms):
    total = terms[0].astype(jnp.float32)
    for term in terms[1:]:
        total = total + term.astype(jnp.float32)
    return total.astype(jnp.bfloat16)


def three_parts(value):
    parts = []
    for _ in range(3):
        part = lax.reduce_precision(value, 8, 7)
        parts.append(part.astype(jnp.bfloat16))
        value = value - part
    return parts


def turn_rows(hidden, turned, spots, rows):
    for block, spot in enumerate(spots):
        turned[spot * rows : (spot + 1) * rows] = hidden[block * rows : (block + 1) * rows]


def down_product(turned, weight, row, chunk, column, width):
    return lax.dot_general(
        turned[row : row + chunk],
        weight[column : column + width],
        (((1,), (1,)), ((), ())),
        preferred_element_type=jnp.float32,
    )


def group_kernel(step, chosen, spots, tp_size, cut, rows, hidden, weight, *refs):
    outs, (held, turned, arrived) = refs[: len(chosen)], refs[len(chosen) :]
    target = lax.rem(lax.axis_index("tp") + step, tp_size)
    copies = []
    for index, part in enumerate(chosen):
        start = pl.multiple_of((target * len(spots) + part) * cut, cut)
        copies.append(
            pltpu.make_async_copy(
                weight.at[pl.ds(start, cut)], held.at[index], arrived.at[index]
            )
        )
    for copy in copies:
        copy.start()
    chunk = min(256, hidden.shape[0])
    for index, part in enumerate(chosen):
        turn_rows(hidden, turned.at[index], spots[part], rows)
        copies[index].wait()
        for row in range(0, hidden.shape[0], chunk):
            outs[index][row : row + chunk] = down_product(
                turned.at[index], held.at[index], row, chunk, 0, cut
            ).astype(jnp.bfloat16)


def down_group(hidden, weight, step, chosen, spots, rows):
    count = len(chosen)
    tp_size = lax.axis_size("tp")
    cut = weight.shape[0] // tp_size // len(spots)
    shape = jax.ShapeDtypeStruct((hidden.shape[0], cut), jnp.bfloat16)
    return kernel_call(
        functools.partial(group_kernel, step, chosen, spots, tp_size, cut, rows),
        [shape] * count,
        [hidden, weight],
        flops=0,
        counted=False,
        spare=count * cut * weight.shape[1] * 2 + (8 << 20),
        in_specs=[WHOLE, pl.BlockSpec(memory_space=pl.ANY)],
        scratch_shapes=[
            pltpu.VMEM((count, cut, weight.shape[1]), weight.dtype),
            pltpu.VMEM((count,) + hidden.shape, hidden.dtype),
            pltpu.SemaphoreType.DMA((count,)),
        ],
    )


def own_kernel(part, parts, spots, cut, rows, count, hidden, weight, *refs):
    others, (kept, sent, held, turned, passed, arrived) = refs[:count], refs[count:]
    start = pl.multiple_of((lax.axis_index("tp") * parts + part) * cut, cut)
    copies = [pltpu.make_async_copy(weight.at[pl.ds(start, cut)], held, arrived.at[count])]
    for index, other in enumerate(others):
        copies.append(pltpu.make_async_copy(other, passed.at[index], arrived.at[index]))
    for copy in copies:
        copy.start()
    turn_rows(hidden, turned, spots, rows)
    for copy in copies:
        copy.wait()
    half = hidden.shape[0] // 2
    chunk = min(256, hidden.shape[0])
    width = cut // 2 if cut % 256 == 0 else cut
    for column in range(0, cut, width):
        for row in range(0, hidden.shape[0], chunk):
            total = down_product(turned, held, row, chunk, column, width)
            for index in range(count):
                total = total + passed[
                    index, row : row + chunk, column : column + width
                ].astype(jnp.float32)
            total = total.astype(jnp.bfloat16)
            for first in range(row, row + chunk, min(chunk, half)):
                out = kept if first < half else sent
                place = first % half
                piece = total[first - row : first - row + min(chunk, half)]
                out[place : place + piece.shape[0], column : column + width] = piece


def down_own(hidden, weight, part, parts, spots, rows, others):
    cut = weight.shape[0] // lax.axis_size("tp") // parts
    shape = jax.ShapeDtypeStruct((hidden.shape[0] // 2, cut), jnp.bfloat16)
    anywhere = pl.BlockSpec(memory_space=pl.ANY)
    return kernel_call(
        functools.partial(own_kernel, part, parts, spots, cut, rows, len(others)),
        [shape, shape],
        [hidden, weight] + others,
        flops=2 * hidden.size * cut,
        spare=(cut * weight.shape[1] + hidden.shape[0] * cut * len(others)) * 2 + (8 << 20),
        in_specs=[WHOLE] + [anywhere] * (1 + len(others)),
        scratch_shapes=[
            pltpu.VMEM((cut, weight.shape[1]), weight.dtype),
            pltpu.VMEM(hidden.shape, hidden.dtype),
            pltpu.VMEM((len(others), hidden.shape[0], cut), jnp.bfloat16),
            pltpu.SemaphoreType.DMA((1 + len(others),)),
        ],
    )


def halves_kernel(parts, first, *refs):
    outs, (held, arrived) = refs[-2 - parts : -2], refs[-2:]
    terms = refs[: -2 - parts]
    count = len(terms) // parts
    half, rows = outs[0].shape[0], 16
    copies = [
        pltpu.make_async_copy(term.at[pl.ds(first, half)], held.at[index], arrived.at[index])
        for index, term in enumerate(terms)
    ]
    for copy in copies:
        copy.start()
    for part in range(parts):
        for index in range(part * count, (part + 1) * count):
            copies[index].wait()
        for row in range(0, half, rows):
            total = held[part * count, row : row + rows].astype(jnp.float32)
            for index in range(part * count + 1, (part + 1) * count):
                total = total + held[index, row : row + rows].astype(jnp.float32)
            outs[part][row : row + rows] = total.astype(jnp.bfloat16)


def add_halves(terms, second):
    parts = len(terms)
    flat = [term for part in terms for term in part]
    half, cut = flat[0].shape[0] // 2, flat[0].shape[1]
    return kernel_call(
        functools.partial(halves_kernel, parts, half if second else 0),
        [jax.ShapeDtypeStruct((half, cut), jnp.bfloat16)] * parts,
        flat,
        flops=half * cut * len(flat),
        spare=half * cut * len(flat) * 2 + (2 << 20),
        in_specs=[pl.BlockSpec(memory_space=pl.ANY)] * len(flat),
        scratch_shapes=[
            pltpu.VMEM((len(flat), half, cut), jnp.bfloat16),
            pltpu.SemaphoreType.DMA((len(flat),)),
        ],
    )


def order_kernel(index, *refs):
    rows, out = refs[:-1], refs[-1]
    columns = lax.broadcasted_iota(jnp.int32, (out.shape[0], rows[0].shape[0]), 1)
    total = jnp.zeros(out.shape, jnp.float32)
    for step, ref in enumerate(rows):
        hot = (columns == index[:, step : step + 1]).astype(jnp.bfloat16)
        total = total + jnp.dot(hot, ref[...], preferred_element_type=jnp.float32)
    out[...] = total.astype(out.dtype)


def cache_out(latent_cache):
    ep_size = lax.axis_size("ep")
    slots, block_size, latent = latent_cache.shape
    share = slots // lax.axis_size("tp")
    mine = lax.dynamic_slice_in_dim(latent_cache, lax.axis_index("tp") * share, share, axis=0)
    return mine.reshape(share, ep_size, block_size * latent // ep_size).transpose(1, 0, 2)


def cache_turn(spread, block_source, slots):
    ep_size = lax.axis_size("ep")
    tp_size = lax.axis_size("tp")
    tp_index = lax.axis_index("tp")
    share, piece = spread.shape[1:]
    wanted = lax.dynamic_slice_in_dim(
        block_source.reshape(ep_size, tp_size, share), tp_index, 1, axis=1
    ).reshape(-1)
    place = (wanted // slots) * share + wanted % share
    holder = (wanted % slots) // share
    from_step = (tp_index + tp_size - holder) % tp_size
    index = jnp.where(
        from_step[:, None] == jnp.arange(tp_size, dtype=jnp.int32)[None, :], place[:, None], -1
    )
    rows = [part.reshape(-1, piece) for part in [spread] + swap_tp(spread)]
    shape = jax.ShapeDtypeStruct(rows[0].shape, rows[0].dtype)
    ordered = kernel_call(
        order_kernel,
        shape,
        [index] + rows,
        flops=2 * tp_size * rows[0].size * rows[0].shape[0],
        spare=6 << 20,
    )
    return ordered.reshape(ep_size, share, piece)


def cache_in(ordered, block_size, latent):
    share, piece = ordered.shape[1:]
    arrived = lax.all_to_all(ordered, "ep", split_axis=0, concat_axis=0, tiled=True)
    if piece != latent:
        arrived = arrived.transpose(1, 0, 2).reshape(share, block_size, latent).transpose(1, 0, 2)
    return arrived


def attention_kernel(heads, chunk, owner, queries, *refs):
    keys, out = refs[:-1], refs[-1]
    for start in range(0, queries.shape[0], chunk):
        row = lax.broadcasted_iota(jnp.int32, (chunk, keys[0].shape[0]), 0) + start
        if heads & (heads - 1):
            row = row // heads
        else:
            row = row >> (heads.bit_length() - 1)
        scores = []
        for step, key in enumerate(keys):
            part = lax.dot_general(
                queries[start : start + chunk],
                key[...],
                (((1,), (1,)), ((), ())),
                preferred_element_type=jnp.float32,
            )
            scores.append(
                jnp.where(row == owner[step : step + 1, :], part * score_scale, -jnp.inf)
            )
        row_max = scores[0].max(axis=1, keepdims=True)
        for part in scores[1:]:
            row_max = jnp.maximum(row_max, part.max(axis=1, keepdims=True))
        terms = [jnp.exp(part - row_max) for part in scores]
        total = 1.0 / sum(term.sum(axis=1, keepdims=True) for term in terms)
        attended = jnp.zeros((chunk, KV), jnp.float32)
        for term, key in zip(terms, keys):
            attended = attended + jnp.dot(
                (term * total).astype(jnp.bfloat16),
                key[:, :KV],
                preferred_element_type=jnp.float32,
            )
        out[start : start + chunk] = attended.astype(out.dtype)


def token_owners(block_request, block_used, block_size):
    tp_size = lax.axis_size("tp")
    share = block_request.shape[0] // tp_size
    within = jnp.arange(block_size, dtype=jnp.int32)[:, None]
    owners = []
    for step in range(tp_size):
        first = ((lax.axis_index("tp") + tp_size - step) % tp_size) * share
        owner = lax.dynamic_slice_in_dim(block_request, first, share)[None, :]
        limit = lax.dynamic_slice_in_dim(block_used, first, share)[None, :]
        owners.append(jnp.where(within < limit, owner, -1).reshape(1, -1))
    return jnp.concatenate(owners, axis=0)


def attend(queries, keys, owners):
    row_count, heads, latent = queries.shape
    keys = [part.reshape(-1, latent) for part in keys]
    rows = queries.reshape(-1, latent)
    shape = jax.ShapeDtypeStruct((rows.shape[0], KV), jnp.bfloat16)
    result = kernel_call(
        functools.partial(attention_kernel, heads, min(256, rows.shape[0])),
        shape,
        [owners, rows] + keys,
        flops=4 * rows.size * keys[0].shape[0] * len(keys),
        spare=8 << 20,
    )
    return result.reshape(row_count, heads, KV)


def body(
    tokens,
    expert_ids,
    gate_weights,
    expert_gate_up,
    expert_down,
    queries,
    latent_cache,
    block_source,
    block_request,
    block_used,
):
    row_count, top_count = expert_ids.shape
    slot_total, block_size, latent = latent_cache.shape
    ep_size = lax.axis_size("ep")
    tp_size = lax.axis_size("tp")
    tp_index = lax.axis_index("tp")
    bits = ep_bits()
    orders = (bits, bits[:-2] + [bits[-1], bits[-2]])
    parts = len(orders)
    cut = tokens.shape[1] // parts

    expert_range = jnp.arange(ep_size, dtype=jnp.int32)
    dense_gate = jnp.sum(
        jnp.where(
            expert_ids[:, :, None] == expert_range[None, None, :], gate_weights[:, :, None], 0.0
        ),
        axis=1,
    )
    gate_parts = jnp.concatenate(three_parts(dense_gate), axis=1)
    pad = -gate_parts.shape[1] % 128
    gates = jnp.pad(gate_parts, ((0, 0), (0, pad)))
    ends = tuple(cut * part for part in range(1, parts)) + (tokens.shape[1] + gates.shape[1],)
    held = {}

    def beside_shared(sent):
        pieces = tie(cache_out(latent_cache), sent)
        held["spread"] = lax.all_to_all(pieces, "ep", split_axis=0, concat_axis=0, tiled=True)

    def ahead_of_last(sent):
        sent, held["spread"] = lax.optimization_barrier((sent, held["spread"]))
        return sent

    halves = gather_rows(tokens, gates, orders, ends, beside_shared, ahead_of_last)
    last_sent = halves[-1][0]
    ordered = cache_turn(held["spread"], tie(block_source, last_sent), slot_total)
    keys = cache_in(ordered, block_size, latent)
    owners = token_owners(block_request, block_used, block_size)
    first_late, ordered, owners = lax.optimization_barrier((halves[0][1], ordered, owners))
    halves[0] = (halves[0][0], first_late)
    places = [places_of(order) for order in orders]
    to_first = [[places[0].index(place) for place in own] for own in places]
    from_first = [[own.index(place) for place in places[0]] for own in places]

    passed = [tie(early, last_sent) for early, _ in halves[:-1]]
    passed.append(tie(last_sent, halves[0][1]))
    arrived = [
        [(pass_tp(early, step), pass_tp(late, step)) for early, (_, late) in zip(passed, halves)]
        for step in range(1, tp_size)
    ]
    all_rows = join_rows(
        [halves] + arrived, to_first, tuple(cut * part for part in range(1, parts + 1)), row_count
    )
    gate_halves = [half[..., cut : cut + 3 * ep_size] for half in halves[-1]]
    all_gate = jnp.concatenate(gate_halves, axis=0)
    all_gate = jnp.stack([all_gate[block] for block in from_first[-1]]).astype(jnp.float32)
    mine = (jnp.arange(3 * ep_size, dtype=jnp.int32) % ep_size) == lax.axis_index("ep")
    my_gate = jnp.sum(jnp.where(mine, all_gate, 0.0), axis=2).reshape(-1)
    gate_and_up = jnp.einsum(
        "sd,dgf->sgf", all_rows, expert_gate_up[0], preferred_element_type=jnp.float32
    )
    hidden = (
        jax.nn.silu(gate_and_up[:, 0]) * gate_and_up[:, 1] * my_gate[:, None]
    ).astype(jnp.bfloat16)

    down_weight = pltpu.with_memory_space_constraint(expert_down[0], pltpu.HBM)
    passed = [[] for _ in range(parts)]
    for step in range(1, tp_size):
        others = down_group(hidden, down_weight, step, range(parts), from_first, row_count)
        others, keys = lax.optimization_barrier((others, keys))
        for part in range(parts):
            passed[part].append(pass_tp(others[part], step))
    later = down_group(hidden, down_weight, 0, range(1, parts), from_first, row_count)
    later = [[own] + others for own, others in zip(later, passed[1:])]
    kept, sent = down_own(hidden, down_weight, 0, parts, from_first[0], row_count, passed[0])
    sents = [sent, *add_halves(later, True)]
    kepts = [kept, *add_halves(later, False)]

    def beside_first_sum(sent):
        near = tie(keys, sent)
        held["attended"] = attend(queries, [near] + swap_tp(near), owners)
        return sent

    def beside_second_sum(sent):
        sent, held["attended"] = lax.optimization_barrier((sent, held["attended"]))
        return sent

    hooks = {0: beside_first_sum, 1: beside_second_sum}
    return (scatter_sums(kepts, sents, orders, hooks), held["attended"])


def solution(mesh):
    placed = (
        P("ep", "tp"),
        P("ep", None),
        P("ep", None),
        P("ep", None, None, "tp"),
        P("ep", None, "tp"),
        P("ep", "tp", None),
        P("ep", None, None),
        P(),
        P("ep"),
        P("ep"),
    )
    return jax.shard_map(
        body,
        mesh=mesh,
        in_specs=placed,
        out_specs=(P("ep", "tp"), P("ep", "tp", None)),
        check_vma=False,
    )
```

```python
import functools

import jax
import jax.numpy as jnp
from jax import lax
from jax.experimental import pallas as pl
from jax.experimental.pallas import tpu as pltpu
from jax.sharding import PartitionSpec as P

KV = 512


score_scale = 192.0 ** (-0.5)

WHOLE = pl.BlockSpec(memory_space=pltpu.VMEM)


def kernel_call(
    kernel, out_shape, arguments, flops, spare, in_specs=None, scratch_shapes=(), counted=True
):
    held = sum(array.size * array.dtype.itemsize for array in jax.tree.leaves(out_shape))
    for array, spec in zip(arguments, in_specs or [WHOLE] * len(arguments)):
        held += array.size * array.dtype.itemsize if spec is WHOLE else 0
    moved = sum(array.size * array.dtype.itemsize for array in arguments)
    return pl.pallas_call(
        kernel,
        out_shape=out_shape,
        in_specs=in_specs or [WHOLE] * len(arguments),
        out_specs=jax.tree.map(lambda _: WHOLE, out_shape),
        scratch_shapes=scratch_shapes,
        compiler_params=pltpu.CompilerParams(vmem_limit_bytes=held + spare),
        cost_estimate=pl.CostEstimate(
            flops=flops, bytes_accessed=(moved + held) * counted, transcendentals=0
        ),
    )(*arguments)


def tie(values, others):
    return lax.optimization_barrier((values, others))[0]


def ep_bits():
    ep_size = lax.axis_size("ep")
    return [1 << place for place in reversed(range(ep_size.bit_length() - 1))]


def exchange(value, bit):
    ep_size = lax.axis_size("ep")
    return lax.ppermute(value, "ep", [(index, index ^ bit) for index in range(ep_size)])


def pass_tp(value, step):
    tp_size = lax.axis_size("tp")
    return lax.ppermute(
        value, "tp", [(index, (index + step) % tp_size) for index in range(tp_size)]
    )


def swap_tp(value):
    return [pass_tp(value, step) for step in range(1, lax.axis_size("tp"))]


def gather_rows(rows, others, orders, ends, beside, ahead):
    shared = orders[0][:-2]
    values = [
        jnp.concatenate([value[None], exchange(value[None], shared[0])], axis=0)
        for value in (rows, others)
    ]
    value = jnp.concatenate(values, axis=2)
    for bit in shared[1:]:
        if bit == shared[-1]:
            beside(value)
        value = jnp.concatenate([value, exchange(value, bit)], axis=0)
    halves = []
    for order, start, end in zip(orders, (0,) + ends, ends):
        part = value[:, :, start:end]
        part = jnp.concatenate([part, exchange(part, order[-2])], axis=0)
        if end == ends[-1]:
            part = ahead(part)
        halves.append((part, exchange(part, order[-1])))
    return halves


def places_of(order):
    places = [0]
    for bit in order:
        places = places + [place ^ bit for place in places]
    return places


def join_kernel(spots, ends, count, tp_size, *refs):
    out = refs[-1]
    parts = len(spots)
    rows = out.shape[0] // len(spots[0])
    width = out.shape[1] // tp_size
    index = lax.axis_index("tp")

    def place(tp_index):
        for step in range(tp_size):
            owner = (tp_index - step) % tp_size
            for part in range(parts):
                start, end = ((0,) + ends)[part], ends[part]
                for half in range(2):
                    ref = refs[(step * parts + part) * 2 + half]
                    blocks = ref.shape[0] // rows
                    for block in range(blocks):
                        spot = spots[part][half * blocks + block] * rows
                        out[spot : spot + rows, owner * width + start : owner * width + end] = ref[
                            block * rows : (block + 1) * rows, : end - start
                        ]

    for tp_index in range(tp_size):
        pl.when(index == tp_index)(functools.partial(place, tp_index))


def join_rows(by_step, spots, ends, rows):
    tp_size = len(by_step)
    arrays = [
        half.reshape(-1, half.shape[-1]) for parts in by_step for pair in parts for half in pair
    ]
    shape = jax.ShapeDtypeStruct((len(spots[0]) * rows, ends[-1] * tp_size), jnp.bfloat16)
    return kernel_call(
        functools.partial(join_kernel, spots, ends, len(arrays), tp_size),
        shape,
        arrays,
        flops=0,
        spare=4 << 20,
        counted=False,
    )


def scatter_sums(kepts, sents, orders, hooks):
    steps = len(orders[0])
    sents = list(sents)
    for step in range(steps):
        if step in hooks:
            sents[-1] = hooks[step](sents[-1])
        terms = [
            [kept, exchange(sent, order[steps - 1 - step])]
            for kept, sent, order in zip(kepts, sents, orders)
        ]
        if step == steps - 1:
            break
        half = kepts[0].shape[0] // 2
        sents = [add_up([term[half:] for term in pair]) for pair in terms]
        kepts = [add_up([term[:half] for term in pair]) for pair in terms]
        if step == 1:
            sents = [jnp.concatenate(sents, axis=1)]
            kepts = [jnp.concatenate(kepts, axis=1)]
    kept, arrived = terms[0]
    return add_up([kept, arrived])


def add_up(terms):
    total = terms[0].astype(jnp.float32)
    for term in terms[1:]:
        total = total + term.astype(jnp.float32)
    return total.astype(jnp.bfloat16)


def three_parts(value):
    parts = []
    for _ in range(3):
        part = lax.reduce_precision(value, 8, 7)
        parts.append(part.astype(jnp.bfloat16))
        value = value - part
    return parts


def turn_rows(hidden, turned, spots, rows):
    for block, spot in enumerate(spots):
        turned[spot * rows : (spot + 1) * rows] = hidden[block * rows : (block + 1) * rows]


def down_product(turned, weight, row, chunk, column, width):
    return lax.dot_general(
        turned[row : row + chunk],
        weight[column : column + width],
        (((1,), (1,)), ((), ())),
        preferred_element_type=jnp.float32,
    )


def group_kernel(step, chosen, spots, tp_size, cut, rows, hidden, weight, *refs):
    outs, (held, turned, arrived) = refs[: len(chosen)], refs[len(chosen) :]
    target = lax.rem(lax.axis_index("tp") + step, tp_size)
    pieces = 2 if cut % 256 == 0 else 1
    width = cut // pieces
    copies = []
    for index, part in enumerate(chosen):
        for piece in range(pieces):
            start = pl.multiple_of((target * len(spots) + part) * cut + piece * width, width)
            copies.append(
                pltpu.make_async_copy(
                    weight.at[pl.ds(start, width)],
                    held.at[index, pl.ds(piece * width, width)],
                    arrived.at[index * pieces + piece],
                )
            )
    for copy in copies:
        copy.start()
    chunk = min(256, hidden.shape[0])
    for index, part in enumerate(chosen):
        turn_rows(hidden, turned.at[index], spots[part], rows)
        for piece in range(pieces):
            copies[index * pieces + piece].wait()
            column = piece * width
            for row in range(0, hidden.shape[0], chunk):
                outs[index][row : row + chunk, column : column + width] = down_product(
                    turned.at[index], held.at[index], row, chunk, column, width
                ).astype(jnp.bfloat16)


def down_group(hidden, weight, step, chosen, spots, rows):
    count = len(chosen)
    tp_size = lax.axis_size("tp")
    cut = weight.shape[0] // tp_size // len(spots)
    shape = jax.ShapeDtypeStruct((hidden.shape[0], cut), jnp.bfloat16)
    return kernel_call(
        functools.partial(group_kernel, step, chosen, spots, tp_size, cut, rows),
        [shape] * count,
        [hidden, weight],
        flops=0,
        counted=False,
        spare=count * cut * weight.shape[1] * 2 + (8 << 20),
        in_specs=[WHOLE, pl.BlockSpec(memory_space=pl.ANY)],
        scratch_shapes=[
            pltpu.VMEM((count, cut, weight.shape[1]), weight.dtype),
            pltpu.VMEM((count,) + hidden.shape, hidden.dtype),
            pltpu.SemaphoreType.DMA((2 * count,)),
        ],
    )


def own_kernel(part, parts, spots, cut, rows, count, hidden, weight, *refs):
    others, (kept, sent, held, turned, passed, arrived) = refs[:count], refs[count:]
    start = pl.multiple_of((lax.axis_index("tp") * parts + part) * cut, cut)
    copies = [pltpu.make_async_copy(weight.at[pl.ds(start, cut)], held, arrived.at[count])]
    for index, other in enumerate(others):
        copies.append(pltpu.make_async_copy(other, passed.at[index], arrived.at[index]))
    for copy in copies:
        copy.start()
    turn_rows(hidden, turned, spots, rows)
    for copy in copies:
        copy.wait()
    half = hidden.shape[0] // 2
    chunk = min(256, hidden.shape[0])
    width = cut // 2 if cut % 256 == 0 else cut
    for column in range(0, cut, width):
        for row in range(0, hidden.shape[0], chunk):
            total = down_product(turned, held, row, chunk, column, width)
            for index in range(count):
                total = total + passed[
                    index, row : row + chunk, column : column + width
                ].astype(jnp.float32)
            total = total.astype(jnp.bfloat16)
            for first in range(row, row + chunk, min(chunk, half)):
                out = kept if first < half else sent
                place = first % half
                piece = total[first - row : first - row + min(chunk, half)]
                out[place : place + piece.shape[0], column : column + width] = piece


def down_own(hidden, weight, part, parts, spots, rows, others):
    cut = weight.shape[0] // lax.axis_size("tp") // parts
    shape = jax.ShapeDtypeStruct((hidden.shape[0] // 2, cut), jnp.bfloat16)
    anywhere = pl.BlockSpec(memory_space=pl.ANY)
    return kernel_call(
        functools.partial(own_kernel, part, parts, spots, cut, rows, len(others)),
        [shape, shape],
        [hidden, weight] + others,
        flops=2 * hidden.size * cut,
        spare=(cut * weight.shape[1] + hidden.shape[0] * cut * len(others)) * 2 + (8 << 20),
        in_specs=[WHOLE] + [anywhere] * (1 + len(others)),
        scratch_shapes=[
            pltpu.VMEM((cut, weight.shape[1]), weight.dtype),
            pltpu.VMEM(hidden.shape, hidden.dtype),
            pltpu.VMEM((len(others), hidden.shape[0], cut), jnp.bfloat16),
            pltpu.SemaphoreType.DMA((1 + len(others),)),
        ],
    )


def halves_kernel(parts, first, *refs):
    outs, (held, arrived) = refs[-2 - parts : -2], refs[-2:]
    terms = refs[: -2 - parts]
    count = len(terms) // parts
    half, rows = outs[0].shape[0], 16
    copies = [
        pltpu.make_async_copy(term.at[pl.ds(first, half)], held.at[index], arrived.at[index])
        for index, term in enumerate(terms)
    ]
    for copy in copies:
        copy.start()
    for part in range(parts):
        for index in range(part * count, (part + 1) * count):
            copies[index].wait()
        for row in range(0, half, rows):
            total = held[part * count, row : row + rows].astype(jnp.float32)
            for index in range(part * count + 1, (part + 1) * count):
                total = total + held[index, row : row + rows].astype(jnp.float32)
            outs[part][row : row + rows] = total.astype(jnp.bfloat16)


def add_halves(terms, second):
    parts = len(terms)
    flat = [term for part in terms for term in part]
    half, cut = flat[0].shape[0] // 2, flat[0].shape[1]
    return kernel_call(
        functools.partial(halves_kernel, parts, half if second else 0),
        [jax.ShapeDtypeStruct((half, cut), jnp.bfloat16)] * parts,
        flat,
        flops=half * cut * len(flat),
        spare=half * cut * len(flat) * 2 + (2 << 20),
        in_specs=[pl.BlockSpec(memory_space=pl.ANY)] * len(flat),
        scratch_shapes=[
            pltpu.VMEM((len(flat), half, cut), jnp.bfloat16),
            pltpu.SemaphoreType.DMA((len(flat),)),
        ],
    )


def order_kernel(index, *refs):
    rows, out = refs[:-1], refs[-1]
    columns = lax.broadcasted_iota(jnp.int32, (out.shape[0], rows[0].shape[0]), 1)
    total = jnp.zeros(out.shape, jnp.float32)
    for step, ref in enumerate(rows):
        hot = (columns == index[:, step : step + 1]).astype(jnp.bfloat16)
        total = total + jnp.dot(hot, ref[...], preferred_element_type=jnp.float32)
    out[...] = total.astype(out.dtype)


def cache_out(latent_cache):
    ep_size = lax.axis_size("ep")
    slots, block_size, latent = latent_cache.shape
    share = slots // lax.axis_size("tp")
    mine = lax.dynamic_slice_in_dim(latent_cache, lax.axis_index("tp") * share, share, axis=0)
    return mine.reshape(share, ep_size, block_size * latent // ep_size).transpose(1, 0, 2)


def cache_turn(spread, block_source, slots):
    ep_size = lax.axis_size("ep")
    tp_size = lax.axis_size("tp")
    tp_index = lax.axis_index("tp")
    share, piece = spread.shape[1:]
    wanted = lax.dynamic_slice_in_dim(
        block_source.reshape(ep_size, tp_size, share), tp_index, 1, axis=1
    ).reshape(-1)
    place = (wanted // slots) * share + wanted % share
    holder = (wanted % slots) // share
    from_step = (tp_index + tp_size - holder) % tp_size
    index = jnp.where(
        from_step[:, None] == jnp.arange(tp_size, dtype=jnp.int32)[None, :], place[:, None], -1
    )
    rows = [part.reshape(-1, piece) for part in [spread] + swap_tp(spread)]
    shape = jax.ShapeDtypeStruct(rows[0].shape, rows[0].dtype)
    ordered = kernel_call(
        order_kernel,
        shape,
        [index] + rows,
        flops=2 * tp_size * rows[0].size * rows[0].shape[0],
        spare=6 << 20,
    )
    return ordered.reshape(ep_size, share, piece)


def cache_in(ordered, block_size, latent):
    share, piece = ordered.shape[1:]
    arrived = lax.all_to_all(ordered, "ep", split_axis=0, concat_axis=0, tiled=True)
    if piece != latent:
        arrived = arrived.transpose(1, 0, 2).reshape(share, block_size, latent).transpose(1, 0, 2)
    return arrived


def attention_kernel(heads, chunk, owner, queries, *refs):
    keys, out = refs[:-1], refs[-1]
    for start in range(0, queries.shape[0], chunk):
        row = lax.broadcasted_iota(jnp.int32, (chunk, keys[0].shape[0]), 0) + start
        if heads & (heads - 1):
            row = row // heads
        else:
            row = row >> (heads.bit_length() - 1)
        scores = []
        for step, key in enumerate(keys):
            part = lax.dot_general(
                queries[start : start + chunk],
                key[...],
                (((1,), (1,)), ((), ())),
                preferred_element_type=jnp.float32,
            )
            scores.append(
                jnp.where(row == owner[step : step + 1, :], part * score_scale, -jnp.inf)
            )
        row_max = scores[0].max(axis=1, keepdims=True)
        for part in scores[1:]:
            row_max = jnp.maximum(row_max, part.max(axis=1, keepdims=True))
        terms = [jnp.exp(part - row_max) for part in scores]
        total = 1.0 / sum(term.sum(axis=1, keepdims=True) for term in terms)
        attended = jnp.zeros((chunk, KV), jnp.float32)
        for term, key in zip(terms, keys):
            attended = attended + jnp.dot(
                (term * total).astype(jnp.bfloat16),
                key[:, :KV],
                preferred_element_type=jnp.float32,
            )
        out[start : start + chunk] = attended.astype(out.dtype)


def token_owners(block_request, block_used, block_size):
    tp_size = lax.axis_size("tp")
    share = block_request.shape[0] // tp_size
    within = jnp.arange(block_size, dtype=jnp.int32)[:, None]
    owners = []
    for step in range(tp_size):
        first = ((lax.axis_index("tp") + tp_size - step) % tp_size) * share
        owner = lax.dynamic_slice_in_dim(block_request, first, share)[None, :]
        limit = lax.dynamic_slice_in_dim(block_used, first, share)[None, :]
        owners.append(jnp.where(within < limit, owner, -1).reshape(1, -1))
    return jnp.concatenate(owners, axis=0)


def attend(queries, keys, owners):
    row_count, heads, latent = queries.shape
    keys = [part.reshape(-1, latent) for part in keys]
    rows = queries.reshape(-1, latent)
    shape = jax.ShapeDtypeStruct((rows.shape[0], KV), jnp.bfloat16)
    result = kernel_call(
        functools.partial(attention_kernel, heads, min(256, rows.shape[0])),
        shape,
        [owners, rows] + keys,
        flops=4 * rows.size * keys[0].shape[0] * len(keys),
        spare=8 << 20,
    )
    return result.reshape(row_count, heads, KV)


def body(
    tokens,
    expert_ids,
    gate_weights,
    expert_gate_up,
    expert_down,
    queries,
    latent_cache,
    block_source,
    block_request,
    block_used,
):
    row_count, top_count = expert_ids.shape
    slot_total, block_size, latent = latent_cache.shape
    ep_size = lax.axis_size("ep")
    tp_size = lax.axis_size("tp")
    tp_index = lax.axis_index("tp")
    bits = ep_bits()
    orders = (bits, bits[:-2] + [bits[-1], bits[-2]])
    parts = len(orders)
    cut = tokens.shape[1] // parts

    expert_range = jnp.arange(ep_size, dtype=jnp.int32)
    dense_gate = jnp.sum(
        jnp.where(
            expert_ids[:, :, None] == expert_range[None, None, :], gate_weights[:, :, None], 0.0
        ),
        axis=1,
    )
    gate_parts = jnp.concatenate(three_parts(dense_gate), axis=1)
    pad = -gate_parts.shape[1] % 128
    gates = jnp.pad(gate_parts, ((0, 0), (0, pad)))
    ends = tuple(cut * part for part in range(1, parts)) + (tokens.shape[1] + gates.shape[1],)
    held = {}

    def beside_shared(sent):
        pieces = tie(cache_out(latent_cache), sent)
        held["spread"] = lax.all_to_all(pieces, "ep", split_axis=0, concat_axis=0, tiled=True)

    def ahead_of_last(sent):
        sent, held["spread"] = lax.optimization_barrier((sent, held["spread"]))
        return sent

    halves = gather_rows(tokens, gates, orders, ends, beside_shared, ahead_of_last)
    last_sent = halves[-1][0]
    ordered = cache_turn(held["spread"], tie(block_source, last_sent), slot_total)
    keys = cache_in(ordered, block_size, latent)
    owners = token_owners(block_request, block_used, block_size)
    first_late, ordered, owners = lax.optimization_barrier((halves[0][1], ordered, owners))
    halves[0] = (halves[0][0], first_late)
    places = [places_of(order) for order in orders]
    to_first = [[places[0].index(place) for place in own] for own in places]
    from_first = [[own.index(place) for place in places[0]] for own in places]

    passed = [tie(early, last_sent) for early, _ in halves[:-1]]
    passed.append(tie(last_sent, halves[0][1]))
    arrived = [
        [(pass_tp(early, step), pass_tp(late, step)) for early, (_, late) in zip(passed, halves)]
        for step in range(1, tp_size)
    ]
    all_rows = join_rows(
        [halves] + arrived, to_first, tuple(cut * part for part in range(1, parts + 1)), row_count
    )
    gate_halves = [half[..., cut : cut + 3 * ep_size] for half in halves[-1]]
    all_gate = jnp.concatenate(gate_halves, axis=0)
    all_gate = jnp.stack([all_gate[block] for block in from_first[-1]]).astype(jnp.float32)
    mine = (jnp.arange(3 * ep_size, dtype=jnp.int32) % ep_size) == lax.axis_index("ep")
    my_gate = jnp.sum(jnp.where(mine, all_gate, 0.0), axis=2).reshape(-1)
    gate_and_up = jnp.einsum(
        "sd,dgf->sgf", all_rows, expert_gate_up[0], preferred_element_type=jnp.float32
    )
    hidden = (
        jax.nn.silu(gate_and_up[:, 0]) * gate_and_up[:, 1] * my_gate[:, None]
    ).astype(jnp.bfloat16)

    down_weight = pltpu.with_memory_space_constraint(expert_down[0], pltpu.HBM)
    passed = [[] for _ in range(parts)]
    for step in range(1, tp_size):
        others = down_group(hidden, down_weight, step, range(parts), from_first, row_count)
        others, keys = lax.optimization_barrier((others, keys))
        for part in range(parts):
            passed[part].append(pass_tp(others[part], step))
    later = down_group(hidden, down_weight, 0, range(1, parts), from_first, row_count)
    later = [[own] + others for own, others in zip(later, passed[1:])]
    kept, sent = down_own(hidden, down_weight, 0, parts, from_first[0], row_count, passed[0])
    sents = [sent, *add_halves(later, True)]
    kepts = [kept, *add_halves(later, False)]

    def beside_first_sum(sent):
        near = tie(keys, sent)
        held["attended"] = attend(queries, [near] + swap_tp(near), owners)
        return sent

    def beside_second_sum(sent):
        sent, held["attended"] = lax.optimization_barrier((sent, held["attended"]))
        return sent

    hooks = {0: beside_first_sum, 1: beside_second_sum}
    return (scatter_sums(kepts, sents, orders, hooks), held["attended"])


def solution(mesh):
    placed = (
        P("ep", "tp"),
        P("ep", None),
        P("ep", None),
        P("ep", None, None, "tp"),
        P("ep", None, "tp"),
        P("ep", "tp", None),
        P("ep", None, None),
        P(),
        P("ep"),
        P("ep"),
    )
    return jax.shard_map(
        body,
        mesh=mesh,
        in_specs=placed,
        out_specs=(P("ep", "tp"), P("ep", "tp", None)),
        check_vma=False,
    )
```
